32 devices in a mesh: replica: 4 (over y, x), inner: 8 (over z, core).
Axes of the slice: x: 2, y: 2, z: 4, core: 2. Of those that a mesh axis runs over, the one named last changes fastest.
Arguments:
- tokens: bfloat16 [4096, 2048], P(('replica', 'inner')), may hold values from -6 to 6
- w_query: bfloat16 [2048, 2048], P('inner'), may hold values from -0.15625 to 0.15625
- w_key: bfloat16 [2048, 2048], P('inner'), may hold values from -0.15625 to 0.15625
- w_value: bfloat16 [2048, 2048], P('inner'), may hold values from -0.125 to 0.125
- w_out: bfloat16 [2048, 2048], P('inner'), may hold values from -0.75 to 0.75
- w_gate: bfloat16 [2048, 8192], P('inner'), may hold values from -0.125 to 0.125
- w_up: bfloat16 [2048, 8192], P('inner'), may hold values from -0.125 to 0.125
- w_down: bfloat16 [8192, 2048], P('inner'), may hold values from -0.0625 to 0.0625
- gain_attn: bfloat16 [2048], P('inner'), may hold values from 0.5 to 1.5
- gain_ffn: bfloat16 [2048], P('inner'), may hold values from 0.5 to 1.5
- pieces: int32 [4096], P(('replica', 'inner')), may hold values from -1 to 15, as said below
- positions: int32 [4096], P(('replica', 'inner')), may hold values from 0 to 783, as said below
- cotangent: bfloat16 [4096, 2048], P(('replica', 'inner')), may hold values from -6 to 6
Outputs:
- output: bfloat16 [4096, 2048], P(('replica', 'inner'))
- grad_tokens: float32 [4096, 2048], P(('replica', 'inner'))
- grad_query: float32 [2048, 2048], P('inner')
- grad_key: float32 [2048, 2048], P('inner')
- grad_value: float32 [2048, 2048], P('inner')
- grad_out: float32 [2048, 2048], P('inner')
- grad_gate: float32 [2048, 8192], P('inner')
- grad_up: float32 [2048, 8192], P('inner')
- grad_down: float32 [8192, 2048], P('inner')
- grad_gain_attn: float32 [2048], P('inner')
- grad_gain_ffn: float32 [2048], P('inner')
The draws below stay inside these ranges and needn't reach their ends.
Inputs may be any that keep to these rules, and one draw needn't show every extreme that they name: `pieces`: image tokens come in aligned blocks of 256 tokens of one sequence (2048 on the larger slice) that share one id, the block's index among all 16 blocks; text tokens have -1. In every sequence the first block is text and the last block is an image. `positions`: A text token's position is its index within its sequence; an image token's is its block's first index within the sequence plus its index within the block modulo 16.
All inputs are finite; a program needn't handle non-finite values.
Results may differ from the reference program's by a relative error of at most 0.02.
Values may be sent and summed in bfloat16 or wider, within the bound.
A program may use at most 448 MiB of HBM per device.

```python
import math
import jax
import jax.numpy as jnp
from jax import lax

D = 2048
HEADS = 16
HEAD_DIM = 128
FF = 8192
PIECE = 256
GRID = 16
LENGTH = 1024
TOKENS = 4096
N_REPLICA = 4


def layout(key):
    blocks = TOKENS // PIECE
    per_sequence = LENGTH // PIECE
    second_key = jax.random.fold_in(key, 1)
    raw_bits = jax.random.bits(second_key, (blocks,), jnp.uint32)
    image_flag = (raw_bits % 2).astype(jnp.int32)
    within = jnp.arange(blocks) % per_sequence
    image_flag = jnp.where(within == 0, 0, jnp.where(within == per_sequence - 1, 1, image_flag))
    piece_ids = jnp.where(image_flag == 1, jnp.arange(blocks), -1)
    return jnp.repeat(piece_ids, PIECE, total_repeat_length=TOKENS).astype(jnp.int32)


def draw_pieces(key, part):
    return layout(key)


def draw_positions(key, part):
    piece_ids = layout(key)
    inside = jnp.arange(TOKENS) % LENGTH
    block_start = inside - inside % PIECE
    return jnp.where(piece_ids >= 0, block_start + inside % PIECE % GRID, inside).astype(jnp.int32)


def level_of(own_key, shape, cuts, least, largest):
    def one(position, shards_of):
        steps = jax.random.uniform(jax.random.fold_in(jax.random.fold_in(own_key, 6), position), (shards_of,), jnp.float32, least / len(cuts), largest / len(cuts))
        return jnp.repeat(jnp.exp(steps), shape[position] // shards_of).reshape((-1,) + (1,) * (len(shape) - position - 1))

    gain = one(*cuts[0])
    for cut in cuts[1:]:
        gain = gain * one(*cut)
    return gain


def normal_values(own_key, extent, deviation, reach, shards=(), held_as=jnp.bfloat16):
    gain = level_of(own_key, extent, shards, -0.22, 0.18) if shards else 1.0
    array = jax.random.normal(own_key, extent, jnp.float32) * deviation * gain
    return jnp.minimum(jnp.maximum(array, -reach), reach).astype(held_as)


def setup_inputs(seed: int = 0) -> dict:
    key_of = jax.random.split(jax.random.key(seed), 14)
    tokens = normal_values(key_of[0], (TOKENS, D), 1.0, 6.0, ((0, 32),))
    w_query = normal_values(key_of[1], (D, D), (2 * D // 3) ** -0.5, 0.15625, ((0, 8),))
    w_key = normal_values(key_of[2], (D, D), (2 * D // 3) ** -0.5, 0.15625, ((0, 8),))
    w_value = normal_values(key_of[3], (D, D), D ** -0.5, 0.125, ((0, 8),))
    w_out = normal_values(key_of[4], (D, D), (D * 32 // LENGTH) ** -0.5, 0.75, ((0, 8),))
    w_gate = normal_values(key_of[5], (D, FF), D ** -0.5, 0.125, ((0, 8),))
    w_up = normal_values(key_of[6], (D, FF), D ** -0.5, 0.125, ((0, 8),))
    w_down = normal_values(key_of[7], (FF, D), FF ** -0.5, 0.0625, ((0, 8),))
    gain_attn = jnp.clip(1.0 + 0.1 * jax.random.normal(key_of[8], (D,), jnp.float32), 0.5, 1.5).astype(jnp.bfloat16)
    gain_ffn = jnp.clip(1.0 + 0.1 * jax.random.normal(key_of[9], (D,), jnp.float32), 0.5, 1.5).astype(jnp.bfloat16)
    pieces = draw_pieces(jax.random.fold_in(key_of[13], 71), 0)
    positions = draw_positions(jax.random.fold_in(key_of[13], 71), 0)
    cotangent = normal_values(key_of[12], (TOKENS, D), 1.0, 6.0, ((0, 32),))
    return dict(tokens=tokens, w_query=w_query, w_key=w_key, w_value=w_value, w_out=w_out, w_gate=w_gate, w_up=w_up, w_down=w_down, gain_attn=gain_attn, gain_ffn=gain_ffn, pieces=pieces, positions=positions, cotangent=cotangent)


epsilon = 1e-06
rope_base = 10000.0
highest = lax.Precision.HIGHEST

@jax.custom_vjp
def low(v):
    return lax.optimization_barrier(v.astype(jnp.bfloat16)).astype(jnp.float32)

@jax.custom_vjp
def low_back(v):
    return v

def low_keep(v):
    return (low(v), None)

def low_pass(kept, grad):
    return (grad,)

def back_keep(v):
    return (v, None)

def back_low(kept, grad):
    return (low(grad),)
low.defvjp(low_keep, low_pass)
low_back.defvjp(back_keep, back_low)

def rope_tables(positions):
    half_dim = HEAD_DIM // 2
    frequency = rope_base ** (-jnp.arange(half_dim, dtype=jnp.float32) * 2.0 / HEAD_DIM)
    angle = positions.astype(jnp.float32)[:, None] * frequency[None, :]
    return (jnp.cos(angle), jnp.sin(angle))

def rotate(heads, cosine, sine):
    half_dim = HEAD_DIM // 2
    first_half = heads[..., :half_dim]
    second_half = heads[..., half_dim:]
    cosine = cosine[:, None, :]
    sine = sine[:, None, :]
    return jnp.concatenate([first_half * cosine - second_half * sine, first_half * sine + second_half * cosine], axis=-1)

def rms_unit(values):
    return values * lax.rsqrt(lax.optimization_barrier(jnp.mean(values * values, axis=1, keepdims=True)) + epsilon)

def block_forward(inputs, w_query, w_key, w_value, w_out, w_gate, w_up, w_down, gain_attn, gain_ffn, cosine, sine, piece_ids):
    count_tok = inputs.shape[0]
    normed_one = low(rms_unit(inputs) * gain_attn)
    query_lin = low_back(jnp.dot(normed_one, w_query, precision=highest))
    key_lin = low_back(jnp.dot(normed_one, w_key, precision=highest))
    value_lin = low_back(jnp.dot(normed_one, w_value, precision=highest))
    query = low(rotate(query_lin.reshape(count_tok, HEADS, HEAD_DIM), cosine, sine))
    keys = low(rotate(key_lin.reshape(count_tok, HEADS, HEAD_DIM), cosine, sine))
    values = low(value_lin).reshape(count_tok, HEADS, HEAD_DIM)
    token_index = jnp.arange(count_tok)
    score_bias = -math.log(LENGTH)
    block_rows = math.gcd(LENGTH, 512)

    def attend(block):
        query_block, index_block, piece_block = block
        score = jnp.einsum('qhd,khd->hqk', query_block, keys, precision=highest) / math.sqrt(HEAD_DIM) + score_bias
        score = low_back(score)
        visible = (token_index[None, :] <= index_block[:, None]) | (piece_ids[None, :] == piece_block[:, None]) & (piece_block[:, None] >= 0)
        prob = low(jax.nn.sigmoid(score) * visible[None].astype(score.dtype))
        return jnp.einsum('hqk,khd->qhd', prob, values, precision=highest)
    blocks = count_tok // block_rows
    attended = lax.map(jax.checkpoint(attend), (query.reshape(blocks, block_rows, HEADS, HEAD_DIM), token_index.reshape(blocks, block_rows), piece_ids.reshape(blocks, block_rows)))
    attended = low(low_back(attended.reshape(count_tok, D)))
    attn_out = low_back(jnp.dot(attended, w_out, precision=highest))
    middle = inputs + attn_out
    normed_two = low(rms_unit(middle) * gain_ffn)
    gate = low_back(jnp.dot(normed_two, w_gate, precision=highest))
    up_lin = low_back(jnp.dot(normed_two, w_up, precision=highest))
    hidden = low(jax.nn.silu(gate) * up_lin)
    mlp = low_back(jnp.dot(hidden, w_down, precision=highest))
    return middle + mlp

def reference(tokens, w_query, w_key, w_value, w_out, w_gate, w_up, w_down, gain_attn, gain_ffn, pieces, positions, cotangent):
    params = (w_query.astype(jnp.float32), w_key.astype(jnp.float32), w_value.astype(jnp.float32), w_out.astype(jnp.float32), w_gate.astype(jnp.float32), w_up.astype(jnp.float32), w_down.astype(jnp.float32), gain_attn.astype(jnp.float32), gain_ffn.astype(jnp.float32))
    sequences = (tokens.astype(jnp.float32).reshape(N_REPLICA, LENGTH, D), cotangent.astype(jnp.float32).reshape(N_REPLICA, LENGTH, D), pieces.reshape(N_REPLICA, LENGTH), positions.reshape(N_REPLICA, LENGTH))

    def per_sequence(summed, sequence):
        inputs, upstream, piece_ids, token_pos = sequence
        cosine, sine = rope_tables(token_pos)

        def forward(inputs, *weights):
            return block_forward(inputs, *weights, cosine, sine, piece_ids)
        result, pullback = jax.vjp(forward, inputs, *params)
        grads = pullback(upstream)
        summed = tuple((earlier + addend for earlier, addend in zip(summed, grads[1:])))
        return (summed, (result, grads[0]))
    initial = tuple((jnp.zeros_like(tensor) for tensor in params))
    summed, (results, grad_inputs) = lax.scan(per_sequence, initial, sequences)
    return (results.reshape(TOKENS, D).astype(jnp.bfloat16), grad_inputs.reshape(TOKENS, D), summed[0], summed[1], summed[2], summed[3], summed[4], summed[5], summed[6], summed[7], summed[8])
```

```python
import math

import jax
import jax.numpy as jnp
from jax import lax
from jax.sharding import PartitionSpec as P

HEAD_DIM = 128
PIECE = 256
epsilon = 1e-06
rope_base = 10000.0
dims_rows = (((1,), (1,)), ((), ()))
dims_cols = (((0,), (0,)), ((), ()))
f32 = jnp.float32
bf16 = jnp.bfloat16


def dot(a, b):
    return jnp.dot(a, b, preferred_element_type=f32)


def dot_t(a, b):
    return lax.dot_general(a, b, dims_rows, preferred_element_type=f32)


def t_dot(a, b):
    return lax.dot_general(a, b, dims_cols, preferred_element_type=f32)


def rope_tables(positions):
    half_dim = HEAD_DIM // 2
    frequency = rope_base ** (-jnp.arange(half_dim, dtype=f32) * 2.0 / HEAD_DIM)
    angle = positions.astype(f32)[:, None] * frequency[None, :]
    return jnp.cos(angle), jnp.sin(angle)


def rotate(flat, cosine, sine):
    half_dim = HEAD_DIM // 2
    heads = flat.reshape(flat.shape[0], -1, HEAD_DIM)
    a = heads[..., :half_dim]
    b = heads[..., half_dim:]
    cosine = cosine[:, None, :]
    sine = sine[:, None, :]
    return jnp.concatenate([a * cosine - b * sine, a * sine + b * cosine], axis=-1).reshape(flat.shape)


def rms_scale(values):
    return lax.rsqrt(jnp.mean(values * values, axis=1, keepdims=True) + epsilon)


def gather_tokens(block):
    return lax.all_gather(block, "inner", axis=0, tiled=True)


def scatter_tokens(partial):
    return lax.psum_scatter(partial.astype(bf16), "inner", scatter_dimension=0, tiled=True).astype(f32)


def column_shard(w):
    n = lax.axis_size("inner")
    nr = lax.axis_size("replica")
    rows, cols = w.shape
    part = rows // nr
    mine = lax.dynamic_slice_in_dim(w, lax.axis_index("replica") * part, part, 0)
    mine = mine.reshape(part, n, cols // n)
    got = lax.all_to_all(mine, "inner", split_axis=1, concat_axis=0, tiled=False)
    got = got.reshape(n, part, cols // n)
    full = lax.all_gather(got, "replica", axis=1, tiled=False)
    return full.reshape(n * rows, cols // n)


def owner_rows(g):
    n = lax.axis_size("inner")
    nr = lax.axis_size("replica")
    rows = g.shape[0] // n
    part = rows // nr
    cols = g.shape[1]
    g = g.astype(bf16).reshape(n, nr, part, cols).transpose(1, 0, 2, 3).reshape(nr * n * part, cols)
    mine = lax.psum_scatter(g, "replica", scatter_dimension=0, tiled=True).reshape(n, part, cols)
    got = lax.all_to_all(mine, "inner", split_axis=0, concat_axis=1, tiled=False)
    got = got.reshape(part, n * cols)
    return lax.all_gather(got, "replica", axis=0, tiled=True).astype(f32)


def sum_copies(g):
    mine = lax.psum_scatter(g.astype(bf16), "replica", scatter_dimension=0, tiled=True)
    return lax.all_gather(mine, "replica", axis=0, tiled=True).astype(f32)


def local(
    tokens,
    w_query,
    w_key,
    w_value,
    w_out,
    w_gate,
    w_up,
    w_down,
    gain_attn,
    gain_ffn,
    pieces,
    positions,
    cotangent,
):
    n = lax.axis_size("inner")
    place = lax.axis_index("inner")
    own = tokens.shape[0]
    length = own * n
    score_bias = -math.log(length)
    inv_root = 1.0 / math.sqrt(HEAD_DIM)
    heads = w_query.shape[1] // n // HEAD_DIM

    gains = lax.all_gather(jnp.stack([gain_attn, gain_ffn]), "inner", axis=1, tiled=True).astype(f32)
    attn_gain, ffn_gain = gains[0], gains[1]
    marks = lax.all_gather(jnp.stack([pieces, positions]), "inner", axis=1, tiled=True)
    pieces, positions = marks[0], marks[1]

    wq, wk, wv = column_shard(w_query), column_shard(w_key), column_shard(w_value)
    wg, wu = column_shard(w_gate), column_shard(w_up)

    x = gather_tokens(tokens).astype(f32)
    cot = gather_tokens(cotangent)
    cosine, sine = rope_tables(positions)
    r1 = rms_scale(x)
    u1 = x * r1
    n1 = (u1 * attn_gain).astype(bf16)
    q = rotate(dot(n1, wq), cosine, sine).astype(bf16).reshape(length, heads, HEAD_DIM)
    k = rotate(dot(n1, wk), cosine, sine).astype(bf16).reshape(length, heads, HEAD_DIM)
    v = dot(n1, wv).astype(bf16).reshape(length, heads, HEAD_DIM)

    index = jnp.arange(length)
    visible = (index[None, :] <= index[:, None]) | (
        (index[None, :] // PIECE == index[:, None] // PIECE) & (pieces[:, None] >= 0)
    )
    visible = visible.astype(f32)[None]

    def weights():
        score = jnp.einsum("qhd,khd->hqk", q, k, preferred_element_type=f32) * inv_root + score_bias
        sg = jax.nn.sigmoid(score)
        return sg, (sg * visible).astype(bf16)

    sg, p = weights()
    o = jnp.einsum("hqk,khd->qhd", p, v, preferred_element_type=f32).astype(bf16).reshape(length, -1)
    a = scatter_tokens(dot(o, w_out))
    mid = tokens.astype(f32) + a
    r2 = rms_scale(mid)
    u2 = mid * r2
    n2 = gather_tokens((u2 * ffn_gain).astype(bf16))

    gate = dot(n2, wg)
    up = dot(n2, wu)
    s = jax.nn.sigmoid(gate)
    silu = gate * s
    hid = (silu * up).astype(bf16)
    mlp = scatter_tokens(dot(hid, w_down))
    output = (mid + mlp).astype(bf16)

    ghid = dot_t(cot, w_down)
    ggate = (ghid * up * s * (1.0 + gate * (1.0 - s))).astype(bf16)
    gup = (ghid * silu).astype(bf16)
    gn2 = scatter_tokens(dot_t(ggate, wg) + dot_t(gup, wu))
    gu2 = gn2 * ffn_gain
    ffn_gain_part = jnp.sum(gn2 * u2, axis=0)
    gmid = cotangent.astype(f32) + r2 * (gu2 - u2 * jnp.mean(gu2 * u2, axis=1, keepdims=True))
    ga = gather_tokens(gmid.astype(bf16))

    grad_down = sum_copies(t_dot(hid, cot))
    grad_gate = owner_rows(t_dot(n2, ggate))
    grad_up = owner_rows(t_dot(n2, gup))

    go = dot_t(ga, w_out).astype(bf16).reshape(length, heads, HEAD_DIM)
    grad_out = sum_copies(t_dot(o, ga))
    gp = jnp.einsum("qhd,khd->hqk", go, v, preferred_element_type=f32)
    gs = (gp * sg * (1.0 - sg) * visible).astype(bf16)
    gq = jnp.einsum("hqk,khd->qhd", gs, k, preferred_element_type=f32).reshape(length, -1) * inv_root
    gk = jnp.einsum("hqk,qhd->khd", gs, q, preferred_element_type=f32).reshape(length, -1) * inv_root
    gv = jnp.einsum("hqk,qhd->khd", p, go, preferred_element_type=f32).reshape(length, -1)
    gql = rotate(gq, cosine, -sine).astype(bf16)
    gkl = rotate(gk, cosine, -sine).astype(bf16)
    gvl = gv.astype(bf16)
    gn1 = scatter_tokens(dot_t(gql, wq) + dot_t(gkl, wk) + dot_t(gvl, wv))
    grad_query = owner_rows(t_dot(n1, gql))
    grad_key = owner_rows(t_dot(n1, gkl))
    grad_value = owner_rows(t_dot(n1, gvl))

    own_x = tokens.astype(f32)
    r1 = rms_scale(own_x)
    u1 = own_x * r1
    gu1 = gn1 * attn_gain
    attn_gain_part = jnp.sum(gn1 * u1, axis=0)
    grad_tokens = gmid + r1 * (gu1 - u1 * jnp.mean(gu1 * u1, axis=1, keepdims=True))
    gain_sum = lax.psum(jnp.stack([attn_gain_part, ffn_gain_part]), ("replica", "inner"))
    rows = gain_attn.shape[0]
    gain_sum = lax.dynamic_slice_in_dim(gain_sum, place * rows, rows, 1)
    return (
        output,
        grad_tokens,
        grad_query,
        grad_key,
        grad_value,
        grad_out,
        grad_gate,
        grad_up,
        grad_down,
        gain_sum[0],
        gain_sum[1],
    )


def solution(mesh):
    tok = P(("replica", "inner"), None)
    row = P("inner", None)
    vec = P("inner")
    mark = P(("replica", "inner"))
    return jax.shard_map(
        local,
        mesh=mesh,
        in_specs=(tok, row, row, row, row, row, row, row, vec, vec, mark, mark, tok),
        out_specs=(tok, tok, row, row, row, row, row, row, row, vec, vec),
        check_vma=False,
    )
```

```python
import functools
import math

import jax
import jax.numpy as jnp
from jax import lax
from jax.experimental import pallas as pl
from jax.experimental.pallas import tpu as pltpu
from jax.sharding import PartitionSpec as P

HEAD_DIM = 128
PIECE = 256
epsilon = 1e-06
rope_base = 10000.0
dims_rows = (((1,), (1,)), ((), ()))
dims_cols = (((0,), (0,)), ((), ()))
f32 = jnp.float32
bf16 = jnp.bfloat16


def dot(a, b):
    return jnp.dot(a, b, preferred_element_type=f32)


def dot_t(a, b):
    return lax.dot_general(a, b, dims_rows, preferred_element_type=f32)


def t_dot(a, b):
    return lax.dot_general(a, b, dims_cols, preferred_element_type=f32)


def rope_tables(positions):
    half_dim = HEAD_DIM // 2
    frequency = rope_base ** (-jnp.arange(half_dim, dtype=f32) * 2.0 / HEAD_DIM)
    angle = positions.astype(f32)[:, None] * frequency[None, :]
    cosine, sine = jnp.cos(angle), jnp.sin(angle)
    return jnp.concatenate([cosine, cosine], axis=1), jnp.concatenate([-sine, sine], axis=1)


def rms_scale(values):
    return lax.rsqrt(jnp.mean(values * values, axis=1, keepdims=True) + epsilon)


def rcopy(src, dst, ssem, rsem, to):
    return pltpu.make_async_remote_copy(
        src_ref=src,
        dst_ref=dst,
        send_sem=ssem,
        recv_sem=rsem,
        device_id={"inner": to},
        device_id_type=pl.DeviceIdType.MESH,
    )


def signal(sem, to):
    pl.semaphore_signal(sem, inc=1, device_id={"inner": to}, device_id_type=pl.DeviceIdType.MESH)


def line_body(n, n_ag, n_rs, a2a_blocks, parts, *refs):
    refs = list(refs)
    nz = n // 2
    n_a2a = len(a2a_blocks)
    take = lambda count: [refs.pop(0) for _ in range(count)]
    ag_in, rs_in, a2a_in = take(n_ag), take(n_rs), [take(t[0]) for t in a2a_blocks]
    ag_out, rs_out, a2a_out = take(n_ag), take(n_rs), take(n_a2a)
    ag_sem = [take(7) for _ in range(n_ag)]
    rs_scr = [take(9) for _ in range(n_rs)]
    a2a_sem = [take(3) for _ in range(n_a2a)]
    me = lax.axis_index("inner")
    z, c = me // 2, lax.rem(me, 2)
    sib = me + 1 - 2 * c
    barrier = pltpu.get_barrier_semaphore()
    if n_a2a:
        for k in range(1, n):
            signal(barrier, lax.rem(me + k, n))
        pl.semaphore_wait(barrier, n - 1)
    else:
        signal(barrier, sib)

        @pl.when(z + 1 < nz)
        def _():
            signal(barrier, me + 2)

        @pl.when(z > 0)
        def _():
            signal(barrier, me - 2)

        pl.semaphore_wait(barrier, 1 + (z + nz - 1) // nz + (2 * nz - 2 - z) // nz)

    def rows_of(ref, j):
        count = ref.shape[0] // parts
        return pl.ds(pl.multiple_of(j * count, count), count)

    class Gather:
        def __init__(self, x, out, sems):
            self.x, self.out = x, out
            self.own_sem, self.rs, self.rr, self.ls, self.lr, self.ss, self.sr = sems

        def own(self):
            return pltpu.make_async_copy(self.x, self.out.at[me], self.own_sem)

        def piece(self, block, s, j):
            rows = rows_of(self.x, j)
            return self.x.at[rows] if s == 0 else self.out.at[block, rows]

        def right(self, s, j):
            b = me - 2 * s
            dst = self.out.at[b, rows_of(self.x, j)]
            return rcopy(self.piece(b, s, j), dst, self.rs.at[s, j], self.rr.at[s + 1, j], me + 2)

        def left(self, s, j):
            b = me + 2 * s
            dst = self.out.at[b, rows_of(self.x, j)]
            return rcopy(self.piece(b, s, j), dst, self.ls.at[s, j], self.lr.at[s + 1, j], me - 2)

        def side(self, s, k, j):
            b = me - 2 * s if k == 0 else me + 2 * s
            dst = self.out.at[b, rows_of(self.x, j)]
            return rcopy(self.piece(b, s, j), dst, self.ss.at[k, s, j], self.sr.at[k, s, j], sib)

        def from_left(self, s, j):
            dst = self.out.at[me - 2 * s, rows_of(self.x, j)]
            return rcopy(dst, dst, self.rs.at[s, j], self.rr.at[s, j], me - 2)

        def from_right(self, s, j):
            dst = self.out.at[me + 2 * s, rows_of(self.x, j)]
            return rcopy(dst, dst, self.ls.at[s, j], self.lr.at[s, j], me + 2)

        def from_side(self, s, k, j):
            b = sib - 2 * s if k == 0 else sib + 2 * s
            dst = self.out.at[b, rows_of(self.x, j)]
            return rcopy(dst, dst, self.ss.at[k, s, j], self.sr.at[k, s, j], sib)

        def begin(self):
            @pl.loop(0, parts)
            def _(j):
                @pl.when(z + 1 < nz)
                def _():
                    self.right(0, j).start()

                @pl.when(z > 0)
                def _():
                    self.left(0, j).start()

            self.own().start()

            @pl.loop(0, parts)
            def _(j):
                self.side(0, 0, j).start()

        def step(self, s, j):
            @pl.when(z >= s)
            def _():
                self.from_left(s, j).wait_recv()

                @pl.when(z + 1 < nz)
                def _():
                    self.right(s, j).start()

                self.side(s, 0, j).start()

            @pl.when(z + s < nz)
            def _():
                self.from_right(s, j).wait_recv()

                @pl.when(z > 0)
                def _():
                    self.left(s, j).start()

                self.side(s, 1, j).start()

        def end(self):
            self.own().wait()
            for s in range(nz):
                @pl.loop(0, parts)
                def _(j):
                    @pl.when(z >= s)
                    def _():
                        @pl.when(z + 1 < nz)
                        def _():
                            self.right(s, j).wait_send()

                        self.side(s, 0, j).wait_send()
                        self.from_side(s, 0, j).wait_recv()

                    @pl.when(z + s < nz)
                    def _():
                        @pl.when(z > 0)
                        def _():
                            self.left(s, j).wait_send()

                        if s > 0:
                            self.side(s, 1, j).wait_send()
                            self.from_side(s, 1, j).wait_recv()

    class Scatter:
        def __init__(self, p, out, scratch):
            self.p, self.out = p, out
            self.sib_buf, self.l_buf, self.r_buf, self.ss, self.sr, self.rs, self.rr, self.ls, self.lr = scratch
            self.count = out.shape[0] // parts

        def side(self, d, j):
            rows = rows_of(self.out, j)
            return rcopy(self.p.at[2 * d + 1 - c, rows], self.sib_buf.at[d, rows], self.ss.at[d, j], self.sr.at[d, j], sib)

        def right(self, d, j, to=2):
            rows = rows_of(self.out, j)
            return rcopy(self.l_buf.at[d, rows], self.l_buf.at[d, rows], self.rs.at[d, j], self.rr.at[d, j], me + to)

        def left(self, d, j, to=-2):
            rows = rows_of(self.out, j)
            return rcopy(self.r_buf.at[d, rows], self.r_buf.at[d, rows], self.ls.at[d, j], self.lr.at[d, j], me + to)

        def begin(self):
            for s in range(nz // 2):
                for d in (nz - 1 - s, s):
                    @pl.loop(0, parts)
                    def _(j):
                        self.side(d, j).start()

        def pair(self, d, rows):
            return self.p[2 * d + c, rows, :].astype(f32) + self.sib_buf[d, rows, :].astype(f32)

        def step(self, s, j):
            rows = rows_of(self.out, j)
            d = nz - s

            @pl.when(d > z)
            def _():
                self.side(d, j).wait_recv()

                @pl.when(z > 0)
                def _():
                    self.right(d, j, -2).wait_recv()
                    self.l_buf[d, rows, :] = (self.pair(d, rows) + self.l_buf[d, rows, :].astype(f32)).astype(bf16)

                @pl.when(z == 0)
                def _():
                    self.l_buf[d, rows, :] = self.pair(d, rows).astype(bf16)

                self.right(d, j).start()

            e = s - 1

            @pl.when(e < z)
            def _():
                self.side(e, j).wait_recv()

                @pl.when(z + 1 < nz)
                def _():
                    self.left(e, j, 2).wait_recv()
                    self.r_buf[e, rows, :] = (self.pair(e, rows) + self.r_buf[e, rows, :].astype(f32)).astype(bf16)

                @pl.when(z + 1 == nz)
                def _():
                    self.r_buf[e, rows, :] = self.pair(e, rows).astype(bf16)

                self.left(e, j).start()

        def end(self):
            @pl.loop(0, parts)
            def _(j):
                rows = rows_of(self.out, j)
                self.side(z, j).wait_recv()
                self.out[rows, :] = self.pair(z, rows)

                @pl.when(z > 0)
                def _():
                    self.right(z, j, -2).wait_recv()
                    self.out[rows, :] = self.out[rows, :] + self.l_buf[z, rows, :].astype(f32)

                @pl.when(z + 1 < nz)
                def _():
                    self.left(z, j, 2).wait_recv()
                    self.out[rows, :] = self.out[rows, :] + self.r_buf[z, rows, :].astype(f32)

            for d in range(nz):
                @pl.loop(0, parts)
                def _(j):
                    self.side(d, j).wait_send()

                    @pl.when(d > z)
                    def _():
                        self.right(d, j).wait_send()

                    @pl.when(d < z)
                    def _():
                        self.left(d, j).wait_send()

    class Exchange:
        def __init__(self, src, dst, sems, blocks):
            self.src, self.dst = src, dst
            self.own_sem, self.send, self.recv = sems
            _, self.src_of, self.dst_of, self.count = blocks

        def to(self, k, m):
            other = lax.rem(me + k, n)
            return rcopy(
                self.src_of(self.src, other, m), self.dst_of(self.dst, me, m), self.send.at[k, m], self.recv.at[k, m], other
            )

        def came(self, k, m):
            other = lax.rem(me - k + n, n)
            return rcopy(
                self.src_of(self.src, other, m), self.dst_of(self.dst, other, m), self.send.at[k, m], self.recv.at[k, m], other
            )

        def own(self, m):
            return pltpu.make_async_copy(
                self.src_of(self.src, me, m), self.dst_of(self.dst, me, m), self.own_sem.at[m]
            )

        def begin(self):
            for k in range(1, n):
                for m in range(self.count):
                    self.to(k, m).start()
            for m in range(self.count):
                self.own(m).start()

        def step(self, s, j):
            pass

        def end(self):
            for m in range(self.count):
                self.own(m).wait()
            for k in range(1, n):
                for m in range(self.count):
                    self.came(k, m).wait_recv()
                    self.to(k, m).wait_send()

    parts_of = [Gather(*t) for t in zip(ag_in, ag_out, ag_sem)]
    parts_of += [Scatter(*t) for t in zip(rs_in, rs_out, rs_scr)]
    parts_of += [Exchange(*t) for t in zip(a2a_in, a2a_out, a2a_sem, a2a_blocks)]
    for part in parts_of:
        part.begin()
    if n_ag + n_rs:
        for s in range(1, nz):
            @pl.loop(0, parts)
            def _(j):
                for part in parts_of:
                    part.step(s, j)
    for part in parts_of:
        part.end()


def line_comm(cid, name, ag=(), rs=(), a2a=(), parts=2):
    n = lax.axis_size("inner")
    nz = n // 2
    dma = pltpu.SemaphoreType.DMA
    hbm = pl.BlockSpec(memory_space=pl.ANY)
    vmem = pl.BlockSpec(memory_space=pltpu.VMEM)
    rs = [p.reshape((n, p.shape[0] // n) + p.shape[1:]) for p in rs]
    out_shape = [jax.ShapeDtypeStruct((n,) + x.shape, x.dtype) for x in ag]
    out_shape += [jax.ShapeDtypeStruct(p.shape[1:], f32) for p in rs]
    out_shape += [jax.ShapeDtypeStruct(t[1], t[0][0].dtype) for t in a2a]
    scratch = []
    for _ in ag:
        scratch += [dma, dma((nz, parts)), dma((nz + 1, parts)), dma((nz, parts)), dma((nz + 1, parts))]
        scratch += [dma((2, nz, parts)), dma((2, nz, parts))]
    for p in rs:
        scratch += [pltpu.VMEM((nz,) + p.shape[1:], bf16)] * 3 + [dma((nz, parts))] * 6
    for t in a2a:
        scratch += [dma((t[4],)), dma((n, t[4])), dma((n, t[4]))]
    outs = pl.pallas_call(
        functools.partial(line_body, n, len(ag), len(rs), [(len(t[0]),) + t[2:5] for t in a2a], parts),
        out_shape=out_shape,
        in_specs=[hbm] * len(ag) + [vmem] * len(rs) + [hbm] * sum(len(t[0]) for t in a2a),
        out_specs=[hbm] * len(ag) + [vmem] * len(rs) + [hbm] * len(a2a),
        scratch_shapes=scratch,
        compiler_params=pltpu.CompilerParams(
            collective_id=cid, has_side_effects=True, vmem_limit_bytes=48 * 2**20
        ),
        name=name,
    )(*ag, *rs, *[w for t in a2a for w in t[0]])
    outs = [o.reshape((-1,) + o.shape[2:]) if i < len(ag) else o for i, o in enumerate(outs)]
    return outs


def rotate(flat, cosine, sine):
    return flat * cosine + pltpu.roll(flat, HEAD_DIM // 2, 1) * sine


def squash(q, k, piece, keys, length):
    scale = -math.log2(math.e) / math.sqrt(HEAD_DIM)
    sg = 1.0 / (1.0 + jnp.exp2(dot_t(q, k) * scale + math.log2(length)))
    row = lax.broadcasted_iota(jnp.int32, (PIECE, PIECE), 0)
    col = lax.broadcasted_iota(jnp.int32, (PIECE, PIECE), 1)
    return sg, (col <= row) | (piece >= 0)


def masked(value, visible, keys):
    last = jnp.where(visible, value[:, keys - PIECE :], 0.0)
    return last if keys == PIECE else jnp.concatenate([value[:, : keys - PIECE], last], axis=1)


def attn_body(heads, length, lin, cosine, sine, piece, out, rot):
    h, b = pl.program_id(0), pl.program_id(1)
    at = lambda part: pl.ds(pl.multiple_of((part * heads + h) * HEAD_DIM, HEAD_DIM), HEAD_DIM)
    blocks = length // PIECE

    @pl.when(b == 0)
    def _():
        @pl.loop(0, blocks)
        def _(i):
            rows = pl.ds(pl.multiple_of(i * PIECE, PIECE), PIECE)
            for part in (0, 1):
                rot[rows, at(part)] = rotate(lin[rows, at(part)], cosine[rows, :], sine[rows, :]).astype(bf16)
            rot[rows, at(2)] = lin[rows, at(2)].astype(bf16)

    for i in range(blocks):
        @pl.when(b == i)
        def _():
            keys = (i + 1) * PIECE
            own = pl.ds(i * PIECE, PIECE)
            sg, visible = squash(rot[own, at(0)], rot[0:keys, at(1)], piece[...], keys, length)
            out[...] = dot(masked(sg, visible, keys).astype(bf16), rot[0:keys, at(2)]).astype(bf16)


def attention(lin, cosine, sine, piece):
    length, width = lin.shape
    heads = width // 3 // HEAD_DIM
    whole = lambda x: pl.BlockSpec(x.shape, lambda h, b: (0, 0))
    return pl.pallas_call(
        functools.partial(attn_body, heads, length),
        grid=(heads, length // PIECE),
        out_shape=[
            jax.ShapeDtypeStruct((length, width // 3), bf16),
            jax.ShapeDtypeStruct((length, width), bf16),
        ],
        in_specs=[whole(lin), whole(cosine), whole(sine), pl.BlockSpec((PIECE, 1), lambda h, b: (b, 0))],
        out_specs=[
            pl.BlockSpec((PIECE, HEAD_DIM), lambda h, b: (b, h)),
            pl.BlockSpec((length, width), lambda h, b: (0, 0)),
        ],
        compiler_params=pltpu.CompilerParams(vmem_limit_bytes=48 * 2**20),
        cost_estimate=pl.CostEstimate(
            flops=4 * heads * length * length * HEAD_DIM // 2, bytes_accessed=8 * length * width, transcendentals=heads * length * length
        ),
        name="attention",
    )(lin, cosine, sine, piece)


def attn_back_body(heads, length, rot, go, cosine, sine, piece, out, gk, gv):
    h, b = pl.program_id(0), pl.program_id(1)
    at = lambda part: pl.ds(pl.multiple_of((part * heads + h) * HEAD_DIM, HEAD_DIM), HEAD_DIM)
    blocks = length // PIECE
    inv_root = 1.0 / math.sqrt(HEAD_DIM)

    @pl.when(b == 0)
    def _():
        gk[...] = jnp.zeros_like(gk)
        gv[...] = jnp.zeros_like(gv)

    for i in range(blocks):
        @pl.when(b == i)
        def _():
            keys = (i + 1) * PIECE
            own = pl.ds(i * PIECE, PIECE)
            q, g = rot[own, at(0)], go[...]
            sg, visible = squash(q, rot[0:keys, at(1)], piece[...], keys, length)
            p = masked(sg, visible, keys).astype(bf16)
            gs = masked(dot_t(g, rot[0:keys, at(2)]) * sg * (1.0 - sg), visible, keys).astype(bf16)
            gq = dot(gs, rot[0:keys, at(1)]) * inv_root
            out[own, at(0)] = rotate(gq, cosine[own, :], -sine[own, :]).astype(bf16)
            gk[0:keys, :] += t_dot(gs, q)
            gv[0:keys, :] += t_dot(p, g)

    @pl.when(b == blocks - 1)
    def _():
        @pl.loop(0, blocks)
        def _(i):
            rows = pl.ds(pl.multiple_of(i * PIECE, PIECE), PIECE)
            out[rows, at(1)] = rotate(gk[rows, :] * inv_root, cosine[rows, :], -sine[rows, :]).astype(bf16)
            out[rows, at(2)] = gv[rows, :].astype(bf16)


def attention_back(rot, go, cosine, sine, piece):
    length, width = rot.shape
    heads = width // 3 // HEAD_DIM
    whole = lambda x: pl.BlockSpec(x.shape, lambda h, b: (0, 0))
    return pl.pallas_call(
        functools.partial(attn_back_body, heads, length),
        grid=(heads, length // PIECE),
        out_shape=jax.ShapeDtypeStruct((length, width), bf16),
        in_specs=[
            whole(rot),
            pl.BlockSpec((PIECE, HEAD_DIM), lambda h, b: (b, h)),
            whole(cosine),
            whole(sine),
            pl.BlockSpec((PIECE, 1), lambda h, b: (b, 0)),
        ],
        out_specs=pl.BlockSpec((length, width), lambda h, b: (0, 0)),
        scratch_shapes=[pltpu.VMEM((length, HEAD_DIM), f32)] * 2,
        compiler_params=pltpu.CompilerParams(vmem_limit_bytes=48 * 2**20),
        cost_estimate=pl.CostEstimate(
            flops=10 * heads * length * length * HEAD_DIM // 2, bytes_accessed=8 * length * width, transcendentals=heads * length * length
        ),
        name="attention_back",
    )(rot, go, cosine, sine, piece)


def gain_body(n, nr, g, out, group, copies, ss, sr, cs, cr):
    me, r = lax.axis_index("inner"), lax.axis_index("replica")
    mesh_id = pl.DeviceIdType.MESH
    barrier = pltpu.get_barrier_semaphore()
    for k in range(1, n):
        signal(barrier, lax.rem(me + k, n))
    for k in range(1, nr):
        pl.semaphore_signal(barrier, inc=1, device_id={"replica": lax.rem(r + k, nr)}, device_id_type=mesh_id)
    pl.semaphore_wait(barrier, n + nr - 2)

    def inside(k):
        to = lax.rem(me + k, n)
        return rcopy(g.at[to], group.at[k], ss.at[k], sr.at[k], to)

    def across(k):
        return pltpu.make_async_remote_copy(
            src_ref=copies.at[0],
            dst_ref=copies.at[k],
            send_sem=cs.at[k],
            recv_sem=cr.at[k],
            device_id={"replica": lax.rem(r + k, nr)},
            device_id_type=mesh_id,
        )

    for k in range(1, n):
        inside(k).start()
    total = g[me]
    for k in range(1, n):
        inside(k).wait_recv()
        total = total + group[k]
    copies[0] = total
    for k in range(1, nr):
        across(k).start()
    for k in range(1, nr):
        across(k).wait_recv()
        total = total + copies[k]
    out[...] = total
    for k in range(1, n):
        inside(k).wait_send()
    for k in range(1, nr):
        across(k).wait_send()


def gain_sum(cid, parts):
    n, nr = lax.axis_size("inner"), lax.axis_size("replica")
    cols = parts.shape[1] // n
    g = jnp.zeros((n, 8, cols), f32).at[:, :2].set(parts.reshape(2, n, cols).transpose(1, 0, 2))
    dma = pltpu.SemaphoreType.DMA
    vmem = pl.BlockSpec(memory_space=pltpu.VMEM)
    return pl.pallas_call(
        functools.partial(gain_body, n, nr),
        out_shape=jax.ShapeDtypeStruct((8, cols), f32),
        in_specs=[vmem],
        out_specs=vmem,
        scratch_shapes=[
            pltpu.VMEM((n, 8, cols), f32),
            pltpu.VMEM((nr, 8, cols), f32),
            dma((n,)),
            dma((n,)),
            dma((nr,)),
            dma((nr,)),
        ],
        compiler_params=pltpu.CompilerParams(collective_id=cid, has_side_effects=True),
        name="gain_sum",
    )(g)[:2]


def columns_out(weights):
    n, nr = lax.axis_size("inner"), lax.axis_size("replica")
    part = weights[0].shape[0] // nr
    cols = weights[0].shape[1] // n

    def source(refs, other, m):
        rows = pl.ds(pl.multiple_of(lax.axis_index("replica") * part, part), part)
        return refs[m].at[rows, pl.ds(pl.multiple_of(other * cols, cols), cols)]

    def target(ref, other, m):
        return ref.at[other, :, pl.ds(m * cols, cols)]

    return (tuple(weights), (n, part, cols * len(weights)), source, target, len(weights))


def to_all(block):
    n = lax.axis_size("inner")
    return ((block,), (n,) + block.shape, lambda refs, other, m: refs[0], lambda ref, other, m: ref.at[other], 1)


def rows_back(share, count):
    n, part, width = share.shape
    cols = width // count

    def source(refs, other, m):
        return refs[0].at[other, :, pl.ds(m * cols, cols)]

    def target(ref, other, m):
        return ref.at[m, :, pl.ds(pl.multiple_of(other * cols, cols), cols)]

    return ((share,), (count, part, n * cols), source, target, count)


def all_copies(block):
    n, part, cols = block.shape
    full = lax.all_gather(block, "replica", axis=0, tiled=False)
    return full.transpose(1, 0, 2, 3).reshape(-1, cols)


def sum_parts(products):
    n, nr = lax.axis_size("inner"), lax.axis_size("replica")
    g = jnp.concatenate([p.astype(bf16) for p in products], axis=1)
    part = g.shape[0] // n // nr
    g = g.reshape(n, nr, part, -1).transpose(1, 0, 2, 3).reshape(nr * n * part, -1)
    return lax.psum_scatter(g, "replica", scatter_dimension=0, tiled=True).reshape(n, part, -1)


def join(block, axis):
    return lax.all_gather(block, "replica", axis=axis, tiled=False)


def local(
    tokens,
    w_query,
    w_key,
    w_value,
    w_out,
    w_gate,
    w_up,
    w_down,
    gain_attn,
    gain_ffn,
    pieces,
    positions,
    cotangent,
):
    n = lax.axis_size("inner")
    nr = lax.axis_size("replica")
    own, width = tokens.shape
    length = own * n
    rows = gain_attn.shape[0]

    marks = jnp.zeros((8, own), jnp.int32).at[0].set(pieces).at[1].set(positions)
    gains = jnp.zeros((8, rows), f32).at[0].set(gain_attn.astype(f32)).at[1].set(gain_ffn.astype(f32))
    qkv_share, marks, gains = line_comm(
        0, "load_attn", a2a=[columns_out([w_query, w_key, w_value]), to_all(marks), to_all(gains)]
    )
    w_qkv = all_copies(qkv_share)
    x, gu_share = line_comm(1, "load_ffn", ag=[tokens], a2a=[columns_out([w_gate, w_up])])
    w_gu = all_copies(gu_share)
    w_g, w_u = w_gu[:, : w_gu.shape[1] // 2], w_gu[:, w_gu.shape[1] // 2 :]
    pieces, positions = marks[:, 0].reshape(length, 1), marks[:, 1].reshape(length)
    attn_gain, ffn_gain = gains[:, 0].reshape(-1), gains[:, 1].reshape(-1)

    x = x.astype(f32)
    cosine, sine = rope_tables(positions)
    u1 = x * rms_scale(x)
    n1 = (u1 * attn_gain).astype(bf16)
    o, rot = attention(dot(n1, w_qkv), cosine, sine, pieces)
    cot, a = line_comm(2, "attn_out", ag=[cotangent], rs=[dot(o, w_out).astype(bf16)])
    mid = tokens.astype(f32) + a
    r2 = rms_scale(mid)
    u2 = mid * r2
    (n2,) = line_comm(3, "gather_n2", ag=[(u2 * ffn_gain).astype(bf16)])

    gate = dot(n2, w_g)
    up = dot(n2, w_u)
    s = jax.nn.sigmoid(gate)
    silu = gate * s
    hid = (silu * up).astype(bf16)
    down_share = lax.psum_scatter(t_dot(hid, cot).astype(bf16), "replica", scatter_dimension=0, tiled=True)
    ghid = dot_t(cot, w_down)
    ggate = (ghid * up * s * (1.0 + gate * (1.0 - s))).astype(bf16)
    gup = (ghid * silu).astype(bf16)
    gu_share = sum_parts([t_dot(n2, ggate), t_dot(n2, gup)])
    (gn2,) = line_comm(4, "scatter_gn2", rs=[(dot_t(ggate, w_g) + dot_t(gup, w_u)).astype(bf16)])
    gu2 = gn2 * ffn_gain
    ffn_gain_part = jnp.sum(gn2 * u2, axis=0)
    gmid = cotangent.astype(f32) + r2 * (gu2 - u2 * jnp.mean(gu2 * u2, axis=1, keepdims=True))
    ga, mlp = line_comm(5, "gather_ga", ag=[gmid.astype(bf16)], rs=[dot(hid, w_down).astype(bf16)])
    output = (mid + mlp).astype(bf16)

    go = dot_t(ga, w_out).astype(bf16)
    out_share = lax.psum_scatter(t_dot(o, ga).astype(bf16), "replica", scatter_dimension=0, tiled=True)
    gqkv = attention_back(rot, go, cosine, sine, pieces)
    qkv_share = sum_parts([t_dot(n1, gqkv)])
    gn1_part = dot_t(gqkv, w_qkv)
    attn_gain_part = jnp.sum(gn1_part * u1, axis=0)
    (gn1,) = line_comm(6, "scatter_gn1", rs=[gn1_part.astype(bf16)])
    (gu_rows,) = line_comm(7, "rows_ffn", a2a=[rows_back(gu_share, 2)])
    (qkv_rows,) = line_comm(8, "rows_attn", a2a=[rows_back(qkv_share, 3)])
    gain_rows = gain_sum(9, jnp.stack([attn_gain_part, ffn_gain_part]))

    grad_down = join(down_share, 0).reshape(w_down.shape).astype(f32)
    grad_out = join(out_share, 0).reshape(w_out.shape).astype(f32)
    grad_gu = join(gu_rows, 0).astype(f32)
    grad_qkv = join(qkv_rows, 0).astype(f32)

    own_x = tokens.astype(f32)
    r1 = rms_scale(own_x)
    u1 = own_x * r1
    gu1 = gn1 * attn_gain
    grad_tokens = gmid + r1 * (gu1 - u1 * jnp.mean(gu1 * u1, axis=1, keepdims=True))
    return (
        output,
        grad_tokens,
        grad_qkv[:, 0].reshape(w_query.shape),
        grad_qkv[:, 1].reshape(w_key.shape),
        grad_qkv[:, 2].reshape(w_value.shape),
        grad_out,
        grad_gu[:, 0].reshape(w_gate.shape),
        grad_gu[:, 1].reshape(w_up.shape),
        grad_down,
        gain_rows[0],
        gain_rows[1],
    )


def solution(mesh):
    tok = P(("replica", "inner"), None)
    row = P("inner", None)
    vec = P("inner")
    mark = P(("replica", "inner"))
    return jax.shard_map(
        local,
        mesh=mesh,
        in_specs=(tok, row, row, row, row, row, row, row, vec, vec, mark, mark, tok),
        out_specs=(tok, tok, row, row, row, row, row, row, row, vec, vec),
        check_vma=False,
    )
```

```python
import functools
import math

import jax
import jax.numpy as jnp
from jax import lax
from jax.experimental import pallas as pl
from jax.experimental.pallas import tpu as pltpu
from jax.sharding import PartitionSpec as P

HEAD_DIM = 128
PIECE = 256
epsilon = 1e-06
rope_base = 10000.0
dims_rows = (((1,), (1,)), ((), ()))
dims_cols = (((0,), (0,)), ((), ()))
f32 = jnp.float32
bf16 = jnp.bfloat16


def dot(a, b):
    return jnp.dot(a, b, preferred_element_type=f32)


def dot_t(a, b):
    return lax.dot_general(a, b, dims_rows, preferred_element_type=f32)


def t_dot(a, b):
    return lax.dot_general(a, b, dims_cols, preferred_element_type=f32)


def rope_tables(positions):
    half_dim = HEAD_DIM // 2
    frequency = rope_base ** (-jnp.arange(half_dim, dtype=f32) * 2.0 / HEAD_DIM)
    angle = positions.astype(f32)[:, None] * frequency[None, :]
    cosine, sine = jnp.cos(angle), jnp.sin(angle)
    return jnp.concatenate([cosine, cosine], axis=1), jnp.concatenate([-sine, sine], axis=1)


def rms_scale(values):
    return lax.rsqrt(jnp.mean(values * values, axis=1, keepdims=True) + epsilon)


def rcopy(src, dst, ssem, rsem, to, axis="inner"):
    return pltpu.make_async_remote_copy(
        src_ref=src,
        dst_ref=dst,
        send_sem=ssem,
        recv_sem=rsem,
        device_id={axis: to},
        device_id_type=pl.DeviceIdType.MESH,
    )


def signal(sem, to, axis="inner"):
    pl.semaphore_signal(sem, inc=1, device_id={axis: to}, device_id_type=pl.DeviceIdType.MESH)


def line_body(n, n_ag, n_rs, a2a_blocks, spreads, n_sum, parts, *refs):
    refs = list(refs)
    nz = n // 2
    n_a2a = len(a2a_blocks)
    take = lambda count: [refs.pop(0) for _ in range(count)]
    n_sp = len(spreads)
    ag_in, rs_in, a2a_in = take(n_ag), take(n_rs), [take(t[0]) for t in a2a_blocks]
    sp_in, sum_in = take(n_sp), take(n_sum)
    ag_out, rs_out, a2a_out, sp_out, sum_out = take(n_ag), take(n_rs), take(n_a2a), take(n_sp), take(n_sum)
    ag_sem = [take(7) for _ in range(n_ag)]
    rs_scr = [take(9) for _ in range(n_rs)]
    a2a_sem = [take(3) for _ in range(n_a2a)]
    sp_sem = [take(5) for _ in range(n_sp)]
    sum_scr = [take(6) for _ in range(n_sum)]
    me = lax.axis_index("inner")
    z, c = me // 2, lax.rem(me, 2)
    sib = me + 1 - 2 * c
    r = lax.axis_index("replica")
    across_x, across_y = r + 1 - 2 * lax.rem(r, 2), r + 2 - 4 * (r // 2)
    barrier = pltpu.get_barrier_semaphore()
    more = 0
    if n_sp + n_sum:
        signal(barrier, across_x, "replica")
        signal(barrier, across_y, "replica")
        more = 2
    if n_a2a:
        for k in range(1, n):
            signal(barrier, lax.rem(me + k, n))
        pl.semaphore_wait(barrier, n - 1 + more)
    else:
        signal(barrier, sib)

        @pl.when(z + 1 < nz)
        def _():
            signal(barrier, me + 2)

        @pl.when(z > 0)
        def _():
            signal(barrier, me - 2)

        pl.semaphore_wait(barrier, 1 + more + (z + nz - 1) // nz + (2 * nz - 2 - z) // nz)

    def rows_of(ref, j):
        count = ref.shape[0] // parts
        return pl.ds(pl.multiple_of(j * count, count), count)

    class Gather:
        def __init__(self, x, out, sems):
            self.x, self.out = x, out
            self.own_sem, self.rs, self.rr, self.ls, self.lr, self.ss, self.sr = sems

        def own(self):
            return pltpu.make_async_copy(self.x, self.out.at[me], self.own_sem)

        def piece(self, block, s, j):
            rows = rows_of(self.x, j)
            return self.x.at[rows] if s == 0 else self.out.at[block, rows]

        def right(self, s, j):
            b = me - 2 * s
            dst = self.out.at[b, rows_of(self.x, j)]
            return rcopy(self.piece(b, s, j), dst, self.rs.at[s, j], self.rr.at[s + 1, j], me + 2)

        def left(self, s, j):
            b = me + 2 * s
            dst = self.out.at[b, rows_of(self.x, j)]
            return rcopy(self.piece(b, s, j), dst, self.ls.at[s, j], self.lr.at[s + 1, j], me - 2)

        def side(self, s, k, j):
            b = me - 2 * s if k == 0 else me + 2 * s
            dst = self.out.at[b, rows_of(self.x, j)]
            return rcopy(self.piece(b, s, j), dst, self.ss.at[k, s, j], self.sr.at[k, s, j], sib)

        def from_left(self, s, j):
            dst = self.out.at[me - 2 * s, rows_of(self.x, j)]
            return rcopy(dst, dst, self.rs.at[s, j], self.rr.at[s, j], me - 2)

        def from_right(self, s, j):
            dst = self.out.at[me + 2 * s, rows_of(self.x, j)]
            return rcopy(dst, dst, self.ls.at[s, j], self.lr.at[s, j], me + 2)

        def from_side(self, s, k, j):
            b = sib - 2 * s if k == 0 else sib + 2 * s
            dst = self.out.at[b, rows_of(self.x, j)]
            return rcopy(dst, dst, self.ss.at[k, s, j], self.sr.at[k, s, j], sib)

        def begin(self):
            @pl.loop(0, parts)
            def _(j):
                @pl.when(z + 1 < nz)
                def _():
                    self.right(0, j).start()

                @pl.when(z > 0)
                def _():
                    self.left(0, j).start()

            self.own().start()

            @pl.loop(0, parts)
            def _(j):
                self.side(0, 0, j).start()

        def step(self, s, j):
            @pl.when(z >= s)
            def _():
                self.from_left(s, j).wait_recv()

                @pl.when(z + 1 < nz)
                def _():
                    self.right(s, j).start()

                self.side(s, 0, j).start()

            @pl.when(z + s < nz)
            def _():
                self.from_right(s, j).wait_recv()

                @pl.when(z > 0)
                def _():
                    self.left(s, j).start()

                self.side(s, 1, j).start()

        def end(self):
            self.own().wait()
            for s in range(nz):
                @pl.loop(0, parts)
                def _(j):
                    @pl.when(z >= s)
                    def _():
                        @pl.when(z + 1 < nz)
                        def _():
                            self.right(s, j).wait_send()

                        self.side(s, 0, j).wait_send()
                        self.from_side(s, 0, j).wait_recv()

                    @pl.when(z + s < nz)
                    def _():
                        @pl.when(z > 0)
                        def _():
                            self.left(s, j).wait_send()

                        if s > 0:
                            self.side(s, 1, j).wait_send()
                            self.from_side(s, 1, j).wait_recv()

    class Scatter:
        def __init__(self, p, out, scratch):
            self.p, self.out = p, out
            self.sib_buf, self.l_buf, self.r_buf, self.ss, self.sr, self.rs, self.rr, self.ls, self.lr = scratch
            self.count = out.shape[0] // parts

        def side(self, d, j):
            rows = rows_of(self.out, j)
            return rcopy(self.p.at[2 * d + 1 - c, rows], self.sib_buf.at[d, rows], self.ss.at[d, j], self.sr.at[d, j], sib)

        def right(self, d, j, to=2):
            rows = rows_of(self.out, j)
            return rcopy(self.l_buf.at[d, rows], self.l_buf.at[d, rows], self.rs.at[d, j], self.rr.at[d, j], me + to)

        def left(self, d, j, to=-2):
            rows = rows_of(self.out, j)
            return rcopy(self.r_buf.at[d, rows], self.r_buf.at[d, rows], self.ls.at[d, j], self.lr.at[d, j], me + to)

        def begin(self):
            for s in range(nz // 2):
                for d in (nz - 1 - s, s):
                    @pl.loop(0, parts)
                    def _(j):
                        self.side(d, j).start()

        def pair(self, d, rows):
            return self.p[2 * d + c, rows, :].astype(f32) + self.sib_buf[d, rows, :].astype(f32)

        def step(self, s, j):
            rows = rows_of(self.out, j)
            d = nz - s

            @pl.when(d > z)
            def _():
                self.side(d, j).wait_recv()

                @pl.when(z > 0)
                def _():
                    self.right(d, j, -2).wait_recv()
                    self.l_buf[d, rows, :] = (self.pair(d, rows) + self.l_buf[d, rows, :].astype(f32)).astype(bf16)

                @pl.when(z == 0)
                def _():
                    self.l_buf[d, rows, :] = self.pair(d, rows).astype(bf16)

                self.right(d, j).start()

            e = s - 1

            @pl.when(e < z)
            def _():
                self.side(e, j).wait_recv()

                @pl.when(z + 1 < nz)
                def _():
                    self.left(e, j, 2).wait_recv()
                    self.r_buf[e, rows, :] = (self.pair(e, rows) + self.r_buf[e, rows, :].astype(f32)).astype(bf16)

                @pl.when(z + 1 == nz)
                def _():
                    self.r_buf[e, rows, :] = self.pair(e, rows).astype(bf16)

                self.left(e, j).start()

        def end(self):
            @pl.loop(0, parts)
            def _(j):
                rows = rows_of(self.out, j)
                self.side(z, j).wait_recv()
                self.out[rows, :] = self.pair(z, rows)

                @pl.when(z > 0)
                def _():
                    self.right(z, j, -2).wait_recv()
                    self.out[rows, :] = self.out[rows, :] + self.l_buf[z, rows, :].astype(f32)

                @pl.when(z + 1 < nz)
                def _():
                    self.left(z, j, 2).wait_recv()
                    self.out[rows, :] = self.out[rows, :] + self.r_buf[z, rows, :].astype(f32)

            for d in range(nz):
                @pl.loop(0, parts)
                def _(j):
                    self.side(d, j).wait_send()

                    @pl.when(d > z)
                    def _():
                        self.right(d, j).wait_send()

                    @pl.when(d < z)
                    def _():
                        self.left(d, j).wait_send()

    class Exchange:
        def __init__(self, src, dst, sems, blocks):
            self.src, self.dst = src, dst
            self.own_sem, self.send, self.recv = sems
            _, self.src_of, self.dst_of, self.count = blocks

        def to(self, k, m):
            other = lax.rem(me + k, n)
            return rcopy(
                self.src_of(self.src, other, m), self.dst_of(self.dst, me, m), self.send.at[k, m], self.recv.at[k, m], other
            )

        def came(self, k, m):
            other = lax.rem(me - k + n, n)
            return rcopy(
                self.src_of(self.src, other, m), self.dst_of(self.dst, other, m), self.send.at[k, m], self.recv.at[k, m], other
            )

        def own(self, m):
            return pltpu.make_async_copy(
                self.src_of(self.src, me, m), self.dst_of(self.dst, me, m), self.own_sem.at[m]
            )

        def begin(self):
            for k in range(1, n):
                for m in range(self.count):
                    self.to(k, m).start()
            for m in range(self.count):
                self.own(m).start()

        def step(self, s, j):
            pass

        def end(self):
            for m in range(self.count):
                self.own(m).wait()
            for k in range(1, n):
                for m in range(self.count):
                    self.came(k, m).wait_recv()
                    self.to(k, m).wait_send()

    class Spread:
        def __init__(self, src, out, sems, phases):
            self.src, self.out, self.phases = src, out, phases
            self.own_sem, self.send, self.recv, self.send_half, self.recv_half = sems
            self.half = out.shape[1] // 2

        def own(self):
            return pltpu.make_async_copy(self.src, self.out.at[r], self.own_sem)

        def first(self, axis):
            to = across_y if axis else across_x
            return rcopy(self.src, self.out.at[r], self.send.at[axis], self.recv.at[axis], to, "replica")

        def first_came(self, axis):
            who = across_y if axis else across_x
            return rcopy(self.out.at[who], self.out.at[who], self.send.at[axis], self.recv.at[axis], who, "replica")

        def half_of(self, block, axis):
            return self.out.at[block, pl.ds(axis * self.half, self.half)]

        def second(self, axis):
            block, to = (across_x, across_y) if axis else (across_y, across_x)
            piece = self.half_of(block, axis)
            return rcopy(piece, piece, self.send_half.at[axis], self.recv_half.at[axis], to, "replica")

        def second_came(self, axis):
            piece = self.half_of(3 - r, axis)
            who = across_y if axis else across_x
            return rcopy(piece, piece, self.send_half.at[axis], self.recv_half.at[axis], who, "replica")

        def begin(self):
            if 1 in self.phases:
                self.first(0).start()
                self.first(1).start()
                self.own().start()
            else:
                self.second(0).start()
                self.second(1).start()

        def step(self, s, j):
            pass

        def mid(self):
            if self.phases == (1, 2):
                self.first_came(0).wait_recv()
                self.second(1).start()
                self.first_came(1).wait_recv()
                self.second(0).start()

        def end(self):
            if 1 in self.phases:
                self.own().wait()
                for axis in (0, 1):
                    self.first(axis).wait_send()
                    if 2 not in self.phases:
                        self.first_came(axis).wait_recv()
            if 2 in self.phases:
                for axis in (0, 1):
                    self.second(axis).wait_send()
                    self.second_came(axis).wait_recv()

    parts_of = [Gather(*t) for t in zip(ag_in, ag_out, ag_sem)]
    parts_of += [Scatter(*t) for t in zip(rs_in, rs_out, rs_scr)]
    parts_of += [Exchange(*t) for t in zip(a2a_in, a2a_out, a2a_sem, a2a_blocks)]
    class Sum:
        def __init__(self, p, out, scratch):
            self.p, self.out = p, out
            self.a, self.b, self.send_a, self.recv_a, self.send_b, self.recv_b = scratch
            self.half = out.shape[0] // 2
            self.bits = (lax.rem(r, 2), r // 2)

        def rows(self, h):
            return pl.ds(h * self.half, self.half)

        def who(self, h):
            return across_y if h else across_x

        def first(self, h, k):
            other = 1 - self.bits[h]
            q = 2 * other + k if h else other + 2 * k
            return rcopy(
                self.p.at[q, self.rows(h)], self.a.at[h, k], self.send_a.at[h, k], self.recv_a.at[h, k], self.who(h), "replica"
            )

        def second(self, h):
            piece = self.a.at[h, 1 - self.bits[1 - h]]
            return rcopy(piece, self.b.at[h], self.send_b.at[h], self.recv_b.at[h], self.who(1 - h), "replica")

        def each(self, h, put):
            step = 16

            @pl.loop(0, self.half // step)
            def _(i):
                put(pl.multiple_of(i * step, step), step)

        def mine(self, h, k, at, step):
            q = 2 * self.bits[1] + k if h else self.bits[0] + 2 * k
            rows = pl.ds(h * self.half + at, step)
            return self.p[q, rows, :].astype(f32) + self.a[h, k, pl.ds(at, step), :].astype(f32)

        def begin(self):
            for h in (0, 1):
                self.first(h, 1 - self.bits[1 - h]).start()
            for h in (0, 1):
                self.first(h, self.bits[1 - h]).start()

        def step(self, s, j):
            pass

        def mid(self):
            for h in (0, 1):
                k = 1 - self.bits[1 - h]
                self.first(h, k).wait_recv()

                def put(at, step):
                    self.a[h, k, pl.ds(at, step), :] = self.mine(h, k, at, step).astype(bf16)

                self.each(h, put)
                self.second(h).start()

        def end(self):
            for h in (0, 1):
                k = self.bits[1 - h]
                self.first(h, k).wait_recv()
                self.second(h).wait_recv()

                def put(at, step):
                    total = self.mine(h, k, at, step) + self.b[h, pl.ds(at, step), :].astype(f32)
                    self.out[pl.ds(h * self.half + at, step), :] = total.astype(bf16)

                self.each(h, put)
            for h in (0, 1):
                for k in (0, 1):
                    self.first(h, k).wait_send()
                self.second(h).wait_send()

    square_parts = [Spread(*t) for t in zip(sp_in, sp_out, sp_sem, spreads)]
    square_parts += [Sum(*t) for t in zip(sum_in, sum_out, sum_scr)]
    parts_of += square_parts
    for part in parts_of:
        part.begin()
    if n_ag + n_rs:
        for s in range(1, nz):
            @pl.loop(0, parts)
            def _(j):
                for part in parts_of:
                    part.step(s, j)

            if s == nz - 2:
                for part in square_parts:
                    part.mid()
    else:
        for part in square_parts:
            part.mid()
    for part in parts_of:
        part.end()


def line_comm(cid, name, us, ag=(), rs=(), a2a=(), spread=(), sums=(), parts=2):
    n = lax.axis_size("inner")
    nz = n // 2
    dma = pltpu.SemaphoreType.DMA
    hbm = pl.BlockSpec(memory_space=pl.ANY)
    vmem = pl.BlockSpec(memory_space=pltpu.VMEM)
    rs = [p.reshape((n, p.shape[0] // n) + p.shape[1:]) for p in rs]
    out_shape = [jax.ShapeDtypeStruct((n,) + x.shape, x.dtype) for x in ag]
    out_shape += [jax.ShapeDtypeStruct(p.shape[1:], f32) for p in rs]
    out_shape += [jax.ShapeDtypeStruct(t[1], t[0][0].dtype) for t in a2a]
    out_shape += [jax.ShapeDtypeStruct(b.shape if 1 not in ph else (4,) + b.shape, b.dtype) for b, ph in spread]
    out_shape += [jax.ShapeDtypeStruct((p.shape[0] // 4, p.shape[1]), bf16) for p in sums]
    sums = [p.reshape((4, p.shape[0] // 4) + p.shape[1:]) for p in sums]
    first_in = len(ag) + len(rs) + sum(len(t[0]) for t in a2a)
    first_out = len(ag) + len(rs) + len(a2a)
    aliases = {first_in + i: first_out + i for i, (b, ph) in enumerate(spread) if 1 not in ph}
    scratch = []
    for _ in ag:
        scratch += [dma, dma((nz, parts)), dma((nz + 1, parts)), dma((nz, parts)), dma((nz + 1, parts))]
        scratch += [dma((2, nz, parts)), dma((2, nz, parts))]
    for p in rs:
        scratch += [pltpu.VMEM((nz,) + p.shape[1:], bf16)] * 3 + [dma((nz, parts))] * 6
    for t in a2a:
        scratch += [dma((t[4],)), dma((n, t[4])), dma((n, t[4]))]
    for _ in spread:
        scratch += [dma, dma((2,)), dma((2,)), dma((2,)), dma((2,))]
    for p in sums:
        half = (p.shape[1] // 2, p.shape[2])
        scratch += [pltpu.VMEM((2, 2) + half, bf16), pltpu.VMEM((2,) + half, bf16)]
        scratch += [dma((2, 2)), dma((2, 2)), dma((2,)), dma((2,))]
    outs = pl.pallas_call(
        functools.partial(line_body, n, len(ag), len(rs), [(len(t[0]),) + t[2:5] for t in a2a], [ph for _, ph in spread], len(sums), parts),
        out_shape=out_shape,
        in_specs=[hbm] * len(ag) + [vmem] * len(rs) + [hbm] * (sum(len(t[0]) for t in a2a) + len(spread)) + [vmem] * len(sums),
        out_specs=[hbm] * len(ag) + [vmem] * len(rs) + [hbm] * (len(a2a) + len(spread)) + [vmem] * len(sums),
        input_output_aliases=aliases,
        scratch_shapes=scratch,
        compiler_params=pltpu.CompilerParams(
            collective_id=cid, has_side_effects=True, vmem_limit_bytes=48 * 2**20
        ),
        cost_estimate=pl.CostEstimate(flops=us * 1150000000, bytes_accessed=us * 3600000, transcendentals=0),
        name=name,
    )(*ag, *rs, *[w for t in a2a for w in t[0]], *[b for b, _ in spread], *sums)
    outs = [o.reshape((-1,) + o.shape[2:]) if i < len(ag) else o for i, o in enumerate(outs)]
    return outs


def rotate(flat, cosine, sine):
    return flat * cosine + pltpu.roll(flat, HEAD_DIM // 2, 1) * sine


def squash(q, k, piece, keys, length):
    scale = -math.log2(math.e) / math.sqrt(HEAD_DIM)
    sg = 1.0 / (1.0 + jnp.exp2(dot_t(q, k) * scale + math.log2(length)))
    row = lax.broadcasted_iota(jnp.int32, (PIECE, PIECE), 0)
    col = lax.broadcasted_iota(jnp.int32, (PIECE, PIECE), 1)
    return sg, (col <= row) | (piece >= 0)


def masked(value, visible, keys):
    last = jnp.where(visible, value[:, keys - PIECE :], 0.0)
    return last if keys == PIECE else jnp.concatenate([value[:, : keys - PIECE], last], axis=1)


def attn_body(heads, length, lin, cosine, sine, piece, out, rot):
    h, b = pl.program_id(0), pl.program_id(1)
    at = lambda part: pl.ds(pl.multiple_of((part * heads + h) * HEAD_DIM, HEAD_DIM), HEAD_DIM)
    blocks = length // PIECE

    @pl.when(b == 0)
    def _():
        @pl.loop(0, blocks)
        def _(i):
            rows = pl.ds(pl.multiple_of(i * PIECE, PIECE), PIECE)
            for part in (0, 1):
                rot[rows, at(part)] = rotate(lin[rows, at(part)], cosine[rows, :], sine[rows, :]).astype(bf16)
            rot[rows, at(2)] = lin[rows, at(2)].astype(bf16)

    for i in range(blocks):
        @pl.when(b == i)
        def _():
            keys = (i + 1) * PIECE
            own = pl.ds(i * PIECE, PIECE)
            sg, visible = squash(rot[own, at(0)], rot[0:keys, at(1)], piece[...], keys, length)
            out[...] = dot(masked(sg, visible, keys).astype(bf16), rot[0:keys, at(2)]).astype(bf16)


def attention(lin, cosine, sine, piece):
    length, width = lin.shape
    heads = width // 3 // HEAD_DIM
    whole = lambda x: pl.BlockSpec(x.shape, lambda h, b: (0, 0))
    return pl.pallas_call(
        functools.partial(attn_body, heads, length),
        grid=(heads, length // PIECE),
        out_shape=[
            jax.ShapeDtypeStruct((length, width // 3), bf16),
            jax.ShapeDtypeStruct((length, width), bf16),
        ],
        in_specs=[whole(lin), whole(cosine), whole(sine), pl.BlockSpec((PIECE, 1), lambda h, b: (b, 0))],
        out_specs=[
            pl.BlockSpec((PIECE, HEAD_DIM), lambda h, b: (b, h)),
            pl.BlockSpec((length, width), lambda h, b: (0, 0)),
        ],
        compiler_params=pltpu.CompilerParams(vmem_limit_bytes=48 * 2**20),
        cost_estimate=pl.CostEstimate(
            flops=4 * heads * length * length * HEAD_DIM // 2, bytes_accessed=8 * length * width, transcendentals=heads * length * length
        ),
        name="attention",
    )(lin, cosine, sine, piece)


def attn_back_body(heads, length, rot, go, cosine, sine, piece, out, gk, gv):
    h, b = pl.program_id(0), pl.program_id(1)
    at = lambda part: pl.ds(pl.multiple_of((part * heads + h) * HEAD_DIM, HEAD_DIM), HEAD_DIM)
    blocks = length // PIECE
    inv_root = 1.0 / math.sqrt(HEAD_DIM)

    @pl.when(b == 0)
    def _():
        gk[...] = jnp.zeros_like(gk)
        gv[...] = jnp.zeros_like(gv)

    for i in range(blocks):
        @pl.when(b == i)
        def _():
            keys = (i + 1) * PIECE
            own = pl.ds(i * PIECE, PIECE)
            q, g = rot[own, at(0)], go[...]
            sg, visible = squash(q, rot[0:keys, at(1)], piece[...], keys, length)
            p = masked(sg, visible, keys).astype(bf16)
            gs = masked(dot_t(g, rot[0:keys, at(2)]) * sg * (1.0 - sg), visible, keys).astype(bf16)
            gq = dot(gs, rot[0:keys, at(1)]) * inv_root
            out[own, at(0)] = rotate(gq, cosine[own, :], -sine[own, :]).astype(bf16)
            gk[0:keys, :] += t_dot(gs, q)
            gv[0:keys, :] += t_dot(p, g)

    @pl.when(b == blocks - 1)
    def _():
        @pl.loop(0, blocks)
        def _(i):
            rows = pl.ds(pl.multiple_of(i * PIECE, PIECE), PIECE)
            out[rows, at(1)] = rotate(gk[rows, :] * inv_root, cosine[rows, :], -sine[rows, :]).astype(bf16)
            out[rows, at(2)] = gv[rows, :].astype(bf16)


def attention_back(rot, go, cosine, sine, piece):
    length, width = rot.shape
    heads = width // 3 // HEAD_DIM
    whole = lambda x: pl.BlockSpec(x.shape, lambda h, b: (0, 0))
    return pl.pallas_call(
        functools.partial(attn_back_body, heads, length),
        grid=(heads, length // PIECE),
        out_shape=jax.ShapeDtypeStruct((length, width), bf16),
        in_specs=[
            whole(rot),
            pl.BlockSpec((PIECE, HEAD_DIM), lambda h, b: (b, h)),
            whole(cosine),
            whole(sine),
            pl.BlockSpec((PIECE, 1), lambda h, b: (b, 0)),
        ],
        out_specs=pl.BlockSpec((length, width), lambda h, b: (0, 0)),
        scratch_shapes=[pltpu.VMEM((length, HEAD_DIM), f32)] * 2,
        compiler_params=pltpu.CompilerParams(vmem_limit_bytes=48 * 2**20),
        cost_estimate=pl.CostEstimate(
            flops=10 * heads * length * length * HEAD_DIM // 2, bytes_accessed=8 * length * width, transcendentals=heads * length * length
        ),
        name="attention_back",
    )(rot, go, cosine, sine, piece)


def gain_body(n, nr, g, out, group, copies, ss, sr, cs, cr):
    me, r = lax.axis_index("inner"), lax.axis_index("replica")
    mesh_id = pl.DeviceIdType.MESH
    barrier = pltpu.get_barrier_semaphore()
    for k in range(1, n):
        signal(barrier, lax.rem(me + k, n))
    for k in range(1, nr):
        pl.semaphore_signal(barrier, inc=1, device_id={"replica": lax.rem(r + k, nr)}, device_id_type=mesh_id)
    pl.semaphore_wait(barrier, n + nr - 2)

    def inside(k):
        to = lax.rem(me + k, n)
        return rcopy(g.at[to], group.at[k], ss.at[k], sr.at[k], to)

    def across(k):
        return pltpu.make_async_remote_copy(
            src_ref=copies.at[0],
            dst_ref=copies.at[k],
            send_sem=cs.at[k],
            recv_sem=cr.at[k],
            device_id={"replica": lax.rem(r + k, nr)},
            device_id_type=mesh_id,
        )

    for k in range(1, n):
        inside(k).start()
    total = g[me]
    for k in range(1, n):
        inside(k).wait_recv()
        total = total + group[k]
    copies[0] = total
    for k in range(1, nr):
        across(k).start()
    for k in range(1, nr):
        across(k).wait_recv()
        total = total + copies[k]
    out[...] = total
    for k in range(1, n):
        inside(k).wait_send()
    for k in range(1, nr):
        across(k).wait_send()


def gain_sum(cid, parts):
    n, nr = lax.axis_size("inner"), lax.axis_size("replica")
    cols = parts.shape[1] // n
    g = jnp.zeros((n, 8, cols), f32).at[:, :2].set(parts.reshape(2, n, cols).transpose(1, 0, 2))
    dma = pltpu.SemaphoreType.DMA
    vmem = pl.BlockSpec(memory_space=pltpu.VMEM)
    return pl.pallas_call(
        functools.partial(gain_body, n, nr),
        out_shape=jax.ShapeDtypeStruct((8, cols), f32),
        in_specs=[vmem],
        out_specs=vmem,
        scratch_shapes=[
            pltpu.VMEM((n, 8, cols), f32),
            pltpu.VMEM((nr, 8, cols), f32),
            dma((n,)),
            dma((n,)),
            dma((nr,)),
            dma((nr,)),
        ],
        compiler_params=pltpu.CompilerParams(collective_id=cid, has_side_effects=True),
        name="gain_sum",
    )(g)[:2]


def columns_out(w):
    n, nr = lax.axis_size("inner"), lax.axis_size("replica")
    part = w.shape[0] // nr
    cols = w.shape[1] // n

    def source(refs, other, m):
        rows = pl.ds(pl.multiple_of(lax.axis_index("replica") * part, part), part)
        return refs[0].at[rows, pl.ds(pl.multiple_of(other * cols, cols), cols)]

    return ((w,), (n, part, cols), source, lambda ref, other, m: ref.at[other], 1)


def to_all(block):
    n = lax.axis_size("inner")
    return ((block,), (n,) + block.shape, lambda refs, other, m: refs[0], lambda ref, other, m: ref.at[other], 1)


def rows_back(share, count):
    n, part, width = share.shape
    cols = width // count

    def source(refs, other, m):
        return refs[0].at[other, :, pl.ds(m * cols, cols)]

    def target(ref, other, m):
        return ref.at[m, :, pl.ds(pl.multiple_of(other * cols, cols), cols)]

    return ((share,), (count, part, n * cols), source, target, count)


def shares_first(x):
    n, nr = lax.axis_size("inner"), lax.axis_size("replica")
    part = x.shape[1] // n // nr
    return x.reshape(x.shape[0], n, nr, part).transpose(0, 2, 1, 3).reshape(x.shape)


def owners_first(x):
    n, nr = lax.axis_size("inner"), lax.axis_size("replica")
    part = x.shape[1] // n // nr
    return x.reshape(x.shape[0], nr, n, part).transpose(0, 2, 1, 3).reshape(x.shape)


def sum_share(product):
    return lax.psum_scatter(product.astype(bf16), "replica", scatter_dimension=0, tiled=True)


def join(block):
    return lax.all_gather(block, "replica", axis=0, tiled=False)


def flat(w):
    return w.reshape(-1, w.shape[-1])


def local(
    tokens,
    w_query,
    w_key,
    w_value,
    w_out,
    w_gate,
    w_up,
    w_down,
    gain_attn,
    gain_ffn,
    pieces,
    positions,
    cotangent,
):
    n = lax.axis_size("inner")
    nr = lax.axis_size("replica")
    square = nr == 4
    own, width = tokens.shape
    length = own * n
    rows = gain_attn.shape[0]
    after = lax.optimization_barrier

    marks = jnp.zeros((8, own), jnp.int32).at[0].set(pieces).at[1].set(positions)
    gains = jnp.zeros((8, rows), f32).at[0].set(gain_attn.astype(f32)).at[1].set(gain_ffn.astype(f32))
    q_share, k_share, v_share, marks, gains = line_comm(
        0,
        "load_attn", 25,
        a2a=[columns_out(w_query), columns_out(w_key), columns_out(w_value), to_all(marks), to_all(gains)],
    )
    qkv_share = jnp.concatenate([q_share, k_share, v_share], axis=2)
    loads = [columns_out(w_gate), columns_out(w_up)]
    if square:
        x, g_share, u_share, w_qkv = line_comm(
            1, "load_ffn", 80, ag=[shares_first(tokens)], a2a=loads, spread=[(qkv_share, (1, 2))]
        )
    else:
        w_qkv = join(qkv_share)
        x, g_share, u_share = line_comm(1, "load_ffn", 80, ag=[shares_first(tokens)], a2a=loads)
    w_qkv = flat(w_qkv)
    cot, x = after((cotangent, x))
    cot = lax.all_gather(cot, "inner", axis=0, tiled=True)
    pieces, positions = marks[:, 0].reshape(length, 1), marks[:, 1].reshape(length)
    attn_gain, ffn_gain = gains[:, 0].reshape(1, -1), gains[:, 1].reshape(1, -1)

    x = x.astype(f32)
    cosine, sine = rope_tables(positions)
    u1 = x * rms_scale(x)
    n1 = (u1 * shares_first(attn_gain)).astype(bf16)
    o, rot = attention(dot(n1, w_qkv), cosine, sine, pieces)
    a_part = dot(o, w_out).astype(bf16)
    if square:
        a, w_g, w_u = line_comm(2, "attn_out", 50, rs=[a_part], spread=[(g_share, (1,)), (u_share, (1,))])
    else:
        w_g, w_u = join(g_share), join(u_share)
        (a,) = line_comm(2, "attn_out", 50, rs=[a_part])
    mid = tokens.astype(f32) + a
    r2 = rms_scale(mid)
    u2 = mid * r2
    n2 = shares_first((u2 * ffn_gain).astype(bf16))
    if square:
        n2, w_g, w_u = line_comm(3, "gather_n2", 40, ag=[n2], spread=[(w_g, (2,)), (w_u, (2,))])
    else:
        (n2,) = line_comm(3, "gather_n2", 40, ag=[n2])
    w_g, w_u = flat(w_g), flat(w_u)

    gate = dot(n2, w_g)
    up = dot(n2, w_u)
    s = jax.nn.sigmoid(gate)
    silu = gate * s
    hid = (silu * up).astype(bf16)
    g_down = t_dot(hid, cot).astype(bf16)
    ghid = dot_t(cot, w_down)
    ggate = (ghid * up * s * (1.0 + gate * (1.0 - s))).astype(bf16)
    gup = (ghid * silu).astype(bf16)
    gu = t_dot(n2, jnp.concatenate([ggate, gup], axis=1)).astype(bf16)
    gn2_part = (dot_t(ggate, w_g) + dot_t(gup, w_u)).astype(bf16)
    gu, gn2_part = after((gu, gn2_part))
    gu_share = sum_share(gu)
    (gn2,) = line_comm(4, "scatter_gn2", 44, rs=[gn2_part])
    gn2 = owners_first(gn2)
    gu2 = gn2 * ffn_gain
    ffn_gain_part = jnp.sum(gn2 * u2, axis=0)
    gmid = cotangent.astype(f32) + r2 * (gu2 - u2 * jnp.mean(gu2 * u2, axis=1, keepdims=True))
    if square:
        ga, down_share = line_comm(5, "gather_ga", 40, ag=[gmid.astype(bf16)], sums=[g_down])
    else:
        (ga,) = line_comm(5, "gather_ga", 40, ag=[gmid.astype(bf16)])
        down_share = sum_share(g_down)

    go = dot_t(ga, w_out).astype(bf16)
    gqkv = attention_back(rot, go, cosine, sine, pieces)
    g_out = t_dot(o, ga).astype(bf16)
    g_qkv = t_dot(n1, gqkv).astype(bf16)
    gn1_part = dot_t(gqkv, w_qkv)
    attn_gain_part = jnp.sum(gn1_part * u1, axis=0, keepdims=True)
    gn1_part = gn1_part.astype(bf16)
    gu_back = rows_back(gu_share.reshape(n, -1, gu.shape[1]), 2)
    mlp_part = dot(hid, w_down).astype(bf16)
    if square:
        gn1, gu_rows, grad_down, out_share, qkv_share = line_comm(
            6, "scatter_gn1", 80, rs=[gn1_part], a2a=[gu_back], spread=[(down_share, (1, 2))], sums=[g_out, g_qkv]
        )
        qkv_back = rows_back(qkv_share.reshape(n, -1, gqkv.shape[1]), 3)
        mlp, qkv_rows, grad_gu, grad_out = line_comm(
            7, "rows_ffn", 75, rs=[mlp_part], a2a=[qkv_back], spread=[(gu_rows, (1, 2)), (out_share, (1, 2))]
        )
        (grad_qkv,) = line_comm(8, "rows_attn", 28, spread=[(flat(qkv_rows), (1, 2))])
    else:
        gn1, gu_rows = line_comm(6, "scatter_gn1", 80, rs=[gn1_part], a2a=[gu_back])
        qkv_back = rows_back(sum_share(g_qkv).reshape(n, -1, gqkv.shape[1]), 3)
        mlp, qkv_rows = line_comm(7, "rows_ffn", 75, rs=[mlp_part], a2a=[qkv_back])
        grad_gu, grad_out, grad_down, grad_qkv = join(gu_rows), join(sum_share(g_out)), join(down_share), join(qkv_rows)
    output = (mid + mlp).astype(bf16)
    gain_rows = gain_sum(9, jnp.stack([owners_first(attn_gain_part)[0], ffn_gain_part]))
    grad_down = grad_down.reshape(w_down.shape).astype(f32)
    grad_out = grad_out.reshape(w_out.shape).astype(f32)
    grad_gu = grad_gu.astype(f32)
    grad_qkv = grad_qkv.reshape(nr, 3, -1, width).astype(f32)

    gn1 = owners_first(gn1)
    own_x = tokens.astype(f32)
    r1 = rms_scale(own_x)
    u1 = own_x * r1
    gu1 = gn1 * attn_gain
    grad_tokens = gmid + r1 * (gu1 - u1 * jnp.mean(gu1 * u1, axis=1, keepdims=True))
    return (
        output,
        grad_tokens,
        grad_qkv[:, 0].reshape(w_query.shape),
        grad_qkv[:, 1].reshape(w_key.shape),
        grad_qkv[:, 2].reshape(w_value.shape),
        grad_out,
        grad_gu[:, 0].reshape(w_gate.shape),
        grad_gu[:, 1].reshape(w_up.shape),
        grad_down,
        gain_rows[0],
        gain_rows[1],
    )


def solution(mesh):
    tok = P(("replica", "inner"), None)
    row = P("inner", None)
    vec = P("inner")
    mark = P(("replica", "inner"))
    return jax.shard_map(
        local,
        mesh=mesh,
        in_specs=(tok, row, row, row, row, row, row, row, vec, vec, mark, mark, tok),
        out_specs=(tok, tok, row, row, row, row, row, row, row, vec, vec),
        check_vma=False,
    )
```

```python
import functools
import math

import jax
import jax.numpy as jnp
from jax import lax
from jax.experimental import pallas as pl
from jax.experimental.pallas import tpu as pltpu
from jax.sharding import PartitionSpec as P

HEAD_DIM = 128
PIECE = 256
epsilon = 1e-06
rope_base = 10000.0
dims_rows = (((1,), (1,)), ((), ()))
dims_cols = (((0,), (0,)), ((), ()))
f32 = jnp.float32
bf16 = jnp.bfloat16


def dot(a, b):
    return jnp.dot(a, b, preferred_element_type=f32)


def dot_t(a, b):
    return lax.dot_general(a, b, dims_rows, preferred_element_type=f32)


def t_dot(a, b):
    return lax.dot_general(a, b, dims_cols, preferred_element_type=f32)


def rope_tables(positions):
    half_dim = HEAD_DIM // 2
    frequency = rope_base ** (-jnp.arange(half_dim, dtype=f32) * 2.0 / HEAD_DIM)
    angle = positions.astype(f32)[:, None] * frequency[None, :]
    cosine, sine = jnp.cos(angle), jnp.sin(angle)
    return jnp.concatenate([cosine, cosine], axis=1), jnp.concatenate([-sine, sine], axis=1)


def rms_scale(values):
    return lax.rsqrt(jnp.mean(values * values, axis=1, keepdims=True) + epsilon)


def rcopy(src, dst, ssem, rsem, to, axis="inner"):
    return pltpu.make_async_remote_copy(
        src_ref=src,
        dst_ref=dst,
        send_sem=ssem,
        recv_sem=rsem,
        device_id={axis: to},
        device_id_type=pl.DeviceIdType.MESH,
    )


def signal(sem, to, axis="inner"):
    pl.semaphore_signal(sem, inc=1, device_id={axis: to}, device_id_type=pl.DeviceIdType.MESH)


def line_body(n, n_ag, n_rs, a2a_blocks, spreads, n_sum, chain, chain_at, parts, *refs):
    refs = list(refs)
    nz = n // 2
    n_a2a = len(a2a_blocks)
    take = lambda count: [refs.pop(0) for _ in range(count)]
    n_sp = len(spreads)
    ag_in, rs_in, a2a_in = take(n_ag), take(n_rs), [take(t[0]) for t in a2a_blocks]
    sp_in, sum_in = take(n_sp), take(n_sum)
    ag_out, rs_out, a2a_out, sp_out, sum_out = take(n_ag), take(n_rs), take(n_a2a), take(n_sp), take(n_sum)
    chain_out = take(len(chain))
    ag_sem = [take(7) for _ in range(n_ag)]
    rs_scr = [take(9) for _ in range(n_rs)]
    a2a_sem = [take(3) for _ in range(n_a2a)]
    sp_sem = [take(5) for _ in range(n_sp)]
    sum_scr = [take(6) for _ in range(n_sum)]
    chain_sem = [take(5) for _ in chain]
    me = lax.axis_index("inner")
    z, c = me // 2, lax.rem(me, 2)
    sib = me + 1 - 2 * c
    r = lax.axis_index("replica")
    across_x, across_y = r + 1 - 2 * lax.rem(r, 2), r + 2 - 4 * (r // 2)
    barrier = pltpu.get_barrier_semaphore()
    more = 0
    if n_sp + n_sum + len(chain):
        signal(barrier, across_x, "replica")
        signal(barrier, across_y, "replica")
        more = 2
    if n_a2a:
        for k in range(1, n):
            signal(barrier, lax.rem(me + k, n))
        pl.semaphore_wait(barrier, n - 1 + more)
    else:
        signal(barrier, sib)

        @pl.when(z + 1 < nz)
        def _():
            signal(barrier, me + 2)

        @pl.when(z > 0)
        def _():
            signal(barrier, me - 2)

        pl.semaphore_wait(barrier, 1 + more + (z + nz - 1) // nz + (2 * nz - 2 - z) // nz)

    def rows_of(ref, j):
        count = ref.shape[0] // parts
        return pl.ds(pl.multiple_of(j * count, count), count)

    class Gather:
        def __init__(self, x, out, sems):
            self.x, self.out = x, out
            self.own_sem, self.rs, self.rr, self.ls, self.lr, self.ss, self.sr = sems

        def own(self):
            return pltpu.make_async_copy(self.x, self.out.at[me], self.own_sem)

        def piece(self, block, s, j):
            rows = rows_of(self.x, j)
            return self.x.at[rows] if s == 0 else self.out.at[block, rows]

        def right(self, s, j):
            b = me - 2 * s
            dst = self.out.at[b, rows_of(self.x, j)]
            return rcopy(self.piece(b, s, j), dst, self.rs.at[s, j], self.rr.at[s + 1, j], me + 2)

        def left(self, s, j):
            b = me + 2 * s
            dst = self.out.at[b, rows_of(self.x, j)]
            return rcopy(self.piece(b, s, j), dst, self.ls.at[s, j], self.lr.at[s + 1, j], me - 2)

        def side(self, s, k, j):
            b = me - 2 * s if k == 0 else me + 2 * s
            dst = self.out.at[b, rows_of(self.x, j)]
            return rcopy(self.piece(b, s, j), dst, self.ss.at[k, s, j], self.sr.at[k, s, j], sib)

        def from_left(self, s, j):
            dst = self.out.at[me - 2 * s, rows_of(self.x, j)]
            return rcopy(dst, dst, self.rs.at[s, j], self.rr.at[s, j], me - 2)

        def from_right(self, s, j):
            dst = self.out.at[me + 2 * s, rows_of(self.x, j)]
            return rcopy(dst, dst, self.ls.at[s, j], self.lr.at[s, j], me + 2)

        def from_side(self, s, k, j):
            b = sib - 2 * s if k == 0 else sib + 2 * s
            dst = self.out.at[b, rows_of(self.x, j)]
            return rcopy(dst, dst, self.ss.at[k, s, j], self.sr.at[k, s, j], sib)

        def begin(self):
            @pl.loop(0, parts)
            def _(j):
                @pl.when(z + 1 < nz)
                def _():
                    self.right(0, j).start()

                @pl.when(z > 0)
                def _():
                    self.left(0, j).start()

            self.own().start()

            @pl.loop(0, parts)
            def _(j):
                self.side(0, 0, j).start()

        def step(self, s, j):
            @pl.when(z >= s)
            def _():
                self.from_left(s, j).wait_recv()

                @pl.when(z + 1 < nz)
                def _():
                    self.right(s, j).start()

                self.side(s, 0, j).start()

            @pl.when(z + s < nz)
            def _():
                self.from_right(s, j).wait_recv()

                @pl.when(z > 0)
                def _():
                    self.left(s, j).start()

                self.side(s, 1, j).start()

        def end(self):
            self.own().wait()
            for s in range(nz):
                @pl.loop(0, parts)
                def _(j):
                    @pl.when(z >= s)
                    def _():
                        @pl.when(z + 1 < nz)
                        def _():
                            self.right(s, j).wait_send()

                        self.side(s, 0, j).wait_send()
                        self.from_side(s, 0, j).wait_recv()

                    @pl.when(z + s < nz)
                    def _():
                        @pl.when(z > 0)
                        def _():
                            self.left(s, j).wait_send()

                        if s > 0:
                            self.side(s, 1, j).wait_send()
                            self.from_side(s, 1, j).wait_recv()

    class Scatter:
        def __init__(self, p, out, scratch):
            self.p, self.out = p, out
            self.sib_buf, self.l_buf, self.r_buf, self.ss, self.sr, self.rs, self.rr, self.ls, self.lr = scratch
            self.count = out.shape[0] // parts

        def side(self, d, j):
            rows = rows_of(self.out, j)
            return rcopy(self.p.at[2 * d + 1 - c, rows], self.sib_buf.at[d, rows], self.ss.at[d, j], self.sr.at[d, j], sib)

        def right(self, d, j, to=2):
            rows = rows_of(self.out, j)
            return rcopy(self.l_buf.at[d, rows], self.l_buf.at[d, rows], self.rs.at[d, j], self.rr.at[d, j], me + to)

        def left(self, d, j, to=-2):
            rows = rows_of(self.out, j)
            return rcopy(self.r_buf.at[d, rows], self.r_buf.at[d, rows], self.ls.at[d, j], self.lr.at[d, j], me + to)

        def begin(self):
            for s in range(nz // 2):
                for d in (nz - 1 - s, s):
                    @pl.loop(0, parts)
                    def _(j):
                        self.side(d, j).start()

        def pair(self, d, rows):
            return self.p[2 * d + c, rows, :].astype(f32) + self.sib_buf[d, rows, :].astype(f32)

        def step(self, s, j):
            rows = rows_of(self.out, j)
            d = nz - s

            @pl.when(d > z)
            def _():
                self.side(d, j).wait_recv()

                @pl.when(z > 0)
                def _():
                    self.right(d, j, -2).wait_recv()
                    self.l_buf[d, rows, :] = (self.pair(d, rows) + self.l_buf[d, rows, :].astype(f32)).astype(bf16)

                @pl.when(z == 0)
                def _():
                    self.l_buf[d, rows, :] = self.pair(d, rows).astype(bf16)

                self.right(d, j).start()

            e = s - 1

            @pl.when(e < z)
            def _():
                self.side(e, j).wait_recv()

                @pl.when(z + 1 < nz)
                def _():
                    self.left(e, j, 2).wait_recv()
                    self.r_buf[e, rows, :] = (self.pair(e, rows) + self.r_buf[e, rows, :].astype(f32)).astype(bf16)

                @pl.when(z + 1 == nz)
                def _():
                    self.r_buf[e, rows, :] = self.pair(e, rows).astype(bf16)

                self.left(e, j).start()

        def end(self):
            @pl.loop(0, parts)
            def _(j):
                rows = rows_of(self.out, j)
                self.side(z, j).wait_recv()
                self.out[rows, :] = self.pair(z, rows)

                @pl.when(z > 0)
                def _():
                    self.right(z, j, -2).wait_recv()
                    self.out[rows, :] = self.out[rows, :] + self.l_buf[z, rows, :].astype(f32)

                @pl.when(z + 1 < nz)
                def _():
                    self.left(z, j, 2).wait_recv()
                    self.out[rows, :] = self.out[rows, :] + self.r_buf[z, rows, :].astype(f32)

            for d in range(nz):
                @pl.loop(0, parts)
                def _(j):
                    self.side(d, j).wait_send()

                    @pl.when(d > z)
                    def _():
                        self.right(d, j).wait_send()

                    @pl.when(d < z)
                    def _():
                        self.left(d, j).wait_send()

    class Exchange:
        def __init__(self, src, dst, sems, blocks):
            self.src, self.dst = src, dst
            self.own_sem, self.sent, self.recv = sems
            _, self.src_of, self.dst_of, self.count, self.late = blocks
            self.arrived = False

        def to(self, k, m):
            other = lax.rem(me + k, n)
            return rcopy(
                self.src_of(self.src, other, m), self.dst_of(self.dst, me, m), self.sent.at[k, m], self.recv.at[k, m], other
            )

        def came(self, k, m):
            other = lax.rem(me - k + n, n)
            return rcopy(
                self.src_of(self.src, other, m), self.dst_of(self.dst, other, m), self.sent.at[k, m], self.recv.at[k, m], other
            )

        def own(self, m):
            return pltpu.make_async_copy(
                self.src_of(self.src, me, m), self.dst_of(self.dst, me, m), self.own_sem.at[m]
            )

        def send(self, first, last):
            for k in range(first, last):
                for m in range(self.count):
                    self.to(k, m).start()

        def begin(self):
            if not self.late:
                self.send(1, n)
            for m in range(self.count):
                self.own(m).start()

        def step(self, s, j):
            pass

        def after_step(self, s):
            if self.late:
                self.send(1 + (n - 1) * (s - 1) // (nz - 1), 1 + (n - 1) * s // (nz - 1))

        def arrive(self):
            if not self.arrived:
                self.arrived = True
                for m in range(self.count):
                    self.own(m).wait()
                for k in range(1, n):
                    for m in range(self.count):
                        self.came(k, m).wait_recv()

        def end(self):
            self.arrive()
            for k in range(1, n):
                for m in range(self.count):
                    self.to(k, m).wait_send()

    class Spread:
        def __init__(self, src, out, sems, phases):
            self.src, self.out, self.phases = src, out, phases
            self.own_sem, self.send, self.recv, self.send_half, self.recv_half = sems
            self.half = out.shape[1] // 2

        def own(self):
            return pltpu.make_async_copy(self.src, self.out.at[r], self.own_sem)

        def first(self, axis):
            to = across_y if axis else across_x
            return rcopy(self.src, self.out.at[r], self.send.at[axis], self.recv.at[axis], to, "replica")

        def first_came(self, axis):
            who = across_y if axis else across_x
            return rcopy(self.out.at[who], self.out.at[who], self.send.at[axis], self.recv.at[axis], who, "replica")

        def half_of(self, block, axis):
            return self.out.at[block, pl.ds(axis * self.half, self.half)]

        def second(self, axis):
            block, to = (across_x, across_y) if axis else (across_y, across_x)
            piece = self.half_of(block, axis)
            return rcopy(piece, piece, self.send_half.at[axis], self.recv_half.at[axis], to, "replica")

        def second_came(self, axis):
            piece = self.half_of(3 - r, axis)
            who = across_y if axis else across_x
            return rcopy(piece, piece, self.send_half.at[axis], self.recv_half.at[axis], who, "replica")

        def begin(self):
            if 1 in self.phases:
                self.first(0).start()
                self.first(1).start()
                self.own().start()
            else:
                self.second(0).start()
                self.second(1).start()

        def step(self, s, j):
            pass

        def mid(self):
            if self.phases == (1, 2):
                self.first_came(0).wait_recv()
                self.second(1).start()
                self.first_came(1).wait_recv()
                self.second(0).start()

        def end(self):
            if 1 in self.phases:
                self.own().wait()
                for axis in (0, 1):
                    self.first(axis).wait_send()
                    if 2 not in self.phases:
                        self.first_came(axis).wait_recv()
            if 2 in self.phases:
                for axis in (0, 1):
                    self.second(axis).wait_send()
                    self.second_came(axis).wait_recv()

    parts_of = [Gather(*t) for t in zip(ag_in, ag_out, ag_sem)]
    parts_of += [Scatter(*t) for t in zip(rs_in, rs_out, rs_scr)]
    parts_of += [Exchange(*t) for t in zip(a2a_in, a2a_out, a2a_sem, a2a_blocks)]
    class Sum:
        def __init__(self, p, out, scratch):
            self.p, self.out = p, out
            self.a, self.b, self.send_a, self.recv_a, self.send_b, self.recv_b = scratch
            self.half = out.shape[0] // 2
            self.bits = (lax.rem(r, 2), r // 2)

        def rows(self, h):
            return pl.ds(h * self.half, self.half)

        def who(self, h):
            return across_y if h else across_x

        def first(self, h, k):
            other = 1 - self.bits[h]
            q = 2 * other + k if h else other + 2 * k
            return rcopy(
                self.p.at[q, self.rows(h)], self.a.at[h, k], self.send_a.at[h, k], self.recv_a.at[h, k], self.who(h), "replica"
            )

        def second(self, h):
            piece = self.a.at[h, 1 - self.bits[1 - h]]
            return rcopy(piece, self.b.at[h], self.send_b.at[h], self.recv_b.at[h], self.who(1 - h), "replica")

        def each(self, h, put):
            step = 16

            @pl.loop(0, self.half // step)
            def _(i):
                put(pl.multiple_of(i * step, step), step)

        def mine(self, h, k, at, step):
            q = 2 * self.bits[1] + k if h else self.bits[0] + 2 * k
            rows = pl.ds(h * self.half + at, step)
            return self.p[q, rows, :].astype(f32) + self.a[h, k, pl.ds(at, step), :].astype(f32)

        def begin(self):
            for h in (0, 1):
                self.first(h, 1 - self.bits[1 - h]).start()
            for h in (0, 1):
                self.first(h, self.bits[1 - h]).start()

        def step(self, s, j):
            pass

        def mid(self):
            for h in (0, 1):
                k = 1 - self.bits[1 - h]
                self.first(h, k).wait_recv()

                def put(at, step):
                    self.a[h, k, pl.ds(at, step), :] = self.mine(h, k, at, step).astype(bf16)

                self.each(h, put)
                self.second(h).start()

        def end(self):
            for h in (0, 1):
                k = self.bits[1 - h]
                self.first(h, k).wait_recv()
                self.second(h).wait_recv()

                def put(at, step):
                    total = self.mine(h, k, at, step) + self.b[h, pl.ds(at, step), :].astype(f32)
                    self.out[pl.ds(h * self.half + at, step), :] = total.astype(bf16)

                self.each(h, put)
            for h in (0, 1):
                for k in (0, 1):
                    self.first(h, k).wait_send()
                self.second(h).wait_send()

    square_parts = [Spread(*t) for t in zip(sp_in, sp_out, sp_sem, spreads)]
    square_parts += [Sum(*t) for t in zip(sum_in, sum_out, sum_scr)]
    exchanges = parts_of[n_ag + n_rs :]
    chained = [Spread(a2a_out[i], out, sems, (1, 2)) for i, out, sems in zip(chain, chain_out, chain_sem)]

    def begin_chain():
        for i, part in zip(chain, chained):
            exchanges[i].arrive()
            part.begin()

    parts_of += square_parts
    for part in parts_of:
        part.begin()
    if n_ag + n_rs:
        if chain_at == 0:
            begin_chain()
        for s in range(1, nz):
            @pl.loop(0, parts)
            def _(j):
                for part in parts_of:
                    part.step(s, j)

            for part in exchanges:
                part.after_step(s)
            if s == chain_at:
                begin_chain()
            if s == max(1, chain_at):
                for part in square_parts:
                    part.mid()
    else:
        begin_chain()
        for part in square_parts:
            part.mid()
    if chained:
        for part in parts_of[: n_ag + n_rs]:
            part.end()
        for part in chained:
            part.mid()
        parts_of = parts_of[n_ag + n_rs :] + chained
    for part in parts_of:
        part.end()


def line_comm(cid, name, us, ag=(), rs=(), a2a=(), spread=(), sums=(), chain=(), chain_at=None, parts=2):
    n = lax.axis_size("inner")
    nz = n // 2
    chain_at = nz - 2 if chain_at is None else chain_at
    dma = pltpu.SemaphoreType.DMA
    hbm = pl.BlockSpec(memory_space=pl.ANY)
    vmem = pl.BlockSpec(memory_space=pltpu.VMEM)
    rs = [p.reshape((n, p.shape[0] // n) + p.shape[1:]) for p in rs]
    out_shape = [jax.ShapeDtypeStruct((n,) + x.shape, x.dtype) for x in ag]
    out_shape += [jax.ShapeDtypeStruct(p.shape[1:], f32) for p in rs]
    out_shape += [jax.ShapeDtypeStruct(t[1], t[0][0].dtype) for t in a2a]
    out_shape += [jax.ShapeDtypeStruct(b.shape if 1 not in ph else (4,) + b.shape, b.dtype) for b, ph in spread]
    out_shape += [jax.ShapeDtypeStruct((p.shape[0] // 4, p.shape[1]), bf16) for p in sums]
    out_shape += [jax.ShapeDtypeStruct((4,) + a2a[i][1], a2a[i][0][0].dtype) for i in chain]
    sums = [p.reshape((4, p.shape[0] // 4) + p.shape[1:]) for p in sums]
    first_in = len(ag) + len(rs) + sum(len(t[0]) for t in a2a)
    first_out = len(ag) + len(rs) + len(a2a)
    aliases = {first_in + i: first_out + i for i, (b, ph) in enumerate(spread) if 1 not in ph}
    scratch = []
    for _ in ag:
        scratch += [dma, dma((nz, parts)), dma((nz + 1, parts)), dma((nz, parts)), dma((nz + 1, parts))]
        scratch += [dma((2, nz, parts)), dma((2, nz, parts))]
    for p in rs:
        scratch += [pltpu.VMEM((nz,) + p.shape[1:], bf16)] * 3 + [dma((nz, parts))] * 6
    for t in a2a:
        scratch += [dma((t[4],)), dma((n, t[4])), dma((n, t[4]))]
    for _ in spread:
        scratch += [dma, dma((2,)), dma((2,)), dma((2,)), dma((2,))]
    for p in sums:
        half = (p.shape[1] // 2, p.shape[2])
        scratch += [pltpu.VMEM((2, 2) + half, bf16), pltpu.VMEM((2,) + half, bf16)]
        scratch += [dma((2, 2)), dma((2, 2)), dma((2,)), dma((2,))]
    for _ in chain:
        scratch += [dma, dma((2,)), dma((2,)), dma((2,)), dma((2,))]
    outs = pl.pallas_call(
        functools.partial(line_body, n, len(ag), len(rs), [(len(t[0]),) + t[2:6] for t in a2a], [ph for _, ph in spread], len(sums), chain, chain_at, parts),
        out_shape=out_shape,
        in_specs=[hbm] * len(ag) + [vmem] * len(rs) + [hbm] * (sum(len(t[0]) for t in a2a) + len(spread)) + [vmem] * len(sums),
        out_specs=[hbm] * len(ag) + [vmem] * len(rs) + [hbm] * (len(a2a) + len(spread)) + [vmem] * len(sums) + [hbm] * len(chain),
        input_output_aliases=aliases,
        scratch_shapes=scratch,
        compiler_params=pltpu.CompilerParams(
            collective_id=cid, has_side_effects=True, vmem_limit_bytes=48 * 2**20
        ),
        cost_estimate=pl.CostEstimate(flops=us * 1150000000, bytes_accessed=us * 3600000, transcendentals=0),
        name=name,
    )(*ag, *rs, *[w for t in a2a for w in t[0]], *[b for b, _ in spread], *sums)
    outs = [o.reshape((-1,) + o.shape[2:]) if i < len(ag) else o for i, o in enumerate(outs)]
    return outs


def rotate(flat, cosine, sine):
    return flat * cosine + pltpu.roll(flat, HEAD_DIM // 2, 1) * sine


def squash(q, k, piece, keys, length):
    scale = -math.log2(math.e) / math.sqrt(HEAD_DIM)
    sg = 1.0 / (1.0 + jnp.exp2(dot_t(q, k) * scale + math.log2(length)))
    row = lax.broadcasted_iota(jnp.int32, (PIECE, PIECE), 0)
    col = lax.broadcasted_iota(jnp.int32, (PIECE, PIECE), 1)
    return sg, (col <= row) | (piece >= 0)


def masked(value, visible, keys):
    last = jnp.where(visible, value[:, keys - PIECE :], 0.0)
    return last if keys == PIECE else jnp.concatenate([value[:, : keys - PIECE], last], axis=1)


def attn_body(heads, length, lin, cosine, sine, piece, out, rot):
    h, b = pl.program_id(0), pl.program_id(1)
    at = lambda part: pl.ds(pl.multiple_of((part * heads + h) * HEAD_DIM, HEAD_DIM), HEAD_DIM)
    blocks = length // PIECE

    @pl.when(b == 0)
    def _():
        @pl.loop(0, blocks)
        def _(i):
            rows = pl.ds(pl.multiple_of(i * PIECE, PIECE), PIECE)
            for part in (0, 1):
                rot[rows, at(part)] = rotate(lin[rows, at(part)], cosine[rows, :], sine[rows, :]).astype(bf16)
            rot[rows, at(2)] = lin[rows, at(2)].astype(bf16)

    for i in range(blocks):
        @pl.when(b == i)
        def _():
            keys = (i + 1) * PIECE
            own = pl.ds(i * PIECE, PIECE)
            sg, visible = squash(rot[own, at(0)], rot[0:keys, at(1)], piece[...], keys, length)
            out[...] = dot(masked(sg, visible, keys).astype(bf16), rot[0:keys, at(2)]).astype(bf16)


def attention(lin, cosine, sine, piece):
    length, width = lin.shape
    heads = width // 3 // HEAD_DIM
    whole = lambda x: pl.BlockSpec(x.shape, lambda h, b: (0, 0))
    return pl.pallas_call(
        functools.partial(attn_body, heads, length),
        grid=(heads, length // PIECE),
        out_shape=[
            jax.ShapeDtypeStruct((length, width // 3), bf16),
            jax.ShapeDtypeStruct((length, width), bf16),
        ],
        in_specs=[whole(lin), whole(cosine), whole(sine), pl.BlockSpec((PIECE, 1), lambda h, b: (b, 0))],
        out_specs=[
            pl.BlockSpec((PIECE, HEAD_DIM), lambda h, b: (b, h)),
            pl.BlockSpec((length, width), lambda h, b: (0, 0)),
        ],
        compiler_params=pltpu.CompilerParams(vmem_limit_bytes=48 * 2**20),
        cost_estimate=pl.CostEstimate(
            flops=4 * heads * length * length * HEAD_DIM // 2, bytes_accessed=8 * length * width, transcendentals=heads * length * length
        ),
        name="attention",
    )(lin, cosine, sine, piece)


def attn_back_body(heads, length, rot, go, cosine, sine, piece, out, gk, gv):
    h, b = pl.program_id(0), pl.program_id(1)
    at = lambda part: pl.ds(pl.multiple_of((part * heads + h) * HEAD_DIM, HEAD_DIM), HEAD_DIM)
    blocks = length // PIECE
    inv_root = 1.0 / math.sqrt(HEAD_DIM)

    @pl.when(b == 0)
    def _():
        gk[...] = jnp.zeros_like(gk)
        gv[...] = jnp.zeros_like(gv)

    for i in range(blocks):
        @pl.when(b == i)
        def _():
            keys = (i + 1) * PIECE
            own = pl.ds(i * PIECE, PIECE)
            q, g = rot[own, at(0)], go[...]
            sg, visible = squash(q, rot[0:keys, at(1)], piece[...], keys, length)
            p = masked(sg, visible, keys).astype(bf16)
            gs = masked(dot_t(g, rot[0:keys, at(2)]) * sg * (1.0 - sg), visible, keys).astype(bf16)
            gq = dot(gs, rot[0:keys, at(1)]) * inv_root
            out[own, at(0)] = rotate(gq, cosine[own, :], -sine[own, :]).astype(bf16)
            gk[0:keys, :] += t_dot(gs, q)
            gv[0:keys, :] += t_dot(p, g)

    @pl.when(b == blocks - 1)
    def _():
        @pl.loop(0, blocks)
        def _(i):
            rows = pl.ds(pl.multiple_of(i * PIECE, PIECE), PIECE)
            out[rows, at(1)] = rotate(gk[rows, :] * inv_root, cosine[rows, :], -sine[rows, :]).astype(bf16)
            out[rows, at(2)] = gv[rows, :].astype(bf16)


def attention_back(rot, go, cosine, sine, piece):
    length, width = rot.shape
    heads = width // 3 // HEAD_DIM
    whole = lambda x: pl.BlockSpec(x.shape, lambda h, b: (0, 0))
    return pl.pallas_call(
        functools.partial(attn_back_body, heads, length),
        grid=(heads, length // PIECE),
        out_shape=jax.ShapeDtypeStruct((length, width), bf16),
        in_specs=[
            whole(rot),
            pl.BlockSpec((PIECE, HEAD_DIM), lambda h, b: (b, h)),
            whole(cosine),
            whole(sine),
            pl.BlockSpec((PIECE, 1), lambda h, b: (b, 0)),
        ],
        out_specs=pl.BlockSpec((length, width), lambda h, b: (0, 0)),
        scratch_shapes=[pltpu.VMEM((length, HEAD_DIM), f32)] * 2,
        compiler_params=pltpu.CompilerParams(vmem_limit_bytes=48 * 2**20),
        cost_estimate=pl.CostEstimate(
            flops=10 * heads * length * length * HEAD_DIM // 2, bytes_accessed=8 * length * width, transcendentals=heads * length * length
        ),
        name="attention_back",
    )(rot, go, cosine, sine, piece)


def columns_out(w):
    n, nr = lax.axis_size("inner"), lax.axis_size("replica")
    part = w.shape[0] // nr
    cols = w.shape[1] // n

    def source(refs, other, m):
        rows = pl.ds(pl.multiple_of(lax.axis_index("replica") * part, part), part)
        return refs[0].at[rows, pl.ds(pl.multiple_of(other * cols, cols), cols)]

    return ((w,), (n, part, cols), source, lambda ref, other, m: ref.at[other], 1, False)


def to_all(block):
    n = lax.axis_size("inner")
    return ((block,), (n,) + block.shape, lambda refs, other, m: refs[0], lambda ref, other, m: ref.at[other], 1, False)


def rows_back(share, first, count, late=False):
    n, part, _ = share.shape
    cols = first[1]

    def source(refs, other, m):
        return refs[0].at[other, :, pl.ds((first[0] + m) * cols, cols)]

    def target(ref, other, m):
        return ref.at[pl.ds(m * part, part), pl.ds(pl.multiple_of(other * cols, cols), cols)]

    return ((share,), (count * part, n * cols), source, target, count, late)


def sum_blocks(g):
    n = lax.axis_size("inner")
    cols = g.shape[1]
    return ((g,), (n,) + (g.shape[0] // n, cols), lambda refs, other, m: refs[0].at[pl.ds(pl.multiple_of(other * 16, 16), 16)], lambda ref, other, m: ref.at[other], 1, False)


def shares_first(x):
    n, nr = lax.axis_size("inner"), lax.axis_size("replica")
    part = x.shape[1] // n // nr
    return x.reshape(x.shape[0], n, nr, part).transpose(0, 2, 1, 3).reshape(x.shape)


def owners_first(x):
    n, nr = lax.axis_size("inner"), lax.axis_size("replica")
    part = x.shape[1] // n // nr
    return x.reshape(x.shape[0], nr, n, part).transpose(0, 2, 1, 3).reshape(x.shape)


def sum_share(product):
    return lax.psum_scatter(product.astype(bf16), "replica", scatter_dimension=0, tiled=True)


def join(block):
    return lax.all_gather(block, "replica", axis=0, tiled=False)


def flat(w):
    return w.reshape(-1, w.shape[-1])


def local(
    tokens,
    w_query,
    w_key,
    w_value,
    w_out,
    w_gate,
    w_up,
    w_down,
    gain_attn,
    gain_ffn,
    pieces,
    positions,
    cotangent,
):
    n = lax.axis_size("inner")
    nr = lax.axis_size("replica")
    square = nr == 4
    own, width = tokens.shape
    length = own * n
    rows = gain_attn.shape[0]
    after = lax.optimization_barrier

    marks = jnp.zeros((8, own), jnp.int32).at[0].set(pieces).at[1].set(positions)
    gains = jnp.zeros((8, rows), f32).at[0].set(gain_attn.astype(f32)).at[1].set(gain_ffn.astype(f32))
    q_share, k_share, v_share, marks, gains = line_comm(
        0,
        "load_attn", 25,
        a2a=[columns_out(w_query), columns_out(w_key), columns_out(w_value), to_all(marks), to_all(gains)],
    )
    qkv_share = jnp.concatenate([q_share, k_share, v_share], axis=2)
    loads = [columns_out(w_gate), columns_out(w_up)]
    if square:
        x, g_share, u_share, w_qkv = line_comm(
            1, "load_ffn", 80, ag=[shares_first(tokens)], a2a=loads, spread=[(qkv_share, (1, 2))]
        )
    else:
        w_qkv = join(qkv_share)
        x, g_share, u_share = line_comm(1, "load_ffn", 80, ag=[shares_first(tokens)], a2a=loads)
    w_qkv = flat(w_qkv)
    cot, x = after((cotangent, x))
    cot = lax.all_gather(cot, "inner", axis=0, tiled=True)
    pieces, positions = marks[:, 0].reshape(length, 1), marks[:, 1].reshape(length)
    attn_gain, ffn_gain = gains[:, 0].reshape(1, -1), gains[:, 1].reshape(1, -1)

    x = x.astype(f32)
    cosine, sine = rope_tables(positions)
    u1 = x * rms_scale(x)
    n1 = (u1 * shares_first(attn_gain)).astype(bf16)
    o, rot = attention(dot(n1, w_qkv), cosine, sine, pieces)
    a_part = dot(o, w_out).astype(bf16)
    if square:
        a, w_g, w_u = line_comm(2, "attn_out", 50, rs=[a_part], spread=[(g_share, (1,)), (u_share, (1,))])
    else:
        w_g, w_u = join(g_share), join(u_share)
        (a,) = line_comm(2, "attn_out", 50, rs=[a_part])
    mid = tokens.astype(f32) + a
    r2 = rms_scale(mid)
    u2 = mid * r2
    n2 = shares_first((u2 * ffn_gain).astype(bf16))
    if square:
        n2, w_g, w_u = line_comm(3, "gather_n2", 40, ag=[n2], spread=[(w_g, (2,)), (w_u, (2,))])
    else:
        (n2,) = line_comm(3, "gather_n2", 40, ag=[n2])
    w_g, w_u = flat(w_g), flat(w_u)

    gate = dot(n2, w_g)
    up = dot(n2, w_u)
    s = jax.nn.sigmoid(gate)
    silu = gate * s
    hid = (silu * up).astype(bf16)
    g_down = t_dot(hid, cot).astype(bf16)
    ghid = dot_t(cot, w_down)
    ggate = (ghid * up * s * (1.0 + gate * (1.0 - s))).astype(bf16)
    gup = (ghid * silu).astype(bf16)
    gu = t_dot(n2, jnp.concatenate([ggate, gup], axis=1)).astype(bf16)
    gn2_part = (dot_t(ggate, w_g) + dot_t(gup, w_u)).astype(bf16)
    gu, gn2_part = after((gu, gn2_part))
    gu_share = sum_share(gu)
    (gn2,) = line_comm(4, "scatter_gn2", 44, rs=[gn2_part])
    gn2 = owners_first(gn2)
    gu2 = gn2 * ffn_gain
    ffn_gain_part = jnp.sum(gn2 * u2, axis=0)
    gmid = cotangent.astype(f32) + r2 * (gu2 - u2 * jnp.mean(gu2 * u2, axis=1, keepdims=True))
    if square:
        ga, down_share = line_comm(5, "gather_ga", 50, ag=[gmid.astype(bf16)], sums=[g_down])
    else:
        (ga,) = line_comm(5, "gather_ga", 40, ag=[gmid.astype(bf16)])
        down_share = sum_share(g_down)
    ga, down_share, gu_share = after((ga, down_share, gu_share))
    grad_down = join(down_share)

    go = dot_t(ga, w_out).astype(bf16)
    gqkv = attention_back(rot, go, cosine, sine, pieces)
    g_out = t_dot(o, ga).astype(bf16)
    g_qkv = t_dot(n1, gqkv).astype(bf16)
    gn1_part = dot_t(gqkv, w_qkv)
    attn_gain_part = jnp.sum(gn1_part * u1, axis=0, keepdims=True)
    gn1_part = gn1_part.astype(bf16)
    gains = jnp.stack([owners_first(attn_gain_part)[0].reshape(n, rows), ffn_gain_part.reshape(n, rows)], axis=1)
    gains = jnp.pad(gains, ((0, 0), (0, 14), (0, 0))).reshape(n * 16, rows)
    cols = w_gate.shape[1] // n
    head_cols = gqkv.shape[1] // 3
    gu_share = gu_share.reshape(n, -1, 2 * cols)
    if square:
        gn1, gate_rows, up_rows, gains, out_share, qkv_share, grad_gate = line_comm(
            6,
            "scatter_gn1",
            1,
            rs=[gn1_part],
            a2a=[rows_back(gu_share, (0, cols), 1), rows_back(gu_share, (1, cols), 1, True), sum_blocks(gains)],
            sums=[g_out, g_qkv],
            chain=(0,),
            chain_at=0,
        )
        mlp_part, gains = dot(hid, w_down).astype(bf16), jnp.sum(gains, axis=0)
        qkv_back = rows_back(qkv_share.reshape(n, -1, 3 * head_cols), (0, head_cols), 3)
        mlp_part, grad_down = after((mlp_part, grad_down))
        mlp, qkv_rows, grad_up, grad_out, gains, grad_qkv = line_comm(
            7,
            "rows_attn",
            70,
            rs=[mlp_part],
            a2a=[qkv_back],
            spread=[(up_rows, (1, 2)), (out_share, (1, 2)), (gains, (1, 2))],
            chain=(0,),
            chain_at=0,
        )
        gains = jnp.sum(gains, axis=0)
    else:
        gu_back = rows_back(gu_share, (0, cols), 2)
        gn1, gu_rows, gains = line_comm(6, "scatter_gn1", 80, rs=[gn1_part], a2a=[gu_back, sum_blocks(gains)])
        gains = lax.psum(jnp.sum(gains, axis=0), "replica")
        qkv_back = rows_back(sum_share(g_qkv).reshape(n, -1, 3 * head_cols), (0, head_cols), 3)
        mlp_part = dot(hid, w_down).astype(bf16)
        mlp, qkv_rows = line_comm(7, "rows_attn", 75, rs=[mlp_part], a2a=[qkv_back])
        grad_gu = join(gu_rows).reshape(nr, 2, -1, n * cols)
        grad_gate, grad_up, grad_out, grad_qkv = grad_gu[:, 0], grad_gu[:, 1], join(sum_share(g_out)), join(qkv_rows)
    output = (mid + mlp).astype(bf16)
    grad_qkv = grad_qkv.reshape(nr, 3, -1, width).astype(f32)

    gn1 = owners_first(gn1)
    own_x = tokens.astype(f32)
    r1 = rms_scale(own_x)
    u1 = own_x * r1
    gu1 = gn1 * attn_gain
    grad_tokens = gmid + r1 * (gu1 - u1 * jnp.mean(gu1 * u1, axis=1, keepdims=True))
    return (
        output,
        grad_tokens,
        grad_qkv[:, 0].reshape(w_query.shape),
        grad_qkv[:, 1].reshape(w_key.shape),
        grad_qkv[:, 2].reshape(w_value.shape),
        grad_out.reshape(w_out.shape).astype(f32),
        grad_gate.reshape(w_gate.shape).astype(f32),
        grad_up.reshape(w_up.shape).astype(f32),
        grad_down.reshape(w_down.shape).astype(f32),
        gains[0],
        gains[1],
    )


def solution(mesh):
    tok = P(("replica", "inner"), None)
    row = P("inner", None)
    vec = P("inner")
    mark = P(("replica", "inner"))
    return jax.shard_map(
        local,
        mesh=mesh,
        in_specs=(tok, row, row, row, row, row, row, row, vec, vec, mark, mark, tok),
        out_specs=(tok, tok, row, row, row, row, row, row, row, vec, vec),
        check_vma=False,
    )
```

```python
import functools
import math

import jax
import jax.numpy as jnp
from jax import lax
from jax.experimental import pallas as pl
from jax.experimental.pallas import tpu as pltpu
from jax.sharding import PartitionSpec as P

HEAD_DIM = 128
PIECE = 256
epsilon = 1e-06
rope_base = 10000.0
dims_rows = (((1,), (1,)), ((), ()))
dims_cols = (((0,), (0,)), ((), ()))
f32 = jnp.float32
bf16 = jnp.bfloat16


def dot(a, b):
    return jnp.dot(a, b, preferred_element_type=f32)


def dot_t(a, b):
    return lax.dot_general(a, b, dims_rows, preferred_element_type=f32)


def t_dot(a, b):
    return lax.dot_general(a, b, dims_cols, preferred_element_type=f32)


def rope_tables(positions):
    half_dim = HEAD_DIM // 2
    frequency = rope_base ** (-jnp.arange(half_dim, dtype=f32) * 2.0 / HEAD_DIM)
    angle = positions.astype(f32)[:, None] * frequency[None, :]
    cosine, sine = jnp.cos(angle), jnp.sin(angle)
    return jnp.concatenate([cosine, cosine], axis=1), jnp.concatenate([-sine, sine], axis=1)


def rms_scale(values):
    return lax.rsqrt(jnp.mean(values * values, axis=1, keepdims=True) + epsilon)


def rcopy(src, dst, ssem, rsem, to, axis="inner"):
    return pltpu.make_async_remote_copy(
        src_ref=src,
        dst_ref=dst,
        send_sem=ssem,
        recv_sem=rsem,
        device_id={axis: to},
        device_id_type=pl.DeviceIdType.MESH,
    )


def signal(sem, to, axis="inner"):
    pl.semaphore_signal(sem, inc=1, device_id={axis: to}, device_id_type=pl.DeviceIdType.MESH)


def line_body(n, n_ag, products, a2a_blocks, spreads, n_sum, chain, chain_at, work, parts, *refs):
    refs = list(refs)
    nz = n // 2
    n_a2a = len(a2a_blocks)
    take = lambda count: [refs.pop(0) for _ in range(count)]
    n_sp, n_rs = len(spreads), len(products)
    ag_in, rs_in, a2a_in = take(n_ag), [take(2 * len(t) or 1) for t in products], [take(t[0]) for t in a2a_blocks]
    sp_in, sum_in = take(n_sp), take(n_sum)
    work_in = take(work[1]) if work else []
    ag_out, rs_out, a2a_out, sp_out, sum_out = take(n_ag), take(n_rs), take(n_a2a), take(n_sp), take(n_sum)
    chain_out = take(len(chain))
    work_out = take(work[2]) if work else []
    ag_sem = [take(7) for _ in range(n_ag)]
    rs_scr = [take(10 if t else 9) for t in products]
    a2a_sem = [take(3) for _ in range(n_a2a)]
    sp_sem = [take(5) for _ in range(n_sp)]
    sum_scr = [take(6) for _ in range(n_sum)]
    chain_sem = [take(5) for _ in chain]
    work_scr = take(work[3]) if work else []
    me = lax.axis_index("inner")
    z, c = me // 2, lax.rem(me, 2)
    sib = me + 1 - 2 * c
    r = lax.axis_index("replica")
    across_x, across_y = r + 1 - 2 * lax.rem(r, 2), r + 2 - 4 * (r // 2)
    barrier = pltpu.get_barrier_semaphore()
    more = 0
    if n_sp + n_sum + len(chain):
        signal(barrier, across_x, "replica")
        signal(barrier, across_y, "replica")
        more = 2
    if n_a2a:
        for k in range(1, n):
            signal(barrier, lax.rem(me + k, n))
        pl.semaphore_wait(barrier, n - 1 + more)
    else:
        signal(barrier, sib)

        @pl.when(z + 1 < nz)
        def _():
            signal(barrier, me + 2)

        @pl.when(z > 0)
        def _():
            signal(barrier, me - 2)

        pl.semaphore_wait(barrier, 1 + more + (z + nz - 1) // nz + (2 * nz - 2 - z) // nz)

    def rows_of(ref, j):
        count = ref.shape[0] // parts
        return pl.ds(pl.multiple_of(j * count, count), count)

    class Gather:
        def __init__(self, x, out, sems):
            self.x, self.out, self.here = x, out, set()
            self.own_sem, self.rs, self.rr, self.ls, self.lr, self.ss, self.sr = sems

        def own(self):
            return pltpu.make_async_copy(self.x, self.out.at[me], self.own_sem)

        def piece(self, block, s, j):
            rows = rows_of(self.x, j)
            return self.x.at[rows] if s == 0 else self.out.at[block, rows]

        def right(self, s, j):
            b = me - 2 * s
            dst = self.out.at[b, rows_of(self.x, j)]
            return rcopy(self.piece(b, s, j), dst, self.rs.at[s, j], self.rr.at[s + 1, j], me + 2)

        def left(self, s, j):
            b = me + 2 * s
            dst = self.out.at[b, rows_of(self.x, j)]
            return rcopy(self.piece(b, s, j), dst, self.ls.at[s, j], self.lr.at[s + 1, j], me - 2)

        def side(self, s, k, j):
            b = me - 2 * s if k == 0 else me + 2 * s
            dst = self.out.at[b, rows_of(self.x, j)]
            return rcopy(self.piece(b, s, j), dst, self.ss.at[k, s, j], self.sr.at[k, s, j], sib)

        def from_left(self, s, j):
            dst = self.out.at[me - 2 * s, rows_of(self.x, j)]
            return rcopy(dst, dst, self.rs.at[s, j], self.rr.at[s, j], me - 2)

        def from_right(self, s, j):
            dst = self.out.at[me + 2 * s, rows_of(self.x, j)]
            return rcopy(dst, dst, self.ls.at[s, j], self.lr.at[s, j], me + 2)

        def from_side(self, s, k, j):
            b = sib - 2 * s if k == 0 else sib + 2 * s
            dst = self.out.at[b, rows_of(self.x, j)]
            return rcopy(dst, dst, self.ss.at[k, s, j], self.sr.at[k, s, j], sib)

        def begin(self):
            @pl.loop(0, parts)
            def _(j):
                @pl.when(z + 1 < nz)
                def _():
                    self.right(0, j).start()

                @pl.when(z > 0)
                def _():
                    self.left(0, j).start()

            self.own().start()

            @pl.loop(0, parts)
            def _(j):
                self.side(0, 0, j).start()

        def step(self, s, j):
            @pl.when(z >= s)
            def _():
                self.from_left(s, j).wait_recv()

                @pl.when(z + 1 < nz)
                def _():
                    self.right(s, j).start()

                self.side(s, 0, j).start()

            @pl.when(z + s < nz)
            def _():
                self.from_right(s, j).wait_recv()

                @pl.when(z > 0)
                def _():
                    self.left(s, j).start()

                self.side(s, 1, j).start()

        def arrive(self, s):
            self.here.add(s)
            if s == 0:
                self.own().wait()

            @pl.loop(0, parts)
            def _(j):
                @pl.when(z >= s)
                def _():
                    self.from_side(s, 0, j).wait_recv()

                if s > 0:
                    @pl.when(z + s < nz)
                    def _():
                        self.from_side(s, 1, j).wait_recv()

        def end(self):
            for s in range(nz):
                if s not in self.here:
                    self.arrive(s)

                @pl.loop(0, parts)
                def _(j):
                    @pl.when(z >= s)
                    def _():
                        @pl.when(z + 1 < nz)
                        def _():
                            self.right(s, j).wait_send()

                        self.side(s, 0, j).wait_send()

                    @pl.when(z + s < nz)
                    def _():
                        @pl.when(z > 0)
                        def _():
                            self.left(s, j).wait_send()

                        if s > 0:
                            self.side(s, 1, j).wait_send()

    class Scatter:
        def __init__(self, operands, flips, out, scratch):
            self.pairs, self.out = [(x, w) + t for x, w, t in zip(operands[::2], operands[1::2], flips)], out
            self.p, *scratch = scratch if flips else operands + scratch
            self.sib_buf, self.l_buf, self.r_buf, self.ss, self.sr, self.rs, self.rr, self.ls, self.lr = scratch
            self.count = out.shape[0] // parts

        def side(self, d, j):
            rows = rows_of(self.out, j)
            return rcopy(self.p.at[2 * d + 1 - c, rows], self.sib_buf.at[d, rows], self.ss.at[d, j], self.sr.at[d, j], sib)

        def right(self, d, j, to=2):
            rows = rows_of(self.out, j)
            return rcopy(self.l_buf.at[d, rows], self.l_buf.at[d, rows], self.rs.at[d, j], self.rr.at[d, j], me + to)

        def left(self, d, j, to=-2):
            rows = rows_of(self.out, j)
            return rcopy(self.r_buf.at[d, rows], self.r_buf.at[d, rows], self.ls.at[d, j], self.lr.at[d, j], me + to)

        def product(self, d):
            own, width = self.out.shape
            rows = pl.ds(d * 2 * own, 2 * own)
            tile = min(512, width)

            @pl.loop(0, width // tile)
            def _(t):
                cols = pl.ds(pl.multiple_of(t * tile, tile), tile)
                total = 0.0
                for x, w, flip, first in self.pairs:
                    x = x[rows, first : first + w.shape[1 if flip else 0]]
                    total += dot_t(x, w[cols, :]) if flip else dot(x, w[:, cols])
                total = total.astype(bf16)
                self.p[2 * d, :, cols] = total[:own]
                self.p[2 * d + 1, :, cols] = total[own:]

        def begin(self):
            for s in range(1 if self.pairs else nz // 2):
                self.offer(s)

        def offer(self, s):
            for d in (nz - 1 - s, s):
                if self.pairs:
                    self.product(d)

                @pl.loop(0, parts)
                def _(j):
                    self.side(d, j).start()

        def after_step(self, s):
            if self.pairs and s < nz // 2:
                self.offer(s)

        def pair(self, d, rows):
            return self.p[2 * d + c, rows, :].astype(f32) + self.sib_buf[d, rows, :].astype(f32)

        def step(self, s, j):
            tick = (s - 1) * parts + j
            k = tick - z

            @pl.when((k >= 0) & (k < (nz - 1 - z) * parts))
            def _():
                d, i = nz - 1 - k // parts, lax.rem(k, parts)
                rows = rows_of(self.out, i)
                self.side(d, i).wait_recv()

                @pl.when(z > 0)
                def _():
                    self.right(d, i, -2).wait_recv()
                    self.l_buf[d, rows, :] = (self.pair(d, rows) + self.l_buf[d, rows, :].astype(f32)).astype(bf16)

                @pl.when(z == 0)
                def _():
                    self.l_buf[d, rows, :] = self.pair(d, rows).astype(bf16)

                self.right(d, i).start()

            m = tick - (nz - 1 - z)

            @pl.when((m >= 0) & (m < z * parts))
            def _():
                d, i = m // parts, lax.rem(m, parts)
                rows = rows_of(self.out, i)
                self.side(d, i).wait_recv()

                @pl.when(z + 1 < nz)
                def _():
                    self.left(d, i, 2).wait_recv()
                    self.r_buf[d, rows, :] = (self.pair(d, rows) + self.r_buf[d, rows, :].astype(f32)).astype(bf16)

                @pl.when(z + 1 == nz)
                def _():
                    self.r_buf[d, rows, :] = self.pair(d, rows).astype(bf16)

                self.left(d, i).start()

        def end(self):
            @pl.loop(0, parts)
            def _(j):
                rows = rows_of(self.out, j)
                self.side(z, j).wait_recv()
                self.out[rows, :] = self.pair(z, rows)

                @pl.when(z > 0)
                def _():
                    self.right(z, j, -2).wait_recv()
                    self.out[rows, :] = self.out[rows, :] + self.l_buf[z, rows, :].astype(f32)

                @pl.when(z + 1 < nz)
                def _():
                    self.left(z, j, 2).wait_recv()
                    self.out[rows, :] = self.out[rows, :] + self.r_buf[z, rows, :].astype(f32)

            for d in range(nz):
                @pl.loop(0, parts)
                def _(j):
                    self.side(d, j).wait_send()

                    @pl.when(d > z)
                    def _():
                        self.right(d, j).wait_send()

                    @pl.when(d < z)
                    def _():
                        self.left(d, j).wait_send()

    class Exchange:
        def __init__(self, src, dst, sems, blocks):
            self.src, self.dst = src, dst
            self.own_sem, self.sent, self.recv = sems
            _, self.src_of, self.dst_of, self.count, self.late = blocks
            self.arrived = False

        def to(self, k, m):
            other = lax.rem(me + k, n)
            return rcopy(
                self.src_of(self.src, other, m), self.dst_of(self.dst, me, m), self.sent.at[k, m], self.recv.at[k, m], other
            )

        def came(self, k, m):
            other = lax.rem(me - k + n, n)
            return rcopy(
                self.src_of(self.src, other, m), self.dst_of(self.dst, other, m), self.sent.at[k, m], self.recv.at[k, m], other
            )

        def own(self, m):
            return pltpu.make_async_copy(
                self.src_of(self.src, me, m), self.dst_of(self.dst, me, m), self.own_sem.at[m]
            )

        def send(self, first, last):
            for k in range(first, last):
                for m in range(self.count):
                    self.to(k, m).start()

        def begin(self):
            if not self.late:
                self.send(1, n)
            for m in range(self.count):
                self.own(m).start()

        def step(self, s, j):
            pass

        def after_step(self, s):
            if self.late:
                self.send(1 + (n - 1) * (s - 1) // (nz - 1), 1 + (n - 1) * s // (nz - 1))

        def arrive(self):
            if not self.arrived:
                self.arrived = True
                for m in range(self.count):
                    self.own(m).wait()
                for k in range(1, n):
                    for m in range(self.count):
                        self.came(k, m).wait_recv()

        def end(self):
            self.arrive()
            for k in range(1, n):
                for m in range(self.count):
                    self.to(k, m).wait_send()

    class Spread:
        def __init__(self, src, out, sems, phases):
            self.src, self.out, self.phases = src, out, phases
            self.own_sem, self.send, self.recv, self.send_half, self.recv_half = sems
            self.half, self.here = out.shape[1] // 2, False

        def own(self):
            return pltpu.make_async_copy(self.src, self.out.at[r], self.own_sem)

        def first(self, axis):
            to = across_y if axis else across_x
            return rcopy(self.src, self.out.at[r], self.send.at[axis], self.recv.at[axis], to, "replica")

        def first_came(self, axis):
            who = across_y if axis else across_x
            return rcopy(self.out.at[who], self.out.at[who], self.send.at[axis], self.recv.at[axis], who, "replica")

        def half_of(self, block, axis):
            return self.out.at[block, pl.ds(axis * self.half, self.half)]

        def second(self, axis):
            block, to = (across_x, across_y) if axis else (across_y, across_x)
            piece = self.half_of(block, axis)
            return rcopy(piece, piece, self.send_half.at[axis], self.recv_half.at[axis], to, "replica")

        def second_came(self, axis):
            piece = self.half_of(3 - r, axis)
            who = across_y if axis else across_x
            return rcopy(piece, piece, self.send_half.at[axis], self.recv_half.at[axis], who, "replica")

        def begin(self):
            if 1 in self.phases:
                self.first(0).start()
                self.first(1).start()
                self.own().start()
            else:
                self.second(0).start()
                self.second(1).start()

        def step(self, s, j):
            pass

        def mid(self):
            if self.phases == (1, 2):
                self.first_came(0).wait_recv()
                self.second(1).start()
                self.first_came(1).wait_recv()
                self.second(0).start()

        def end(self):
            if 1 in self.phases:
                self.own().wait()
                for axis in (0, 1):
                    self.first(axis).wait_send()
                    if 2 not in self.phases:
                        self.first_came(axis).wait_recv()
            if 2 in self.phases:
                for axis in (0, 1):
                    self.second(axis).wait_send()
                if not self.here:
                    self.arrive()

        def arrive(self):
            self.here = True
            for axis in (0, 1):
                self.second_came(axis).wait_recv()

    class Sum:
        def __init__(self, p, out, scratch):
            self.p, self.out = p, out
            self.a, self.b, self.send_a, self.recv_a, self.send_b, self.recv_b = scratch
            self.half = out.shape[0] // 2
            self.bits = (lax.rem(r, 2), r // 2)

        def rows(self, h):
            return pl.ds(h * self.half, self.half)

        def who(self, h):
            return across_y if h else across_x

        def first(self, h, k):
            other = 1 - self.bits[h]
            q = 2 * other + k if h else other + 2 * k
            return rcopy(
                self.p.at[q, self.rows(h)], self.a.at[h, k], self.send_a.at[h, k], self.recv_a.at[h, k], self.who(h), "replica"
            )

        def second(self, h):
            piece = self.a.at[h, 1 - self.bits[1 - h]]
            return rcopy(piece, self.b.at[h], self.send_b.at[h], self.recv_b.at[h], self.who(1 - h), "replica")

        def each(self, h, put):
            step = 16

            @pl.loop(0, self.half // step)
            def _(i):
                put(pl.multiple_of(i * step, step), step)

        def mine(self, h, k, at, step):
            q = 2 * self.bits[1] + k if h else self.bits[0] + 2 * k
            rows = pl.ds(h * self.half + at, step)
            return self.p[q, rows, :].astype(f32) + self.a[h, k, pl.ds(at, step), :].astype(f32)

        def begin(self):
            for h in (0, 1):
                self.first(h, 1 - self.bits[1 - h]).start()
            for h in (0, 1):
                self.first(h, self.bits[1 - h]).start()

        def step(self, s, j):
            pass

        def mid(self):
            for h in (0, 1):
                k = 1 - self.bits[1 - h]
                self.first(h, k).wait_recv()

                def put(at, step):
                    self.a[h, k, pl.ds(at, step), :] = self.mine(h, k, at, step).astype(bf16)

                self.each(h, put)
                self.second(h).start()

        def end(self):
            for h in (0, 1):
                k = self.bits[1 - h]
                self.first(h, k).wait_recv()
                self.second(h).wait_recv()

                def put(at, step):
                    total = self.mine(h, k, at, step) + self.b[h, pl.ds(at, step), :].astype(f32)
                    self.out[pl.ds(h * self.half + at, step), :] = total.astype(bf16)

                self.each(h, put)
            for h in (0, 1):
                for k in (0, 1):
                    self.first(h, k).wait_send()
                self.second(h).wait_send()

    gathers = [Gather(*t) for t in zip(ag_in, ag_out, ag_sem)]
    scatters = [Scatter(*t) for t in zip(rs_in, products, rs_out, rs_scr)]
    exchanges = [Exchange(*t) for t in zip(a2a_in, a2a_out, a2a_sem, a2a_blocks)]
    square_parts = [Spread(*t) for t in zip(sp_in, sp_out, sp_sem, spreads)]
    square_parts += [Sum(*t) for t in zip(sum_in, sum_out, sum_scr)]
    chained = [Spread(a2a_out[i], out, sems, (1, 2)) for i, out, sems in zip(chain, chain_out, chain_sem)]
    worker = work[0](gathers[0], square_parts, nz, z, (r, across_x, across_y, 3 - r), work_in, work_out, work_scr) if work else None

    def begin_chain():
        for i, part in zip(chain, chained):
            exchanges[i].arrive()
            part.begin()

    line_parts = gathers + scatters
    for part in gathers + exchanges + square_parts + scatters:
        part.begin()
    if worker:
        worker.begin()
    if line_parts:
        if chain_at == 0:
            begin_chain()
        for s in range(1, nz):
            @pl.loop(0, parts)
            def _(j):
                for part in line_parts:
                    part.step(s, j)

            for part in exchanges + scatters:
                part.after_step(s)
            if s == chain_at:
                begin_chain()
            if s == max(1, chain_at):
                for part in square_parts:
                    part.mid()
            if worker:
                worker.after_step(s)
    else:
        begin_chain()
        for part in square_parts:
            part.mid()
    for part in line_parts:
        part.end()
    for part in chained:
        part.mid()
    for part in exchanges + square_parts + chained:
        part.end()


class Forward:
    def __init__(self, gather, spreads, nz, z, blocks, ins, outs, scratch):
        self.gather, self.spreads, self.nz, self.z, self.blocks = gather, spreads, nz, z, blocks
        self.cot, self.w_down = ins[:2]
        self.hid, self.ggu = outs
        self.ghid = scratch[0]
        if spreads:
            self.w, self.sem = scratch[1:]
        else:
            self.w = ins[2:]
        self.rows = 2 * gather.x.shape[0]
        self.tile = min(256, self.hid.shape[1])

    def load(self, i, k):
        q = self.blocks[k]
        return pltpu.make_async_copy(self.spreads[i].out.at[q], self.w.at[i, q], self.sem.at[i, k])

    def each_tile(self, put):
        @pl.loop(0, self.hid.shape[1] // self.tile)
        def _(t):
            put(pl.multiple_of(t * self.tile, self.tile))

    def begin(self):
        if self.spreads:
            for i in (0, 1):
                for k in (0, 1, 2):
                    self.load(i, k).start()

        @pl.loop(0, self.nz)
        def _(b):
            rows = pl.ds(pl.multiple_of(b * self.rows, self.rows), self.rows)

            def put(first):
                cols = pl.ds(first, self.tile)
                self.ghid[rows, cols] = dot_t(self.cot[rows, :], self.w_down[cols, :])

            self.each_tile(put)

    def weights(self):
        if self.spreads:
            for i in (0, 1):
                self.spreads[i].arrive()
                self.load(i, 3).start()
            for i in (0, 1):
                for k in range(4):
                    self.load(i, k).wait()

    def chip(self, d):
        width = self.hid.shape[1]
        rows = pl.ds(pl.multiple_of(d * self.rows, self.rows), self.rows)

        def put(first):
            cols = pl.ds(first, self.tile)
            x = self.gather.out[pl.ds(2 * d, 2)].reshape(self.rows, -1)
            if self.spreads:
                gate, up = [dot(x, self.w[i, :, :, :, cols].reshape(x.shape[1], self.tile)) for i in (0, 1)]
            else:
                gate, up = [dot(x, w[:, cols]) for w in self.w]
            ghid = self.ghid[rows, cols]
            s = 1.0 / (1.0 + jnp.exp(-gate))
            silu = gate * s
            self.hid[rows, cols] = (silu * up).astype(bf16)
            self.ggu[rows, cols] = (ghid * up * s * (1.0 + gate * (1.0 - s))).astype(bf16)
            self.ggu[rows, pl.ds(width + first, self.tile)] = (ghid * silu).astype(bf16)

        self.each_tile(put)

    def away(self, s):
        self.gather.arrive(s)

        @pl.when(self.z >= s)
        def _():
            self.chip(self.z - s)

        if s > 0:
            @pl.when(self.z + s < self.nz)
            def _():
                self.chip(self.z + s)

    def after_step(self, s):
        last = max(1, self.nz - 2)
        if s == last:
            self.weights()
            for k in range(last):
                self.away(k)
        if s == self.nz - 1:
            for k in range(last, self.nz):
                self.away(k)


def line_comm(cid, name, us, ag=(), rs=(), a2a=(), spread=(), sums=(), chain=(), chain_at=None, work=None, parts=2):
    n = lax.axis_size("inner")
    nz = n // 2
    chain_at = nz - 2 if chain_at is None else chain_at
    dma = pltpu.SemaphoreType.DMA
    hbm = pl.BlockSpec(memory_space=pl.ANY)
    vmem = pl.BlockSpec(memory_space=pltpu.VMEM)
    products = [tuple(t[2:] for t in p) if isinstance(p, list) else () for p in rs]
    rs_out = [
        (p[0][0].shape[0] // n, p[0][1].shape[0 if p[0][2] else 1]) if isinstance(p, list) else (p.shape[0] // n, p.shape[1])
        for p in rs
    ]
    rs_in = []
    for p, shape in zip(rs, rs_out):
        rs_in += [a for t in p for a in t[:2]] if isinstance(p, list) else [p.reshape((n,) + shape)]
    sums = [p.reshape((4, p.shape[0] // 4) + p.shape[1:]) for p in sums]
    work_in, work_out, work_scratch = work[1:] if work else ((), (), [])
    inputs, in_specs, out_shape, out_specs, scratch = [], [], [], [], []

    def give(arrays, space):
        inputs.extend(arrays)
        in_specs.extend([space] * len(arrays))

    def get(shape, dtype, space):
        out_shape.append(jax.ShapeDtypeStruct(shape, dtype))
        out_specs.append(space)

    near = vmem if work else hbm
    give(ag, hbm)
    give(rs_in, vmem)
    give([w for t in a2a for w in t[0]], hbm)
    aliases = {len(inputs) + i: len(ag) + len(rs) + len(a2a) + i for i, (_, ph) in enumerate(spread) if 1 not in ph}
    give([b for b, _ in spread], hbm)
    give(sums, vmem)
    give(work_in, vmem)
    for x in ag:
        get((n,) + x.shape, x.dtype, near)
        scratch += [dma, dma((nz, parts)), dma((nz + 1, parts)), dma((nz, parts)), dma((nz + 1, parts))]
        scratch += [dma((2, nz, parts)), dma((2, nz, parts))]
    for shape, flips in zip(rs_out, products):
        get(shape, f32, vmem)
        scratch += [pltpu.VMEM((n,) + shape, bf16)] if flips else []
        scratch += [pltpu.VMEM((nz,) + shape, bf16)] * 3 + [dma((nz, parts))] * 6
    for t in a2a:
        get(t[1], t[0][0].dtype, hbm)
        scratch += [dma((t[4],)), dma((n, t[4])), dma((n, t[4]))]
    for b, phases in spread:
        get(b.shape if 1 not in phases else (4,) + b.shape, b.dtype, hbm)
        scratch += [dma, dma((2,)), dma((2,)), dma((2,)), dma((2,))]
    for p in sums:
        get(p.shape[1:], bf16, vmem)
        half = (p.shape[1] // 2, p.shape[2])
        scratch += [pltpu.VMEM((2, 2) + half, bf16), pltpu.VMEM((2,) + half, bf16)]
        scratch += [dma((2, 2)), dma((2, 2)), dma((2,)), dma((2,))]
    for i in chain:
        get((4,) + a2a[i][1], a2a[i][0][0].dtype, hbm)
        scratch += [dma, dma((2,)), dma((2,)), dma((2,)), dma((2,))]
    for shape in work_out:
        get(shape, bf16, vmem)
    scratch += work_scratch
    outs = pl.pallas_call(
        functools.partial(
            line_body,
            n,
            len(ag),
            products,
            [(len(t[0]),) + t[2:6] for t in a2a],
            [ph for _, ph in spread],
            len(sums),
            chain,
            chain_at,
            (work[0], len(work_in), len(work_out), len(work_scratch)) if work else None,
            parts,
        ),
        out_shape=out_shape,
        in_specs=in_specs,
        out_specs=out_specs,
        input_output_aliases=aliases,
        scratch_shapes=scratch,
        compiler_params=pltpu.CompilerParams(
            collective_id=cid, has_side_effects=True, vmem_limit_bytes=62 * 2**20
        ),
        cost_estimate=pl.CostEstimate(flops=us * 1150000000, bytes_accessed=us * 3600000, transcendentals=0),
        name=name,
    )(*inputs)
    return [o.reshape((-1,) + o.shape[2:]) if i < len(ag) else o for i, o in enumerate(outs)]


def rotate(flat, cosine, sine):
    return flat * cosine + pltpu.roll(flat, HEAD_DIM // 2, 1) * sine


def squash(q, k, piece, keys, length):
    scale = -math.log2(math.e) / math.sqrt(HEAD_DIM)
    sg = 1.0 / (1.0 + jnp.exp2(dot_t(q, k) * scale + math.log2(length)))
    row = lax.broadcasted_iota(jnp.int32, (PIECE, PIECE), 0)
    col = lax.broadcasted_iota(jnp.int32, (PIECE, PIECE), 1)
    return sg, (col <= row) | (piece >= 0)


def masked(value, visible, keys):
    last = jnp.where(visible, value[:, keys - PIECE :], 0.0)
    return last if keys == PIECE else jnp.concatenate([value[:, : keys - PIECE], last], axis=1)


def attn_body(heads, length, lin, cosine, sine, piece, out, rot):
    h, b = pl.program_id(0), pl.program_id(1)
    at = lambda part: pl.ds(pl.multiple_of((part * heads + h) * HEAD_DIM, HEAD_DIM), HEAD_DIM)
    blocks = length // PIECE

    @pl.when(b == 0)
    def _():
        @pl.loop(0, blocks)
        def _(i):
            rows = pl.ds(pl.multiple_of(i * PIECE, PIECE), PIECE)
            for part in (0, 1):
                rot[rows, at(part)] = rotate(lin[rows, at(part)], cosine[rows, :], sine[rows, :]).astype(bf16)
            rot[rows, at(2)] = lin[rows, at(2)].astype(bf16)

    for i in range(blocks):
        @pl.when(b == i)
        def _():
            keys = (i + 1) * PIECE
            own = pl.ds(i * PIECE, PIECE)
            sg, visible = squash(rot[own, at(0)], rot[0:keys, at(1)], piece[...], keys, length)
            out[...] = dot(masked(sg, visible, keys).astype(bf16), rot[0:keys, at(2)]).astype(bf16)


def attention(lin, cosine, sine, piece):
    length, width = lin.shape
    heads = width // 3 // HEAD_DIM
    whole = lambda x: pl.BlockSpec(x.shape, lambda h, b: (0, 0))
    return pl.pallas_call(
        functools.partial(attn_body, heads, length),
        grid=(heads, length // PIECE),
        out_shape=[
            jax.ShapeDtypeStruct((length, width // 3), bf16),
            jax.ShapeDtypeStruct((length, width), bf16),
        ],
        in_specs=[whole(lin), whole(cosine), whole(sine), pl.BlockSpec((PIECE, 1), lambda h, b: (b, 0))],
        out_specs=[
            pl.BlockSpec((PIECE, HEAD_DIM), lambda h, b: (b, h)),
            pl.BlockSpec((length, width), lambda h, b: (0, 0)),
        ],
        compiler_params=pltpu.CompilerParams(vmem_limit_bytes=48 * 2**20),
        cost_estimate=pl.CostEstimate(
            flops=4 * heads * length * length * HEAD_DIM // 2, bytes_accessed=8 * length * width, transcendentals=heads * length * length
        ),
        name="attention",
    )(lin, cosine, sine, piece)


def attn_back_body(heads, length, rot, go, cosine, sine, piece, out, gk, gv):
    h, b = pl.program_id(0), pl.program_id(1)
    at = lambda part: pl.ds(pl.multiple_of((part * heads + h) * HEAD_DIM, HEAD_DIM), HEAD_DIM)
    blocks = length // PIECE
    inv_root = 1.0 / math.sqrt(HEAD_DIM)

    @pl.when(b == 0)
    def _():
        gk[...] = jnp.zeros_like(gk)
        gv[...] = jnp.zeros_like(gv)

    for i in range(blocks):
        @pl.when(b == i)
        def _():
            keys = (i + 1) * PIECE
            own = pl.ds(i * PIECE, PIECE)
            q, g = rot[own, at(0)], go[...]
            sg, visible = squash(q, rot[0:keys, at(1)], piece[...], keys, length)
            p = masked(sg, visible, keys).astype(bf16)
            gs = masked(dot_t(g, rot[0:keys, at(2)]) * sg * (1.0 - sg), visible, keys).astype(bf16)
            gq = dot(gs, rot[0:keys, at(1)]) * inv_root
            out[own, at(0)] = rotate(gq, cosine[own, :], -sine[own, :]).astype(bf16)
            gk[0:keys, :] += t_dot(gs, q)
            gv[0:keys, :] += t_dot(p, g)

    @pl.when(b == blocks - 1)
    def _():
        @pl.loop(0, blocks)
        def _(i):
            rows = pl.ds(pl.multiple_of(i * PIECE, PIECE), PIECE)
            out[rows, at(1)] = rotate(gk[rows, :] * inv_root, cosine[rows, :], -sine[rows, :]).astype(bf16)
            out[rows, at(2)] = gv[rows, :].astype(bf16)


def attention_back(rot, go, cosine, sine, piece):
    length, width = rot.shape
    heads = width // 3 // HEAD_DIM
    whole = lambda x: pl.BlockSpec(x.shape, lambda h, b: (0, 0))
    return pl.pallas_call(
        functools.partial(attn_back_body, heads, length),
        grid=(heads, length // PIECE),
        out_shape=jax.ShapeDtypeStruct((length, width), bf16),
        in_specs=[
            whole(rot),
            pl.BlockSpec((PIECE, HEAD_DIM), lambda h, b: (b, h)),
            whole(cosine),
            whole(sine),
            pl.BlockSpec((PIECE, 1), lambda h, b: (b, 0)),
        ],
        out_specs=pl.BlockSpec((length, width), lambda h, b: (0, 0)),
        scratch_shapes=[pltpu.VMEM((length, HEAD_DIM), f32)] * 2,
        compiler_params=pltpu.CompilerParams(vmem_limit_bytes=48 * 2**20),
        cost_estimate=pl.CostEstimate(
            flops=10 * heads * length * length * HEAD_DIM // 2, bytes_accessed=8 * length * width, transcendentals=heads * length * length
        ),
        name="attention_back",
    )(rot, go, cosine, sine, piece)


def columns_out(w):
    n, nr = lax.axis_size("inner"), lax.axis_size("replica")
    part = w.shape[0] // nr
    cols = w.shape[1] // n

    def source(refs, other, m):
        rows = pl.ds(pl.multiple_of(lax.axis_index("replica") * part, part), part)
        return refs[0].at[rows, pl.ds(pl.multiple_of(other * cols, cols), cols)]

    return ((w,), (n, part, cols), source, lambda ref, other, m: ref.at[other], 1, False)


def to_all(block):
    n = lax.axis_size("inner")
    return ((block,), (n,) + block.shape, lambda refs, other, m: refs[0], lambda ref, other, m: ref.at[other], 1, False)


def rows_back(share, first, count, late=False):
    n, part, _ = share.shape
    cols = first[1]

    def source(refs, other, m):
        return refs[0].at[other, :, pl.ds((first[0] + m) * cols, cols)]

    def target(ref, other, m):
        return ref.at[pl.ds(m * part, part), pl.ds(pl.multiple_of(other * cols, cols), cols)]

    return ((share,), (count * part, n * cols), source, target, count, late)


def sum_blocks(g):
    n = lax.axis_size("inner")
    cols = g.shape[1]
    return ((g,), (n,) + (g.shape[0] // n, cols), lambda refs, other, m: refs[0].at[pl.ds(pl.multiple_of(other * 16, 16), 16)], lambda ref, other, m: ref.at[other], 1, False)


def shares_first(x):
    n, nr = lax.axis_size("inner"), lax.axis_size("replica")
    part = x.shape[1] // n // nr
    return x.reshape(x.shape[0], n, nr, part).transpose(0, 2, 1, 3).reshape(x.shape)


def owners_first(x):
    n, nr = lax.axis_size("inner"), lax.axis_size("replica")
    part = x.shape[1] // n // nr
    return x.reshape(x.shape[0], nr, n, part).transpose(0, 2, 1, 3).reshape(x.shape)


def sum_share(product):
    return lax.psum_scatter(product.astype(bf16), "replica", scatter_dimension=0, tiled=True)


def join(block):
    return lax.all_gather(block, "replica", axis=0, tiled=False)


def flat(w):
    return w.reshape(-1, w.shape[-1])


def local(
    tokens,
    w_query,
    w_key,
    w_value,
    w_out,
    w_gate,
    w_up,
    w_down,
    gain_attn,
    gain_ffn,
    pieces,
    positions,
    cotangent,
):
    n = lax.axis_size("inner")
    nr = lax.axis_size("replica")
    square = nr == 4
    own, width = tokens.shape
    length = own * n
    rows = gain_attn.shape[0]
    after = lax.optimization_barrier

    marks = jnp.zeros((8, own), jnp.int32).at[0].set(pieces).at[1].set(positions)
    gains = jnp.zeros((8, rows), f32).at[0].set(gain_attn.astype(f32)).at[1].set(gain_ffn.astype(f32))
    q_share, k_share, v_share, marks, gains = line_comm(
        0,
        "load_attn", 25,
        a2a=[columns_out(w_query), columns_out(w_key), columns_out(w_value), to_all(marks), to_all(gains)],
    )
    qkv_share = jnp.concatenate([q_share, k_share, v_share], axis=2)
    loads = [columns_out(w_gate), columns_out(w_up)]
    if square:
        x, g_share, u_share, w_qkv = line_comm(
            1, "load_ffn", 80, ag=[shares_first(tokens)], a2a=loads, spread=[(qkv_share, (1, 2))]
        )
    else:
        w_qkv = join(qkv_share)
        x, g_share, u_share = line_comm(1, "load_ffn", 80, ag=[shares_first(tokens)], a2a=loads)
    w_qkv = flat(w_qkv)
    cot, x = after((cotangent, x))
    cot = lax.all_gather(cot, "inner", axis=0, tiled=True)
    pieces, positions = marks[:, 0].reshape(length, 1), marks[:, 1].reshape(length)
    attn_gain, ffn_gain = gains[:, 0].reshape(1, -1), gains[:, 1].reshape(1, -1)

    x = x.astype(f32)
    cosine, sine = rope_tables(positions)
    u1 = x * rms_scale(x)
    n1 = (u1 * shares_first(attn_gain)).astype(bf16)
    o, rot = attention(dot(n1, w_qkv), cosine, sine, pieces)
    if square:
        a, w_g, w_u = line_comm(2, "attn_out", 50, rs=[[(o, w_out, False, 0)]], spread=[(g_share, (1,)), (u_share, (1,))])
    else:
        w_g, w_u = join(g_share), join(u_share)
        (a,) = line_comm(2, "attn_out", 50, rs=[[(o, w_out, False, 0)]])
    mid = tokens.astype(f32) + a
    r2 = rms_scale(mid)
    u2 = mid * r2
    n2 = shares_first((u2 * ffn_gain).astype(bf16))
    ffn = w_down.shape[0]
    results = [(length, ffn), (length, 2 * ffn)]
    held = [pltpu.VMEM((length, ffn), f32)]
    if square:
        held += [pltpu.VMEM((2,) + w_g.shape, bf16), pltpu.SemaphoreType.DMA((2, 4))]
        n2, w_g, w_u, hid, ggu = line_comm(
            3,
            "ffn_forward",
            60,
            ag=[n2],
            spread=[(w_g, (2,)), (w_u, (2,))],
            work=(Forward, [cot, w_down], results, held),
        )
        w_g, w_u = flat(w_g), flat(w_u)
    else:
        w_g, w_u = flat(w_g), flat(w_u)
        n2, hid, ggu = line_comm(3, "ffn_forward", 60, ag=[n2], work=(Forward, [cot, w_down, w_g, w_u], results, held))

    g_down = t_dot(hid, cot).astype(bf16)
    gu = t_dot(n2, ggu).astype(bf16)
    gu, ggu = after((gu, ggu))
    gu_share = sum_share(gu)
    (gn2,) = line_comm(4, "scatter_gn2", 44, rs=[[(ggu, w_g, True, 0), (ggu, w_u, True, w_g.shape[1])]])
    gn2 = owners_first(gn2)
    gu2 = gn2 * ffn_gain
    ffn_gain_part = jnp.sum(gn2 * u2, axis=0)
    gmid = cotangent.astype(f32) + r2 * (gu2 - u2 * jnp.mean(gu2 * u2, axis=1, keepdims=True))
    if square:
        ga, down_share = line_comm(5, "gather_ga", 50, ag=[gmid.astype(bf16)], sums=[g_down])
    else:
        (ga,) = line_comm(5, "gather_ga", 40, ag=[gmid.astype(bf16)])
        down_share = sum_share(g_down)
    ga, down_share, gu_share = after((ga, down_share, gu_share))
    grad_down = join(down_share)

    go = dot_t(ga, w_out).astype(bf16)
    gqkv = attention_back(rot, go, cosine, sine, pieces)
    g_out = t_dot(o, ga).astype(bf16)
    g_qkv = t_dot(n1, gqkv).astype(bf16)
    gn1_part = dot_t(gqkv, w_qkv)
    attn_gain_part = jnp.sum(gn1_part * u1, axis=0, keepdims=True)
    gn1_part = gn1_part.astype(bf16)
    gains = jnp.stack([owners_first(attn_gain_part)[0].reshape(n, rows), ffn_gain_part.reshape(n, rows)], axis=1)
    gains = jnp.pad(gains, ((0, 0), (0, 14), (0, 0))).reshape(n * 16, rows)
    cols = w_gate.shape[1] // n
    head_cols = gqkv.shape[1] // 3
    gu_share = gu_share.reshape(n, -1, 2 * cols)
    if square:
        gn1, gate_rows, up_rows, gains, out_share, qkv_share, grad_gate = line_comm(
            6,
            "scatter_gn1",
            1,
            rs=[gn1_part],
            a2a=[rows_back(gu_share, (0, cols), 1), rows_back(gu_share, (1, cols), 1, True), sum_blocks(gains)],
            sums=[g_out, g_qkv],
            chain=(0,),
            chain_at=0,
        )
        gains = jnp.sum(gains, axis=0)
        qkv_back = rows_back(qkv_share.reshape(n, -1, 3 * head_cols), (0, head_cols), 3)
        gains, grad_down = after((gains, grad_down))
        mlp, qkv_rows, grad_up, grad_out, gains, grad_qkv = line_comm(
            7,
            "rows_attn",
            70,
            rs=[[(hid, w_down, False, 0)]],
            a2a=[qkv_back],
            spread=[(up_rows, (1, 2)), (out_share, (1, 2)), (gains, (1, 2))],
            chain=(0,),
            chain_at=0,
        )
        gains = jnp.sum(gains, axis=0)
    else:
        gu_back = rows_back(gu_share, (0, cols), 2)
        gn1, gu_rows, gains = line_comm(6, "scatter_gn1", 80, rs=[gn1_part], a2a=[gu_back, sum_blocks(gains)])
        gains = lax.psum(jnp.sum(gains, axis=0), "replica")
        qkv_back = rows_back(sum_share(g_qkv).reshape(n, -1, 3 * head_cols), (0, head_cols), 3)
        mlp, qkv_rows = line_comm(7, "rows_attn", 75, rs=[[(hid, w_down, False, 0)]], a2a=[qkv_back])
        grad_gu = join(gu_rows).reshape(nr, 2, -1, n * cols)
        grad_gate, grad_up, grad_out, grad_qkv = grad_gu[:, 0], grad_gu[:, 1], join(sum_share(g_out)), join(qkv_rows)
    output = (mid + mlp).astype(bf16)
    grad_qkv = grad_qkv.reshape(nr, 3, -1, width).astype(f32)

    gn1 = owners_first(gn1)
    own_x = tokens.astype(f32)
    r1 = rms_scale(own_x)
    u1 = own_x * r1
    gu1 = gn1 * attn_gain
    grad_tokens = gmid + r1 * (gu1 - u1 * jnp.mean(gu1 * u1, axis=1, keepdims=True))
    return (
        output,
        grad_tokens,
        grad_qkv[:, 0].reshape(w_query.shape),
        grad_qkv[:, 1].reshape(w_key.shape),
        grad_qkv[:, 2].reshape(w_value.shape),
        grad_out.reshape(w_out.shape).astype(f32),
        grad_gate.reshape(w_gate.shape).astype(f32),
        grad_up.reshape(w_up.shape).astype(f32),
        grad_down.reshape(w_down.shape).astype(f32),
        gains[0],
        gains[1],
    )


def solution(mesh):
    tok = P(("replica", "inner"), None)
    row = P("inner", None)
    vec = P("inner")
    mark = P(("replica", "inner"))
    return jax.shard_map(
        local,
        mesh=mesh,
        in_specs=(tok, row, row, row, row, row, row, row, vec, vec, mark, mark, tok),
        out_specs=(tok, tok, row, row, row, row, row, row, row, vec, vec),
        check_vma=False,
    )
```

```python
import functools
import math

import jax
import jax.numpy as jnp
from jax import lax
from jax.experimental import pallas as pl
from jax.experimental.pallas import tpu as pltpu
from jax.sharding import PartitionSpec as P

HEAD_DIM = 128
PIECE = 256
epsilon = 1e-06
rope_base = 10000.0
dims_rows = (((1,), (1,)), ((), ()))
dims_cols = (((0,), (0,)), ((), ()))
f32 = jnp.float32
bf16 = jnp.bfloat16


def dot(a, b):
    return jnp.dot(a, b, preferred_element_type=f32)


def dot_t(a, b):
    return lax.dot_general(a, b, dims_rows, preferred_element_type=f32)


def t_dot(a, b):
    return lax.dot_general(a, b, dims_cols, preferred_element_type=f32)


def rope_tables(positions):
    half_dim = HEAD_DIM // 2
    frequency = rope_base ** (-jnp.arange(half_dim, dtype=f32) * 2.0 / HEAD_DIM)
    angle = positions.astype(f32)[:, None] * frequency[None, :]
    cosine, sine = jnp.cos(angle), jnp.sin(angle)
    return jnp.concatenate([cosine, cosine], axis=1), jnp.concatenate([-sine, sine], axis=1)


def rms_scale(values):
    return lax.rsqrt(jnp.mean(values * values, axis=1, keepdims=True) + epsilon)


def rcopy(src, dst, ssem, rsem, to, axis="inner"):
    return pltpu.make_async_remote_copy(
        src_ref=src,
        dst_ref=dst,
        send_sem=ssem,
        recv_sem=rsem,
        device_id={axis: to},
        device_id_type=pl.DeviceIdType.MESH,
    )


def signal(sem, to, axis="inner"):
    pl.semaphore_signal(sem, inc=1, device_id={axis: to}, device_id_type=pl.DeviceIdType.MESH)


def line_body(n, n_ag, products, a2a_blocks, spreads, sum_kinds, chain, chain_at, work, owners, parts, *refs):
    refs = list(refs)
    nz = n // 2
    n_a2a = len(a2a_blocks)
    take = lambda count: [refs.pop(0) for _ in range(count)]
    n_sp, n_rs, n_sum = len(spreads), len(products), len(sum_kinds)
    ag_in, rs_in, a2a_in = take(n_ag), [take(sum(2 - made for _, _, made in t) or 1) for t in products], [take(t[0]) for t in a2a_blocks]
    sp_in, sum_in = take(n_sp), [take(2 if k == 2 else 1) for k in sum_kinds]
    work_in = take(work[1]) if work else []
    ag_out, rs_out, a2a_out, sp_out, sum_out = take(n_ag), take(n_rs), take(n_a2a), take(n_sp), take(n_sum)
    chain_out = take(len(chain))
    work_out = take(work[2]) if work else []
    ag_sem = [take(7) for _ in range(n_ag)]
    rs_scr = [take(10 if t else 9) for t in products]
    a2a_sem = [take(3) for _ in range(n_a2a)]
    sp_sem = [take(5 + (1 in ph)) for ph in spreads]
    sum_scr = [take(6 if k == 1 else 7) for k in sum_kinds]
    chain_sem = [take(6) for _ in chain]
    work_scr = take(work[3]) if work else []
    me = lax.axis_index("inner")
    z, c = me // 2, lax.rem(me, 2)
    sib = me + 1 - 2 * c
    r = lax.axis_index("replica")
    across_x, across_y = r + 1 - 2 * lax.rem(r, 2), r + 2 - 4 * (r // 2)
    barrier = pltpu.get_barrier_semaphore()
    more = 0
    if n_sp + n_sum + len(chain):
        signal(barrier, across_x, "replica")
        signal(barrier, across_y, "replica")
        more = 2
    if n_a2a:
        for k in range(1, n):
            signal(barrier, lax.rem(me + k, n))
        pl.semaphore_wait(barrier, n - 1 + more)
    else:
        signal(barrier, sib)

        @pl.when(z + 1 < nz)
        def _():
            signal(barrier, me + 2)

        @pl.when(z > 0)
        def _():
            signal(barrier, me - 2)

        pl.semaphore_wait(barrier, 1 + more + (z + nz - 1) // nz + (2 * nz - 2 - z) // nz)

    def rows_of(ref, j):
        count = ref.shape[0] // parts
        return pl.ds(pl.multiple_of(j * count, count), count)

    class Gather:
        def __init__(self, x, out, sems):
            self.x, self.out, self.here = x, out, set()
            self.own_sem, self.rs, self.rr, self.ls, self.lr, self.ss, self.sr = sems

        def own(self):
            return pltpu.make_async_copy(self.x, self.out.at[me], self.own_sem)

        def piece(self, block, s, j):
            rows = rows_of(self.x, j)
            return self.x.at[rows] if s == 0 else self.out.at[block, rows]

        def right(self, s, j):
            b = me - 2 * s
            dst = self.out.at[b, rows_of(self.x, j)]
            return rcopy(self.piece(b, s, j), dst, self.rs.at[s, j], self.rr.at[s + 1, j], me + 2)

        def left(self, s, j):
            b = me + 2 * s
            dst = self.out.at[b, rows_of(self.x, j)]
            return rcopy(self.piece(b, s, j), dst, self.ls.at[s, j], self.lr.at[s + 1, j], me - 2)

        def side(self, s, k, j):
            b = me - 2 * s if k == 0 else me + 2 * s
            dst = self.out.at[b, rows_of(self.x, j)]
            return rcopy(self.piece(b, s, j), dst, self.ss.at[k, s, j], self.sr.at[k, s, j], sib)

        def from_left(self, s, j):
            dst = self.out.at[me - 2 * s, rows_of(self.x, j)]
            return rcopy(dst, dst, self.rs.at[s, j], self.rr.at[s, j], me - 2)

        def from_right(self, s, j):
            dst = self.out.at[me + 2 * s, rows_of(self.x, j)]
            return rcopy(dst, dst, self.ls.at[s, j], self.lr.at[s, j], me + 2)

        def from_side(self, s, k, j):
            b = sib - 2 * s if k == 0 else sib + 2 * s
            dst = self.out.at[b, rows_of(self.x, j)]
            return rcopy(dst, dst, self.ss.at[k, s, j], self.sr.at[k, s, j], sib)

        def begin(self):
            @pl.loop(0, parts)
            def _(j):
                @pl.when(z + 1 < nz)
                def _():
                    self.right(0, j).start()

                @pl.when(z > 0)
                def _():
                    self.left(0, j).start()

            self.own().start()

            @pl.loop(0, parts)
            def _(j):
                self.side(0, 0, j).start()

        def step(self, s, j):
            @pl.when(z >= s)
            def _():
                self.from_left(s, j).wait_recv()

                @pl.when(z + 1 < nz)
                def _():
                    self.right(s, j).start()

                self.side(s, 0, j).start()

            @pl.when(z + s < nz)
            def _():
                self.from_right(s, j).wait_recv()

                @pl.when(z > 0)
                def _():
                    self.left(s, j).start()

                self.side(s, 1, j).start()

        def arrive(self, s):
            self.here.add(s)
            if s == 0:
                self.own().wait()

            @pl.loop(0, parts)
            def _(j):
                @pl.when(z >= s)
                def _():
                    self.from_side(s, 0, j).wait_recv()

                if s > 0:
                    @pl.when(z + s < nz)
                    def _():
                        self.from_side(s, 1, j).wait_recv()

        def end(self):
            for s in range(nz):
                if s not in self.here:
                    self.arrive(s)

                @pl.loop(0, parts)
                def _(j):
                    @pl.when(z >= s)
                    def _():
                        @pl.when(z + 1 < nz)
                        def _():
                            self.right(s, j).wait_send()

                        self.side(s, 0, j).wait_send()

                    @pl.when(z + s < nz)
                    def _():
                        @pl.when(z > 0)
                        def _():
                            self.left(s, j).wait_send()

                        if s > 0:
                            self.side(s, 1, j).wait_send()

    class Scatter:
        def __init__(self, operands, flips, out, scratch):
            self.pairs, self.out = [(x, w) + t[:2] for x, w, t in zip(operands[::2], operands[1::2], flips)], out
            self.p, *scratch = scratch if flips else operands + scratch
            self.sib_buf, self.l_buf, self.r_buf, self.ss, self.sr, self.rs, self.rr, self.ls, self.lr = scratch
            self.count = out.shape[0] // parts

        def side(self, d, j):
            rows = rows_of(self.out, j)
            return rcopy(self.p.at[2 * d + 1 - c, rows], self.sib_buf.at[d, rows], self.ss.at[d, j], self.sr.at[d, j], sib)

        def right(self, d, j, to=2):
            rows = rows_of(self.out, j)
            return rcopy(self.l_buf.at[d, rows], self.l_buf.at[d, rows], self.rs.at[d, j], self.rr.at[d, j], me + to)

        def left(self, d, j, to=-2):
            rows = rows_of(self.out, j)
            return rcopy(self.r_buf.at[d, rows], self.r_buf.at[d, rows], self.ls.at[d, j], self.lr.at[d, j], me + to)

        def product(self, d):
            own, width = self.out.shape
            rows = pl.ds(d * 2 * own, 2 * own)
            tile = min(512, width)

            @pl.loop(0, width // tile)
            def _(t):
                cols = pl.ds(pl.multiple_of(t * tile, tile), tile)
                total = 0.0
                for x, w, flip, first in self.pairs:
                    x = x[rows, first : first + w.shape[1 if flip else 0]]
                    total += dot_t(x, w[cols, :]) if flip else dot(x, w[:, cols])
                total = total.astype(bf16)
                self.p[2 * d, :, cols] = total[:own]
                self.p[2 * d + 1, :, cols] = total[own:]

        def begin(self):
            for s in range(1 if self.pairs else nz // 2):
                self.offer(s)

        def offer(self, s):
            for d in (nz - 1 - s, s):
                if self.pairs:
                    self.product(d)

                @pl.loop(0, parts)
                def _(j):
                    self.side(d, j).start()

        def after_step(self, s):
            if self.pairs and s < nz // 2:
                self.offer(s)

        def pair(self, d, rows):
            return self.p[2 * d + c, rows, :].astype(f32) + self.sib_buf[d, rows, :].astype(f32)

        def step(self, s, j):
            tick = (s - 1) * parts + j
            k = tick - z

            @pl.when((k >= 0) & (k < (nz - 1 - z) * parts))
            def _():
                d, i = nz - 1 - k // parts, lax.rem(k, parts)
                rows = rows_of(self.out, i)
                self.side(d, i).wait_recv()

                @pl.when(z > 0)
                def _():
                    self.right(d, i, -2).wait_recv()
                    self.l_buf[d, rows, :] = (self.pair(d, rows) + self.l_buf[d, rows, :].astype(f32)).astype(bf16)

                @pl.when(z == 0)
                def _():
                    self.l_buf[d, rows, :] = self.pair(d, rows).astype(bf16)

                self.right(d, i).start()

            m = tick - (nz - 1 - z)

            @pl.when((m >= 0) & (m < z * parts))
            def _():
                d, i = m // parts, lax.rem(m, parts)
                rows = rows_of(self.out, i)
                self.side(d, i).wait_recv()

                @pl.when(z + 1 < nz)
                def _():
                    self.left(d, i, 2).wait_recv()
                    self.r_buf[d, rows, :] = (self.pair(d, rows) + self.r_buf[d, rows, :].astype(f32)).astype(bf16)

                @pl.when(z + 1 == nz)
                def _():
                    self.r_buf[d, rows, :] = self.pair(d, rows).astype(bf16)

                self.left(d, i).start()

        def owners_first(self, rows):
            tiles = [self.out[rows, k * 128 : (k + 1) * 128] for k in range(self.out.shape[1] // 128)]
            low = lax.broadcasted_iota(jnp.int32, tiles[0].shape, 1) < 64
            for k in range(len(tiles)):
                i = k // 2
                first = 2 * (k % 2) * n + i
                a, b = tiles[first // 2], tiles[(first + n) // 2]
                new = jnp.where(low, pltpu.roll(a, 64, 1), b) if i % 2 else jnp.where(low, a, pltpu.roll(b, 64, 1))
                self.out[rows, k * 128 : (k + 1) * 128] = new

        def end(self):
            @pl.loop(0, parts)
            def _(j):
                rows = rows_of(self.out, j)
                self.side(z, j).wait_recv()
                self.out[rows, :] = self.pair(z, rows)

                @pl.when(z > 0)
                def _():
                    self.right(z, j, -2).wait_recv()
                    self.out[rows, :] = self.out[rows, :] + self.l_buf[z, rows, :].astype(f32)

                @pl.when(z + 1 < nz)
                def _():
                    self.left(z, j, 2).wait_recv()
                    self.out[rows, :] = self.out[rows, :] + self.r_buf[z, rows, :].astype(f32)

                if owners:
                    self.owners_first(rows)

            for d in range(nz):
                @pl.loop(0, parts)
                def _(j):
                    self.side(d, j).wait_send()

                    @pl.when(d > z)
                    def _():
                        self.right(d, j).wait_send()

                    @pl.when(d < z)
                    def _():
                        self.left(d, j).wait_send()

    class Exchange:
        def __init__(self, src, dst, sems, blocks):
            self.src, self.dst = src, dst
            self.own_sem, self.sent, self.recv = sems
            _, self.src_of, self.dst_of, self.count, self.late = blocks
            self.arrived = False

        def to(self, k, m):
            other = lax.rem(me + k, n)
            return rcopy(
                self.src_of(self.src, other, m), self.dst_of(self.dst, me, m), self.sent.at[k, m], self.recv.at[k, m], other
            )

        def came(self, k, m):
            other = lax.rem(me - k + n, n)
            return rcopy(
                self.src_of(self.src, other, m), self.dst_of(self.dst, other, m), self.sent.at[k, m], self.recv.at[k, m], other
            )

        def own(self, m):
            return pltpu.make_async_copy(
                self.src_of(self.src, me, m), self.dst_of(self.dst, me, m), self.own_sem.at[m]
            )

        def send(self, first, last):
            for k in range(first, last):
                for m in range(self.count):
                    self.to(k, m).start()

        def begin(self):
            if not self.late:
                self.send(1, n)
            for m in range(self.count):
                self.own(m).start()

        def step(self, s, j):
            pass

        def after_step(self, s):
            if self.late:
                self.send(1 + (n - 1) * (s - 1) // (nz - 1), 1 + (n - 1) * s // (nz - 1))

        def arrive(self):
            if not self.arrived:
                self.arrived = True
                for m in range(self.count):
                    self.own(m).wait()
                for k in range(1, n):
                    for m in range(self.count):
                        self.came(k, m).wait_recv()

        def end(self):
            self.arrive()
            for k in range(1, n):
                for m in range(self.count):
                    self.to(k, m).wait_send()

    class Spread:
        def __init__(self, src, out, sems, phases):
            self.src, self.out, self.phases = src, out, phases
            if 1 in phases:
                self.held, *sems = sems
            self.own_sem, self.send, self.recv, self.send_half, self.recv_half = sems
            self.half, self.here = out.shape[1] // 2, False

        def own(self, leg):
            if leg == 0:
                return pltpu.make_async_copy(self.src, self.held, self.own_sem.at[0])
            return pltpu.make_async_copy(self.held, self.out.at[r], self.own_sem.at[1])

        def first(self, axis):
            to = across_y if axis else across_x
            return rcopy(self.src, self.out.at[r], self.send.at[axis], self.recv.at[axis], to, "replica")

        def first_came(self, axis):
            who = across_y if axis else across_x
            return rcopy(self.out.at[who], self.out.at[who], self.send.at[axis], self.recv.at[axis], who, "replica")

        def half_of(self, block, axis):
            return self.out.at[block, pl.ds(axis * self.half, self.half)]

        def second(self, axis):
            block, to = (across_x, across_y) if axis else (across_y, across_x)
            piece = self.half_of(block, axis)
            return rcopy(piece, piece, self.send_half.at[axis], self.recv_half.at[axis], to, "replica")

        def second_came(self, axis):
            piece = self.half_of(3 - r, axis)
            who = across_y if axis else across_x
            return rcopy(piece, piece, self.send_half.at[axis], self.recv_half.at[axis], who, "replica")

        def begin(self):
            if 1 in self.phases:
                self.first(0).start()
                self.first(1).start()
                self.own(0).start()
            else:
                self.second(0).start()
                self.second(1).start()

        def step(self, s, j):
            pass

        def mid(self):
            if self.phases == (1, 2):
                self.first_came(0).wait_recv()
                self.second(1).start()
                self.first_came(1).wait_recv()
                self.second(0).start()

        def end(self):
            if 1 in self.phases:
                self.own(0).wait()
                self.own(1).start()
                self.own(1).wait()
                for axis in (0, 1):
                    self.first(axis).wait_send()
                    if 2 not in self.phases:
                        self.first_came(axis).wait_recv()
            if 2 in self.phases:
                for axis in (0, 1):
                    self.second(axis).wait_send()
                if not self.here:
                    self.arrive()

        def arrive(self):
            self.here = True
            for axis in (0, 1):
                self.second_came(axis).wait_recv()

    class Sum:
        def __init__(self, operands, out, scratch):
            self.factors, self.out = operands if len(operands) > 1 else None, out
            self.p, *scratch = scratch if self.factors else operands + scratch
            self.a, self.b, self.send_a, self.recv_a, self.send_b, self.recv_b = scratch
            self.half = out.shape[0] // 2
            self.bits = (lax.rem(r, 2), r // 2)

        def rows(self, h):
            return pl.ds(h * self.half, self.half)

        def who(self, h):
            return across_y if h else across_x

        def first(self, h, k):
            other = 1 - self.bits[h]
            q = 2 * other + k if h else other + 2 * k
            return rcopy(
                self.p.at[q, self.rows(h)], self.a.at[h, k], self.send_a.at[h, k], self.recv_a.at[h, k], self.who(h), "replica"
            )

        def second(self, h):
            piece = self.a.at[h, 1 - self.bits[1 - h]]
            return rcopy(piece, self.b.at[h], self.send_b.at[h], self.recv_b.at[h], self.who(1 - h), "replica")

        def each(self, h, put):
            step = 16

            @pl.loop(0, self.half // step)
            def _(i):
                put(pl.multiple_of(i * step, step), step)

        def mine(self, h, k, at, step):
            q = 2 * self.bits[1] + k if h else self.bits[0] + 2 * k
            rows = pl.ds(h * self.half + at, step)
            return self.p[q, rows, :].astype(f32) + self.a[h, k, pl.ds(at, step), :].astype(f32)

        def product(self):
            x, w = self.factors
            rows, width = self.out.shape
            tile = min(512, width)
            while width % tile:
                tile -= 128

            @pl.loop(0, width // tile)
            def _(t):
                cols = pl.ds(pl.multiple_of(t * tile, tile), tile)
                if rows % 128:
                    self.p[:, :, cols] = t_dot(x[...], w[:, cols]).astype(bf16).reshape(4, rows, tile)
                else:
                    for q in range(4):
                        self.p[q, :, cols] = t_dot(x[:, q * rows : (q + 1) * rows], w[:, cols]).astype(bf16)

        def begin(self):
            if self.factors:
                self.product()
            for h in (0, 1):
                self.first(h, 1 - self.bits[1 - h]).start()
            for h in (0, 1):
                self.first(h, self.bits[1 - h]).start()

        def step(self, s, j):
            pass

        def mid(self):
            for h in (0, 1):
                k = 1 - self.bits[1 - h]
                self.first(h, k).wait_recv()

                def put(at, step):
                    self.a[h, k, pl.ds(at, step), :] = self.mine(h, k, at, step).astype(bf16)

                self.each(h, put)
                self.second(h).start()

        def end(self):
            for h in (0, 1):
                k = self.bits[1 - h]
                self.first(h, k).wait_recv()
                self.second(h).wait_recv()

                def put(at, step):
                    total = self.mine(h, k, at, step) + self.b[h, pl.ds(at, step), :].astype(f32)
                    self.out[pl.ds(h * self.half + at, step), :] = total.astype(bf16)

                self.each(h, put)
            for h in (0, 1):
                for k in (0, 1):
                    self.first(h, k).wait_send()
                self.second(h).wait_send()

    gathers = [Gather(*t) for t in zip(ag_in, ag_out, ag_sem)]

    def operands(given, flips):
        for i, (_, _, made) in enumerate(flips):
            if made:
                given.insert(2 * i, work_out[0])
        return given

    rs_in = [operands(*t) for t in zip(rs_in, products)]
    sum_in = [given + work_out[:1] if k == 3 else given for given, k in zip(sum_in, sum_kinds)]
    scatters = [Scatter(*t) for t in zip(rs_in, products, rs_out, rs_scr)]
    exchanges = [Exchange(*t) for t in zip(a2a_in, a2a_out, a2a_sem, a2a_blocks)]
    square_parts = [Spread(*t) for t in zip(sp_in, sp_out, sp_sem, spreads)]
    square_parts += [Sum(*t) for t in zip(sum_in, sum_out, sum_scr)]
    chained = [Spread(a2a_out[i], out, sems, (1, 2)) for i, out, sems in zip(chain, chain_out, chain_sem)]
    worker = work[0](gathers, square_parts, nz, z, (r, across_x, across_y, 3 - r), work_in, work_out, work_scr) if work else None

    def begin_chain():
        for i, part in zip(chain, chained):
            exchanges[i].arrive()
            part.begin()

    line_parts = gathers + scatters
    for part in gathers + exchanges:
        part.begin()
    if worker and worker.early:
        worker.begin()
    for part in square_parts:
        part.begin()
    if chain and worker:
        begin_chain()
    for part in scatters:
        part.begin()
    if worker and not worker.early:
        worker.begin()
    if line_parts:
        if chain_at == 0 and not worker:
            begin_chain()
        for s in range(1, nz):
            @pl.loop(0, parts)
            def _(j):
                for part in line_parts:
                    part.step(s, j)

            for part in exchanges + scatters:
                part.after_step(s)
            if s == chain_at:
                begin_chain()
            if s == max(1, chain_at):
                for part in square_parts:
                    part.mid()
            if worker:
                worker.after_step(s)
    else:
        begin_chain()
        for part in square_parts:
            part.mid()
    for part in line_parts:
        part.end()
    for part in chained:
        part.mid()
    for part in exchanges + square_parts + chained:
        part.end()


class Backward:
    early = True

    def __init__(self, gathers, spreads, nz, z, blocks, ins, outs, scratch):
        self.ga, self.w_out, self.rot, self.cosine, self.sine, self.piece = ins
        (self.out,) = outs
        self.go, self.gk, self.gv = scratch

    def begin(self):
        length, width = self.rot.shape
        heads, blocks = width // 3 // HEAD_DIM, length // PIECE
        rot, out, cosine, sine, gk, gv = self.rot, self.out, self.cosine, self.sine, self.gk, self.gv
        inv_root = 1.0 / math.sqrt(HEAD_DIM)

        @pl.loop(0, blocks)
        def _(i):
            rows = pl.ds(pl.multiple_of(i * PIECE, PIECE), PIECE)
            self.go[rows, :] = dot_t(self.ga[rows, :], self.w_out[...]).astype(bf16)

        @pl.loop(0, heads)
        def _(h):
            at = lambda part: pl.ds(pl.multiple_of((part * heads + h) * HEAD_DIM, HEAD_DIM), HEAD_DIM)
            gk[...] = jnp.zeros_like(gk)
            gv[...] = jnp.zeros_like(gv)
            for i in range(blocks):
                keys = (i + 1) * PIECE
                own = pl.ds(i * PIECE, PIECE)
                q, g = rot[own, at(0)], self.go[own, at(0)]
                sg, visible = squash(q, rot[0:keys, at(1)], self.piece[own, :], keys, length)
                p = masked(sg, visible, keys).astype(bf16)
                gs = masked(dot_t(g, rot[0:keys, at(2)]) * sg * (1.0 - sg), visible, keys).astype(bf16)
                gq = dot(gs, rot[0:keys, at(1)]) * inv_root
                out[own, at(0)] = rotate(gq, cosine[own, :], -sine[own, :]).astype(bf16)
                gk[0:keys, :] += t_dot(gs, q)
                gv[0:keys, :] += t_dot(p, g)

            @pl.loop(0, blocks)
            def _(i):
                rows = pl.ds(pl.multiple_of(i * PIECE, PIECE), PIECE)
                out[rows, at(1)] = rotate(gk[rows, :] * inv_root, cosine[rows, :], -sine[rows, :]).astype(bf16)
                out[rows, at(2)] = gv[rows, :].astype(bf16)

    def after_step(self, s):
        pass


class Forward:
    early = False

    def __init__(self, gathers, spreads, nz, z, blocks, ins, outs, scratch):
        (gather,) = gathers
        self.gather, self.spreads, self.nz, self.z, self.blocks = gather, spreads, nz, z, blocks
        self.cot, self.w_down = ins[:2]
        self.hid, self.ggu = outs
        self.ghid = scratch[0]
        if spreads:
            self.w, self.sem = scratch[1:]
        else:
            self.w = ins[2:]
        self.rows = 2 * gather.x.shape[0]
        self.tile = min(256, self.hid.shape[1])

    def load(self, i, k):
        q = self.blocks[k]
        return pltpu.make_async_copy(self.spreads[i].out.at[q], self.w.at[i, q], self.sem.at[i, k])

    def each_tile(self, put):
        @pl.loop(0, self.hid.shape[1] // self.tile)
        def _(t):
            put(pl.multiple_of(t * self.tile, self.tile))

    def begin(self):
        if self.spreads:
            for i in (0, 1):
                for k in (0, 1, 2):
                    self.load(i, k).start()

        @pl.loop(0, self.nz)
        def _(b):
            rows = pl.ds(pl.multiple_of(b * self.rows, self.rows), self.rows)

            def put(first):
                cols = pl.ds(first, self.tile)
                self.ghid[rows, cols] = dot_t(self.cot[rows, :], self.w_down[cols, :])

            self.each_tile(put)

    def weights(self):
        if self.spreads:
            for i in (0, 1):
                self.spreads[i].arrive()
                self.load(i, 3).start()
            for i in (0, 1):
                for k in range(4):
                    self.load(i, k).wait()

    def chip(self, d):
        width = self.hid.shape[1]
        rows = pl.ds(pl.multiple_of(d * self.rows, self.rows), self.rows)

        def put(first):
            cols = pl.ds(first, self.tile)
            x = self.gather.out[pl.ds(2 * d, 2)].reshape(self.rows, -1)
            if self.spreads:
                gate, up = [dot(x, self.w[i, :, :, :, cols].reshape(x.shape[1], self.tile)) for i in (0, 1)]
            else:
                gate, up = [dot(x, w[:, cols]) for w in self.w]
            ghid = self.ghid[rows, cols]
            s = 1.0 / (1.0 + jnp.exp(-gate))
            silu = gate * s
            self.hid[rows, cols] = (silu * up).astype(bf16)
            self.ggu[rows, cols] = (ghid * up * s * (1.0 + gate * (1.0 - s))).astype(bf16)
            self.ggu[rows, pl.ds(width + first, self.tile)] = (ghid * silu).astype(bf16)

        self.each_tile(put)

    def away(self, s):
        self.gather.arrive(s)

        @pl.when(self.z >= s)
        def _():
            self.chip(self.z - s)

        if s > 0:
            @pl.when(self.z + s < self.nz)
            def _():
                self.chip(self.z + s)

    def after_step(self, s):
        last = max(1, self.nz - 2)
        if s == last:
            self.weights()
            for k in range(last):
                self.away(k)
        if s == self.nz - 1:
            for k in range(last, self.nz):
                self.away(k)


class Later:
    early = False

    def __init__(self, gathers, spreads, nz, z, blocks, ins, outs, scratch):
        (self.x, self.w), (self.out,) = ins, outs
        self.steps, self.tile = nz - 1, min(512, self.out.shape[1])

    def begin(self):
        pass

    def after_step(self, s):
        tiles = self.out.shape[1] // self.tile

        @pl.loop(tiles * (s - 1) // self.steps, tiles * s // self.steps)
        def _(t):
            cols = pl.ds(pl.multiple_of(t * self.tile, self.tile), self.tile)
            self.out[:, cols] = t_dot(self.x[...], self.w[:, cols]).astype(bf16)


def line_comm(cid, name, us, ag=(), rs=(), a2a=(), spread=(), sums=(), chain=(), chain_at=None, work=None, owners=False, parts=2):
    n = lax.axis_size("inner")
    nz = n // 2
    chain_at = nz - 2 if chain_at is None else chain_at
    dma = pltpu.SemaphoreType.DMA
    hbm = pl.BlockSpec(memory_space=pl.ANY)
    vmem = pl.BlockSpec(memory_space=pltpu.VMEM)
    products = [tuple(t[2:] + (t[0] is None,) for t in p) if isinstance(p, list) else () for p in rs]
    rs_out = [
        (p[0][0].shape[0] // n if p[0][0] is not None else work[2][0][0] // n, p[0][1].shape[0 if p[0][2] else 1]) if isinstance(p, list) else (p.shape[0] // n, p.shape[1])
        for p in rs
    ]
    rs_in = []
    for p, shape in zip(rs, rs_out):
        rs_in += [a for t in p for a in t[:2] if a is not None] if isinstance(p, list) else [p.reshape((n,) + shape)]
    sum_shapes = [(p[0].shape[1] // 4, p[2]) if isinstance(p, tuple) else (p.shape[0] // 4, p.shape[1]) for p in sums]
    sum_kinds = [(3 if p[1] is None else 2) if isinstance(p, tuple) else 1 for p in sums]
    sums = [p[:2] if isinstance(p, tuple) else (p.reshape((4,) + shape),) for p, shape in zip(sums, sum_shapes)]
    work_in, work_out, work_scratch = work[1:] if work else ((), (), [])
    inputs, in_specs, out_shape, out_specs, scratch = [], [], [], [], []

    def give(arrays, space):
        inputs.extend(arrays)
        in_specs.extend([space] * len(arrays))

    def get(shape, dtype, space):
        out_shape.append(jax.ShapeDtypeStruct(shape, dtype))
        out_specs.append(space)

    near = vmem if work else hbm
    give(ag, hbm)
    give(rs_in, vmem)
    give([w for t in a2a for w in t[0]], hbm)
    aliases = {len(inputs) + i: len(ag) + len(rs) + len(a2a) + i for i, (_, ph) in enumerate(spread) if 1 not in ph}
    give([b for b, _ in spread], hbm)
    give([x for p in sums for x in p if x is not None], vmem)
    give(work_in, vmem)
    for x in ag:
        get((n,) + x.shape, x.dtype, near)
        scratch += [dma, dma((nz, parts)), dma((nz + 1, parts)), dma((nz, parts)), dma((nz + 1, parts))]
        scratch += [dma((2, nz, parts)), dma((2, nz, parts))]
    for shape, flips in zip(rs_out, products):
        get(shape, f32, vmem)
        scratch += [pltpu.VMEM((n,) + shape, bf16)] if flips else []
        scratch += [pltpu.VMEM((nz,) + shape, bf16)] * 3 + [dma((nz, parts))] * 6
    for t in a2a:
        get(t[1], t[0][0].dtype, hbm)
        scratch += [dma((t[4],)), dma((n, t[4])), dma((n, t[4]))]
    for b, phases in spread:
        get(b.shape if 1 not in phases else (4,) + b.shape, b.dtype, hbm)
        scratch += [pltpu.VMEM(b.shape, b.dtype)] if 1 in phases else []
        scratch += [dma((2,)), dma((2,)), dma((2,)), dma((2,)), dma((2,))]
    for p, shape in zip(sums, sum_shapes):
        get(shape, bf16, vmem)
        half = (shape[0] // 2, shape[1])
        scratch += [pltpu.VMEM((4,) + shape, bf16)] if len(p) > 1 else []
        scratch += [pltpu.VMEM((2, 2) + half, bf16), pltpu.VMEM((2,) + half, bf16)]
        scratch += [dma((2, 2)), dma((2, 2)), dma((2,)), dma((2,))]
    for i in chain:
        get((4,) + a2a[i][1], a2a[i][0][0].dtype, hbm)
        scratch += [pltpu.VMEM(a2a[i][1], a2a[i][0][0].dtype), dma((2,)), dma((2,)), dma((2,)), dma((2,)), dma((2,))]
    for shape in work_out:
        get(shape, bf16, vmem)
    scratch += work_scratch
    outs = pl.pallas_call(
        functools.partial(
            line_body,
            n,
            len(ag),
            products,
            [(len(t[0]),) + t[2:6] for t in a2a],
            [ph for _, ph in spread],
            sum_kinds,
            chain,
            chain_at,
            (work[0], len(work_in), len(work_out), len(work_scratch)) if work else None,
            owners,
            parts,
        ),
        out_shape=out_shape,
        in_specs=in_specs,
        out_specs=out_specs,
        input_output_aliases=aliases,
        scratch_shapes=scratch,
        compiler_params=pltpu.CompilerParams(
            collective_id=cid, has_side_effects=True, vmem_limit_bytes=62 * 2**20
        ),
        cost_estimate=pl.CostEstimate(flops=us * 1150000000, bytes_accessed=us * 3600000, transcendentals=0),
        name=name,
    )(*inputs)
    return [o.reshape((-1,) + o.shape[2:]) if i < len(ag) else o for i, o in enumerate(outs)]


def rotate(flat, cosine, sine):
    return flat * cosine + pltpu.roll(flat, HEAD_DIM // 2, 1) * sine


def squash(q, k, piece, keys, length):
    scale = -math.log2(math.e) / math.sqrt(HEAD_DIM)
    sg = 1.0 / (1.0 + jnp.exp2(dot_t(q, k) * scale + math.log2(length)))
    row = lax.broadcasted_iota(jnp.int32, (PIECE, PIECE), 0)
    col = lax.broadcasted_iota(jnp.int32, (PIECE, PIECE), 1)
    return sg, (col <= row) | (piece >= 0)


def masked(value, visible, keys):
    last = jnp.where(visible, value[:, keys - PIECE :], 0.0)
    return last if keys == PIECE else jnp.concatenate([value[:, : keys - PIECE], last], axis=1)


def attn_body(heads, length, lin, cosine, sine, piece, out, rot):
    h, b = pl.program_id(0), pl.program_id(1)
    at = lambda part: pl.ds(pl.multiple_of((part * heads + h) * HEAD_DIM, HEAD_DIM), HEAD_DIM)
    blocks = length // PIECE

    @pl.when(b == 0)
    def _():
        @pl.loop(0, blocks)
        def _(i):
            rows = pl.ds(pl.multiple_of(i * PIECE, PIECE), PIECE)
            for part in (0, 1):
                rot[rows, at(part)] = rotate(lin[rows, at(part)], cosine[rows, :], sine[rows, :]).astype(bf16)
            rot[rows, at(2)] = lin[rows, at(2)].astype(bf16)

    for i in range(blocks):
        @pl.when(b == i)
        def _():
            keys = (i + 1) * PIECE
            own = pl.ds(i * PIECE, PIECE)
            sg, visible = squash(rot[own, at(0)], rot[0:keys, at(1)], piece[...], keys, length)
            out[...] = dot(masked(sg, visible, keys).astype(bf16), rot[0:keys, at(2)]).astype(bf16)


def attention(lin, cosine, sine, piece):
    length, width = lin.shape
    heads = width // 3 // HEAD_DIM
    whole = lambda x: pl.BlockSpec(x.shape, lambda h, b: (0, 0))
    return pl.pallas_call(
        functools.partial(attn_body, heads, length),
        grid=(heads, length // PIECE),
        out_shape=[
            jax.ShapeDtypeStruct((length, width // 3), bf16),
            jax.ShapeDtypeStruct((length, width), bf16),
        ],
        in_specs=[whole(lin), whole(cosine), whole(sine), pl.BlockSpec((PIECE, 1), lambda h, b: (b, 0))],
        out_specs=[
            pl.BlockSpec((PIECE, HEAD_DIM), lambda h, b: (b, h)),
            pl.BlockSpec((length, width), lambda h, b: (0, 0)),
        ],
        compiler_params=pltpu.CompilerParams(vmem_limit_bytes=48 * 2**20),
        cost_estimate=pl.CostEstimate(
            flops=4 * heads * length * length * HEAD_DIM // 2, bytes_accessed=8 * length * width, transcendentals=heads * length * length
        ),
        name="attention",
    )(lin, cosine, sine, piece)


def columns_out(w):
    n, nr = lax.axis_size("inner"), lax.axis_size("replica")
    part = w.shape[0] // nr
    cols = w.shape[1] // n

    def source(refs, other, m):
        rows = pl.ds(pl.multiple_of(lax.axis_index("replica") * part, part), part)
        return refs[0].at[rows, pl.ds(pl.multiple_of(other * cols, cols), cols)]

    return ((w,), (n, part, cols), source, lambda ref, other, m: ref.at[other], 1, False)


def to_all(block):
    n = lax.axis_size("inner")
    return ((block,), (n,) + block.shape, lambda refs, other, m: refs[0], lambda ref, other, m: ref.at[other], 1, False)


def rows_back(share, first, count, late=False):
    n, part, _ = share.shape
    cols = first[1]

    def source(refs, other, m):
        return refs[0].at[other, :, pl.ds((first[0] + m) * cols, cols)]

    def target(ref, other, m):
        return ref.at[pl.ds(m * part, part), pl.ds(pl.multiple_of(other * cols, cols), cols)]

    return ((share,), (count * part, n * cols), source, target, count, late)


def sum_blocks(g):
    n = lax.axis_size("inner")
    cols = g.shape[1]
    return ((g,), (n,) + (g.shape[0] // n, cols), lambda refs, other, m: refs[0].at[pl.ds(pl.multiple_of(other * 16, 16), 16)], lambda ref, other, m: ref.at[other], 1, False)


def shares_first(x):
    n, nr = lax.axis_size("inner"), lax.axis_size("replica")
    part = x.shape[1] // n // nr
    return x.reshape(x.shape[0], n, nr, part).transpose(0, 2, 1, 3).reshape(x.shape)


def owners_first(x):
    n, nr = lax.axis_size("inner"), lax.axis_size("replica")
    part = x.shape[1] // n // nr
    return x.reshape(x.shape[0], nr, n, part).transpose(0, 2, 1, 3).reshape(x.shape)


def sum_share(product):
    return lax.psum_scatter(product.astype(bf16), "replica", scatter_dimension=0, tiled=True)


def join(block):
    return lax.all_gather(block, "replica", axis=0, tiled=False)


def flat(w):
    return w.reshape(-1, w.shape[-1])


def local(
    tokens,
    w_query,
    w_key,
    w_value,
    w_out,
    w_gate,
    w_up,
    w_down,
    gain_attn,
    gain_ffn,
    pieces,
    positions,
    cotangent,
):
    n = lax.axis_size("inner")
    nr = lax.axis_size("replica")
    square = nr == 4
    own, width = tokens.shape
    length = own * n
    rows = gain_attn.shape[0]
    after = lax.optimization_barrier

    marks = jnp.zeros((8, own), jnp.int32).at[0].set(pieces).at[1].set(positions)
    gains = jnp.zeros((8, rows), f32).at[0].set(gain_attn.astype(f32)).at[1].set(gain_ffn.astype(f32))
    q_share, k_share, v_share, marks, gains = line_comm(
        0,
        "load_attn", 25,
        a2a=[columns_out(w_query), columns_out(w_key), columns_out(w_value), to_all(marks), to_all(gains)],
    )
    qkv_share = jnp.concatenate([q_share, k_share, v_share], axis=2)
    loads = [columns_out(w_gate), columns_out(w_up)]
    if square:
        x, g_share, u_share, w_qkv = line_comm(
            1, "load_ffn", 80, ag=[shares_first(tokens)], a2a=loads, spread=[(qkv_share, (1, 2))]
        )
    else:
        w_qkv = join(qkv_share)
        x, g_share, u_share = line_comm(1, "load_ffn", 80, ag=[shares_first(tokens)], a2a=loads)
    w_qkv = flat(w_qkv)
    cot, x = after((cotangent, x))
    cot = lax.all_gather(cot, "inner", axis=0, tiled=True)
    pieces, positions = marks[:, 0].reshape(length, 1), marks[:, 1].reshape(length)
    attn_gain, ffn_gain = gains[:, 0].reshape(1, -1), gains[:, 1].reshape(1, -1)

    x = x.astype(f32)
    cosine, sine = rope_tables(positions)
    u1 = x * rms_scale(x)
    n1 = (u1 * shares_first(attn_gain)).astype(bf16)
    o, rot = attention(dot(n1, w_qkv), cosine, sine, pieces)
    if square:
        a, w_g, w_u = line_comm(2, "attn_out", 50, rs=[[(o, w_out, False, 0)]], spread=[(g_share, (1,)), (u_share, (1,))])
    else:
        w_g, w_u = join(g_share), join(u_share)
        (a,) = line_comm(2, "attn_out", 50, rs=[[(o, w_out, False, 0)]])
    mid = tokens.astype(f32) + a
    r2 = rms_scale(mid)
    u2 = mid * r2
    n2 = shares_first((u2 * ffn_gain).astype(bf16))
    ffn = w_down.shape[0]
    results = [(length, ffn), (length, 2 * ffn)]
    held = [pltpu.VMEM((length, ffn), f32)]
    if square:
        held += [pltpu.VMEM((2,) + w_g.shape, bf16), pltpu.SemaphoreType.DMA((2, 4))]
        n2, w_g, w_u, hid, ggu = line_comm(
            3,
            "ffn_forward",
            60,
            ag=[n2],
            spread=[(w_g, (2,)), (w_u, (2,))],
            work=(Forward, [cot, w_down], results, held),
        )
        w_g, w_u = flat(w_g), flat(w_u)
    else:
        w_g, w_u = flat(w_g), flat(w_u)
        n2, hid, ggu = line_comm(3, "ffn_forward", 60, ag=[n2], work=(Forward, [cot, w_down, w_g, w_u], results, held))

    gu = t_dot(n2, ggu).astype(bf16)
    gu, ggu = after((gu, ggu))
    gu_share = sum_share(gu)
    tidy = square and width // n // nr == 64
    gn2, g_down = line_comm(4, "scatter_gn2", 44, owners=tidy, work=(Later, [hid, cot], [w_down.shape], []), rs=[[(ggu, w_g, True, 0), (ggu, w_u, True, w_g.shape[1])]])
    gn2 = gn2 if tidy else owners_first(gn2)
    gu2 = gn2 * ffn_gain
    ffn_gain_part = jnp.sum(gn2 * u2, axis=0)
    gmid = cotangent.astype(f32) + r2 * (gu2 - u2 * jnp.mean(gu2 * u2, axis=1, keepdims=True))
    if square:
        ga, down_share = line_comm(5, "gather_ga", 50, ag=[gmid.astype(bf16)], sums=[g_down])
    else:
        (ga,) = line_comm(5, "gather_ga", 40, ag=[gmid.astype(bf16)])
        down_share = sum_share(g_down)
    ga, down_share, gu_share = after((ga, down_share, gu_share))
    grad_down = join(down_share)

    cols = w_gate.shape[1] // n
    heads_width = rot.shape[1] // 3
    gu_share = gu_share.reshape(n, -1, 2 * cols)
    own_x = tokens.astype(f32)
    r1 = rms_scale(own_x)
    u1 = own_x * r1

    def gain_parts(gn1):
        both = jnp.stack([jnp.sum(gn1 * u1, axis=0).reshape(n, rows), ffn_gain_part.reshape(n, rows)], axis=1)
        return sum_blocks(jnp.pad(both, ((0, 0), (0, 14), (0, 0))).reshape(n * 16, rows))

    held = [pltpu.VMEM((length, heads_width), bf16)] + [pltpu.VMEM((length, HEAD_DIM), f32)] * 2
    work = (Backward, [ga, w_out, rot, cosine, sine, pieces], [rot.shape], held)
    gn1_part = [(None, w_qkv, True, 0)]
    if square:
        gn1, gate_rows, up_rows, out_share, qkv_share, grad_gate, _ = line_comm(
            6,
            "scatter_gn1",
            1,
            owners=tidy,
            rs=[gn1_part],
            a2a=[rows_back(gu_share, (0, cols), 1), rows_back(gu_share, (1, cols), 1, False)],
            sums=[(o, ga, width), (n1, None, rot.shape[1])],
            chain=(0,),
            chain_at=0,
            work=work,
        )
        gn1 = gn1 if tidy else owners_first(gn1)
        qkv_back = rows_back(qkv_share.reshape(n, -1, 3 * heads_width), (0, heads_width), 3)
        up_rows, grad_down = after((up_rows, grad_down))
        mlp, _, _, grad_up, grad_out, grad_qkv, gains = line_comm(
            7,
            "rows_attn",
            70,
            rs=[[(hid, w_down, False, 0)]],
            a2a=[qkv_back, gain_parts(gn1)],
            spread=[(up_rows, (1, 2)), (out_share, (1, 2))],
            chain=(0, 1),
            chain_at=0,
        )
        gains = jnp.sum(gains, axis=(0, 1))
    else:
        gu_back = rows_back(gu_share, (0, cols), 2)
        gn1, gu_rows, gqkv = line_comm(6, "scatter_gn1", 80, rs=[gn1_part], a2a=[gu_back], work=work)
        gn1 = owners_first(gn1)
        g_qkv = sum_share(t_dot(n1, gqkv))
        qkv_back = rows_back(g_qkv.reshape(n, -1, 3 * heads_width), (0, heads_width), 3)
        mlp, qkv_rows, gains = line_comm(
            7, "rows_attn", 75, rs=[[(hid, w_down, False, 0)]], a2a=[qkv_back, gain_parts(gn1)]
        )
        gains = lax.psum(jnp.sum(gains, axis=0), "replica")
        grad_gu = join(gu_rows).reshape(nr, 2, -1, n * cols)
        grad_gate, grad_up, grad_out, grad_qkv = grad_gu[:, 0], grad_gu[:, 1], join(sum_share(t_dot(o, ga))), join(qkv_rows)
    output = (mid + mlp).astype(bf16)
    grad_qkv = grad_qkv.reshape(nr, 3, -1, width).astype(f32)

    gu1 = gn1 * attn_gain
    grad_tokens = gmid + r1 * (gu1 - u1 * jnp.mean(gu1 * u1, axis=1, keepdims=True))
    return (
        output,
        grad_tokens,
        grad_qkv[:, 0].reshape(w_query.shape),
        grad_qkv[:, 1].reshape(w_key.shape),
        grad_qkv[:, 2].reshape(w_value.shape),
        grad_out.reshape(w_out.shape).astype(f32),
        grad_gate.reshape(w_gate.shape).astype(f32),
        grad_up.reshape(w_up.shape).astype(f32),
        grad_down.reshape(w_down.shape).astype(f32),
        gains[0],
        gains[1],
    )


def solution(mesh):
    tok = P(("replica", "inner"), None)
    row = P("inner", None)
    vec = P("inner")
    mark = P(("replica", "inner"))
    return jax.shard_map(
        local,
        mesh=mesh,
        in_specs=(tok, row, row, row, row, row, row, row, vec, vec, mark, mark, tok),
        out_specs=(tok, tok, row, row, row, row, row, row, row, vec, vec),
        check_vma=False,
    )
```

```python
import functools
import math

import jax
import jax.numpy as jnp
from jax import lax
from jax.experimental import pallas as pl
from jax.experimental.pallas import tpu as pltpu
from jax.sharding import PartitionSpec as P

HEAD_DIM = 128
PIECE = 256
epsilon = 1e-06
rope_base = 10000.0
dims_rows = (((1,), (1,)), ((), ()))
dims_cols = (((0,), (0,)), ((), ()))
f32 = jnp.float32
bf16 = jnp.bfloat16


def dot(a, b):
    return jnp.dot(a, b, preferred_element_type=f32)


def dot_t(a, b):
    return lax.dot_general(a, b, dims_rows, preferred_element_type=f32)


def t_dot(a, b):
    return lax.dot_general(a, b, dims_cols, preferred_element_type=f32)


def rope_tables(positions):
    half_dim = HEAD_DIM // 2
    frequency = rope_base ** (-jnp.arange(half_dim, dtype=f32) * 2.0 / HEAD_DIM)
    angle = positions.astype(f32)[:, None] * frequency[None, :]
    cosine, sine = jnp.cos(angle), jnp.sin(angle)
    return jnp.concatenate([cosine, cosine], axis=1), jnp.concatenate([-sine, sine], axis=1)


def rms_scale(values):
    return lax.rsqrt(jnp.mean(values * values, axis=1, keepdims=True) + epsilon)


def rcopy(src, dst, ssem, rsem, to, axis="inner"):
    return pltpu.make_async_remote_copy(
        src_ref=src,
        dst_ref=dst,
        send_sem=ssem,
        recv_sem=rsem,
        device_id={axis: to},
        device_id_type=pl.DeviceIdType.MESH,
    )


def signal(sem, to, axis="inner"):
    pl.semaphore_signal(sem, inc=1, device_id={axis: to}, device_id_type=pl.DeviceIdType.MESH)


def line_body(n, n_ag, products, a2a_blocks, spreads, sum_kinds, chain, chain_at, work, owners, parts, *refs):
    refs = list(refs)
    nz = n // 2
    n_a2a = len(a2a_blocks)
    take = lambda count: [refs.pop(0) for _ in range(count)]
    n_sp, n_rs, n_sum = len(spreads), len(products), len(sum_kinds)
    ag_in, rs_in, a2a_in = take(n_ag), [take(sum(2 - made for _, _, made in t) or 1) for t in products], [take(t[0]) for t in a2a_blocks]
    sp_in, sum_in = take(n_sp), [take(2 if k == 2 else 1) for k in sum_kinds]
    work_in = take(work[1]) if work else []
    ag_out, rs_out, a2a_out, sp_out, sum_out = take(n_ag), take(n_rs), take(n_a2a), take(n_sp), take(n_sum)
    chain_out = take(len(chain))
    work_out = take(work[2]) if work else []
    ag_sem = [take(7) for _ in range(n_ag)]
    rs_scr = [take(10 if t else 9) for t in products]
    a2a_sem = [take(3) for _ in range(n_a2a)]
    sp_sem = [take(5 + (1 in ph)) for ph in spreads]
    sum_scr = [take(6 if k == 1 else 7) for k in sum_kinds]
    chain_sem = [take(6) for _ in chain]
    work_scr = take(work[3]) if work else []
    me = lax.axis_index("inner")
    z, c = me // 2, lax.rem(me, 2)
    sib = me + 1 - 2 * c
    r = lax.axis_index("replica")
    across_x, across_y = r + 1 - 2 * lax.rem(r, 2), r + 2 - 4 * (r // 2)
    barrier = pltpu.get_barrier_semaphore()
    more = 0
    if n_sp + n_sum + len(chain):
        signal(barrier, across_x, "replica")
        signal(barrier, across_y, "replica")
        more = 2
    if n_a2a:
        for k in range(1, n):
            signal(barrier, lax.rem(me + k, n))
        pl.semaphore_wait(barrier, n - 1 + more)
    else:
        signal(barrier, sib)

        @pl.when(z + 1 < nz)
        def _():
            signal(barrier, me + 2)

        @pl.when(z > 0)
        def _():
            signal(barrier, me - 2)

        pl.semaphore_wait(barrier, 1 + more + (z + nz - 1) // nz + (2 * nz - 2 - z) // nz)

    def rows_of(ref, j):
        count = ref.shape[0] // parts
        return pl.ds(pl.multiple_of(j * count, count), count)

    class Gather:
        def __init__(self, x, out, sems):
            self.x, self.out, self.here = x, out, set()
            self.own_sem, self.rs, self.rr, self.ls, self.lr, self.ss, self.sr = sems

        def own(self):
            return pltpu.make_async_copy(self.x, self.out.at[me], self.own_sem)

        def piece(self, block, s, j):
            rows = rows_of(self.x, j)
            return self.x.at[rows] if s == 0 else self.out.at[block, rows]

        def right(self, s, j):
            b = me - 2 * s
            dst = self.out.at[b, rows_of(self.x, j)]
            return rcopy(self.piece(b, s, j), dst, self.rs.at[s, j], self.rr.at[s + 1, j], me + 2)

        def left(self, s, j):
            b = me + 2 * s
            dst = self.out.at[b, rows_of(self.x, j)]
            return rcopy(self.piece(b, s, j), dst, self.ls.at[s, j], self.lr.at[s + 1, j], me - 2)

        def side(self, s, k, j):
            b = me - 2 * s if k == 0 else me + 2 * s
            dst = self.out.at[b, rows_of(self.x, j)]
            return rcopy(self.piece(b, s, j), dst, self.ss.at[k, s, j], self.sr.at[k, s, j], sib)

        def from_left(self, s, j):
            dst = self.out.at[me - 2 * s, rows_of(self.x, j)]
            return rcopy(dst, dst, self.rs.at[s, j], self.rr.at[s, j], me - 2)

        def from_right(self, s, j):
            dst = self.out.at[me + 2 * s, rows_of(self.x, j)]
            return rcopy(dst, dst, self.ls.at[s, j], self.lr.at[s, j], me + 2)

        def from_side(self, s, k, j):
            b = sib - 2 * s if k == 0 else sib + 2 * s
            dst = self.out.at[b, rows_of(self.x, j)]
            return rcopy(dst, dst, self.ss.at[k, s, j], self.sr.at[k, s, j], sib)

        def begin(self):
            @pl.loop(0, parts)
            def _(j):
                @pl.when(z + 1 < nz)
                def _():
                    self.right(0, j).start()

                @pl.when(z > 0)
                def _():
                    self.left(0, j).start()

            self.own().start()

            @pl.loop(0, parts)
            def _(j):
                self.side(0, 0, j).start()

        def step(self, s, j):
            @pl.when(z >= s)
            def _():
                self.from_left(s, j).wait_recv()

                @pl.when(z + 1 < nz)
                def _():
                    self.right(s, j).start()

                self.side(s, 0, j).start()

            @pl.when(z + s < nz)
            def _():
                self.from_right(s, j).wait_recv()

                @pl.when(z > 0)
                def _():
                    self.left(s, j).start()

                self.side(s, 1, j).start()

        def arrive(self, s):
            self.here.add(s)
            if s == 0:
                self.own().wait()

            @pl.loop(0, parts)
            def _(j):
                @pl.when(z >= s)
                def _():
                    self.from_side(s, 0, j).wait_recv()

                if s > 0:
                    @pl.when(z + s < nz)
                    def _():
                        self.from_side(s, 1, j).wait_recv()

        def end(self):
            for s in range(nz):
                if s not in self.here:
                    self.arrive(s)

                @pl.loop(0, parts)
                def _(j):
                    @pl.when(z >= s)
                    def _():
                        @pl.when(z + 1 < nz)
                        def _():
                            self.right(s, j).wait_send()

                        self.side(s, 0, j).wait_send()

                    @pl.when(z + s < nz)
                    def _():
                        @pl.when(z > 0)
                        def _():
                            self.left(s, j).wait_send()

                        if s > 0:
                            self.side(s, 1, j).wait_send()

    class Scatter:
        def __init__(self, operands, flips, out, scratch):
            self.pairs, self.out = [(x, w) + t[:2] for x, w, t in zip(operands[::2], operands[1::2], flips)], out
            self.p, *scratch = scratch if flips else operands + scratch
            self.sib_buf, self.l_buf, self.r_buf, self.ss, self.sr, self.rs, self.rr, self.ls, self.lr = scratch
            self.count = out.shape[0] // parts

        def side(self, d, j):
            rows = rows_of(self.out, j)
            return rcopy(self.p.at[2 * d + 1 - c, rows], self.sib_buf.at[d, rows], self.ss.at[d, j], self.sr.at[d, j], sib)

        def right(self, d, j, to=2):
            rows = rows_of(self.out, j)
            return rcopy(self.l_buf.at[d, rows], self.l_buf.at[d, rows], self.rs.at[d, j], self.rr.at[d, j], me + to)

        def left(self, d, j, to=-2):
            rows = rows_of(self.out, j)
            return rcopy(self.r_buf.at[d, rows], self.r_buf.at[d, rows], self.ls.at[d, j], self.lr.at[d, j], me + to)

        def product(self, d):
            own, width = self.out.shape
            rows = pl.ds(d * 2 * own, 2 * own)
            tile = min(512, width)

            @pl.loop(0, width // tile)
            def _(t):
                cols = pl.ds(pl.multiple_of(t * tile, tile), tile)
                total = 0.0
                for x, w, flip, first in self.pairs:
                    x = x[rows, first : first + w.shape[1 if flip else 0]]
                    total += dot_t(x, w[cols, :]) if flip else dot(x, w[:, cols])
                total = total.astype(bf16)
                self.p[2 * d, :, cols] = total[:own]
                self.p[2 * d + 1, :, cols] = total[own:]

        def begin(self):
            for s in range(1 if self.pairs else nz // 2):
                self.offer(s)

        def offer(self, s):
            for d in (nz - 1 - s, s):
                if self.pairs:
                    self.product(d)

                @pl.loop(0, parts)
                def _(j):
                    self.side(d, j).start()

        def after_step(self, s):
            if self.pairs and s < nz // 2:
                self.offer(s)

        def pair(self, d, rows):
            return self.p[2 * d + c, rows, :].astype(f32) + self.sib_buf[d, rows, :].astype(f32)

        def step(self, s, j):
            tick = (s - 1) * parts + j
            k = tick - z

            @pl.when((k >= 0) & (k < (nz - 1 - z) * parts))
            def _():
                d, i = nz - 1 - k // parts, lax.rem(k, parts)
                rows = rows_of(self.out, i)
                self.side(d, i).wait_recv()

                @pl.when(z > 0)
                def _():
                    self.right(d, i, -2).wait_recv()
                    self.l_buf[d, rows, :] = (self.pair(d, rows) + self.l_buf[d, rows, :].astype(f32)).astype(bf16)

                @pl.when(z == 0)
                def _():
                    self.l_buf[d, rows, :] = self.pair(d, rows).astype(bf16)

                self.right(d, i).start()

            m = tick - (nz - 1 - z)

            @pl.when((m >= 0) & (m < z * parts))
            def _():
                d, i = m // parts, lax.rem(m, parts)
                rows = rows_of(self.out, i)
                self.side(d, i).wait_recv()

                @pl.when(z + 1 < nz)
                def _():
                    self.left(d, i, 2).wait_recv()
                    self.r_buf[d, rows, :] = (self.pair(d, rows) + self.r_buf[d, rows, :].astype(f32)).astype(bf16)

                @pl.when(z + 1 == nz)
                def _():
                    self.r_buf[d, rows, :] = self.pair(d, rows).astype(bf16)

                self.left(d, i).start()

        def owners_first(self, rows):
            tiles = [self.out[rows, k * 128 : (k + 1) * 128] for k in range(self.out.shape[1] // 128)]
            low = lax.broadcasted_iota(jnp.int32, tiles[0].shape, 1) < 64
            for k in range(len(tiles)):
                i = k // 2
                first = 2 * (k % 2) * n + i
                a, b = tiles[first // 2], tiles[(first + n) // 2]
                new = jnp.where(low, pltpu.roll(a, 64, 1), b) if i % 2 else jnp.where(low, a, pltpu.roll(b, 64, 1))
                self.out[rows, k * 128 : (k + 1) * 128] = new

        def end(self):
            @pl.loop(0, parts)
            def _(j):
                rows = rows_of(self.out, j)
                self.side(z, j).wait_recv()
                self.out[rows, :] = self.pair(z, rows)

                @pl.when(z > 0)
                def _():
                    self.right(z, j, -2).wait_recv()
                    self.out[rows, :] = self.out[rows, :] + self.l_buf[z, rows, :].astype(f32)

                @pl.when(z + 1 < nz)
                def _():
                    self.left(z, j, 2).wait_recv()
                    self.out[rows, :] = self.out[rows, :] + self.r_buf[z, rows, :].astype(f32)

                if owners:
                    self.owners_first(rows)

            for d in range(nz):
                @pl.loop(0, parts)
                def _(j):
                    self.side(d, j).wait_send()

                    @pl.when(d > z)
                    def _():
                        self.right(d, j).wait_send()

                    @pl.when(d < z)
                    def _():
                        self.left(d, j).wait_send()

    class Exchange:
        def __init__(self, src, dst, sems, blocks):
            self.src, self.dst = src, dst
            self.own_sem, self.sent, self.recv = sems
            _, self.src_of, self.dst_of, self.count, self.late = blocks
            self.arrived = False

        def to(self, k, m):
            other = lax.rem(me + k, n)
            return rcopy(
                self.src_of(self.src, other, m), self.dst_of(self.dst, me, m), self.sent.at[k, m], self.recv.at[k, m], other
            )

        def came(self, k, m):
            other = lax.rem(me - k + n, n)
            return rcopy(
                self.src_of(self.src, other, m), self.dst_of(self.dst, other, m), self.sent.at[k, m], self.recv.at[k, m], other
            )

        def own(self, m):
            return pltpu.make_async_copy(
                self.src_of(self.src, me, m), self.dst_of(self.dst, me, m), self.own_sem.at[m]
            )

        def send(self, first, last):
            for k in range(first, last):
                for m in range(self.count):
                    self.to(k, m).start()

        def begin(self):
            if not self.late:
                self.send(1, n)
            for m in range(self.count):
                self.own(m).start()

        def step(self, s, j):
            pass

        def after_step(self, s):
            if self.late:
                self.send(1 + (n - 1) * (s - 1) // (nz - 1), 1 + (n - 1) * s // (nz - 1))

        def arrive(self):
            if not self.arrived:
                self.arrived = True
                for m in range(self.count):
                    self.own(m).wait()
                for k in range(1, n):
                    for m in range(self.count):
                        self.came(k, m).wait_recv()

        def end(self):
            self.arrive()
            for k in range(1, n):
                for m in range(self.count):
                    self.to(k, m).wait_send()

    class Spread:
        factors = None

        def __init__(self, src, out, sems, phases):
            self.src, self.out, self.phases = src, out, phases
            if 1 in phases:
                self.held, *sems = sems
            self.own_sem, self.send, self.recv, self.send_half, self.recv_half = sems
            self.half, self.here = out.shape[1] // 2, False

        def own(self, leg):
            if leg == 0:
                return pltpu.make_async_copy(self.src, self.held, self.own_sem.at[0])
            return pltpu.make_async_copy(self.held, self.out.at[r], self.own_sem.at[1])

        def first(self, axis):
            to = across_y if axis else across_x
            return rcopy(self.src, self.out.at[r], self.send.at[axis], self.recv.at[axis], to, "replica")

        def first_came(self, axis):
            who = across_y if axis else across_x
            return rcopy(self.out.at[who], self.out.at[who], self.send.at[axis], self.recv.at[axis], who, "replica")

        def half_of(self, block, axis):
            return self.out.at[block, pl.ds(axis * self.half, self.half)]

        def second(self, axis):
            block, to = (across_x, across_y) if axis else (across_y, across_x)
            piece = self.half_of(block, axis)
            return rcopy(piece, piece, self.send_half.at[axis], self.recv_half.at[axis], to, "replica")

        def second_came(self, axis):
            piece = self.half_of(3 - r, axis)
            who = across_y if axis else across_x
            return rcopy(piece, piece, self.send_half.at[axis], self.recv_half.at[axis], who, "replica")

        def begin(self):
            if 1 in self.phases:
                self.first(0).start()
                self.first(1).start()
                self.own(0).start()
            else:
                self.second(0).start()
                self.second(1).start()

        def step(self, s, j):
            pass

        def mid(self):
            if self.phases == (1, 2):
                self.first_came(0).wait_recv()
                self.second(1).start()
                self.first_came(1).wait_recv()
                self.second(0).start()

        def end(self):
            if 1 in self.phases:
                self.own(0).wait()
                self.own(1).start()
                self.own(1).wait()
                for axis in (0, 1):
                    self.first(axis).wait_send()
                    if 2 not in self.phases:
                        self.first_came(axis).wait_recv()
            if 2 in self.phases:
                for axis in (0, 1):
                    self.second(axis).wait_send()
                if not self.here:
                    self.arrive()

        def arrive(self):
            self.here = True
            for axis in (0, 1):
                self.second_came(axis).wait_recv()

    class Sum:
        def __init__(self, operands, out, scratch):
            self.factors, self.out = operands if len(operands) > 1 else None, out
            self.p, *scratch = scratch if self.factors else operands + scratch
            self.a, self.b, self.send_a, self.recv_a, self.send_b, self.recv_b = scratch
            self.half = out.shape[0] // 2
            self.bits = (lax.rem(r, 2), r // 2)

        def rows(self, h):
            return pl.ds(h * self.half, self.half)

        def who(self, h):
            return across_y if h else across_x

        def first(self, h, k):
            other = 1 - self.bits[h]
            q = 2 * other + k if h else other + 2 * k
            return rcopy(
                self.p.at[q, self.rows(h)], self.a.at[h, k], self.send_a.at[h, k], self.recv_a.at[h, k], self.who(h), "replica"
            )

        def second(self, h):
            piece = self.a.at[h, 1 - self.bits[1 - h]]
            return rcopy(piece, self.b.at[h], self.send_b.at[h], self.recv_b.at[h], self.who(1 - h), "replica")

        def each(self, h, put):
            step = 16

            @pl.loop(0, self.half // step)
            def _(i):
                put(pl.multiple_of(i * step, step), step)

        def mine(self, h, k, at, step):
            q = 2 * self.bits[1] + k if h else self.bits[0] + 2 * k
            rows = pl.ds(h * self.half + at, step)
            return self.p[q, rows, :].astype(f32) + self.a[h, k, pl.ds(at, step), :].astype(f32)

        def product(self):
            x, w = self.factors
            rows, width = self.out.shape
            tile = min(512, width)
            while width % tile:
                tile -= 128

            @pl.loop(0, width // tile)
            def _(t):
                cols = pl.ds(pl.multiple_of(t * tile, tile), tile)
                if rows % 128:
                    self.p[:, :, cols] = t_dot(x[...], w[:, cols]).astype(bf16).reshape(4, rows, tile)
                else:
                    for q in range(4):
                        self.p[q, :, cols] = t_dot(x[:, q * rows : (q + 1) * rows], w[:, cols]).astype(bf16)

        def begin(self):
            if self.factors:
                self.product()
            for h in (0, 1):
                self.first(h, 1 - self.bits[1 - h]).start()
            for h in (0, 1):
                self.first(h, self.bits[1 - h]).start()

        def step(self, s, j):
            pass

        def mid(self):
            for h in (0, 1):
                k = 1 - self.bits[1 - h]
                self.first(h, k).wait_recv()

                def put(at, step):
                    self.a[h, k, pl.ds(at, step), :] = self.mine(h, k, at, step).astype(bf16)

                self.each(h, put)
                self.second(h).start()

        def end(self):
            for h in (0, 1):
                k = self.bits[1 - h]
                self.first(h, k).wait_recv()
                self.second(h).wait_recv()

                def put(at, step):
                    total = self.mine(h, k, at, step) + self.b[h, pl.ds(at, step), :].astype(f32)
                    self.out[pl.ds(h * self.half + at, step), :] = total.astype(bf16)

                self.each(h, put)
            for h in (0, 1):
                for k in (0, 1):
                    self.first(h, k).wait_send()
                self.second(h).wait_send()

    gathers = [Gather(*t) for t in zip(ag_in, ag_out, ag_sem)]

    def operands(given, flips):
        for i, (_, _, made) in enumerate(flips):
            if made:
                given.insert(2 * i, work_out[0])
        return given

    rs_in = [operands(*t) for t in zip(rs_in, products)]
    sum_in = [given + work_out[:1] if k == 3 else given for given, k in zip(sum_in, sum_kinds)]
    scatters = [Scatter(*t) for t in zip(rs_in, products, rs_out, rs_scr)]
    exchanges = [Exchange(*t) for t in zip(a2a_in, a2a_out, a2a_sem, a2a_blocks)]
    square_parts = [Spread(*t) for t in zip(sp_in, sp_out, sp_sem, spreads)]
    square_parts += [Sum(*t) for t in zip(sum_in, sum_out, sum_scr)]
    chained = [Spread(a2a_out[i], out, sems, (1, 2)) for i, out, sems in zip(chain, chain_out, chain_sem)]
    worker = work[0](gathers, square_parts, nz, z, (r, across_x, across_y, 3 - r), work_in, work_out, work_scr) if work else None

    def begin_chain():
        for i, part in zip(chain, chained):
            exchanges[i].arrive()
            part.begin()

    line_parts = gathers + scatters
    for part in gathers + exchanges:
        part.begin()
    early = []
    if worker and worker.early:
        early = [part for part in square_parts if not part.factors]
        for part in early:
            part.begin()
        worker.begin()
    late = [part for part in square_parts if part not in early]
    for part in late:
        part.begin()
    for part in early:
        part.mid()
    if chain and worker:
        begin_chain()
    for part in scatters:
        part.begin()
    if worker and not worker.early:
        worker.begin()
    if line_parts:
        if chain_at == 0 and not worker:
            begin_chain()
        for s in range(1, nz):
            @pl.loop(0, parts)
            def _(j):
                for part in line_parts:
                    part.step(s, j)

            for part in exchanges + scatters:
                part.after_step(s)
            if s == chain_at:
                begin_chain()
            if s == max(1, chain_at):
                for part in late:
                    part.mid()
            if worker:
                worker.after_step(s)
    else:
        begin_chain()
        for part in late:
            part.mid()
    for part in line_parts:
        part.end()
    for part in chained:
        part.mid()
    for part in exchanges + square_parts + chained:
        part.end()


class Backward:
    early = True

    def __init__(self, gathers, spreads, nz, z, blocks, ins, outs, scratch):
        self.ga, self.w_out, self.rot, self.cosine, self.sine, self.piece = ins
        (self.out,) = outs
        self.go, self.gk, self.gv = scratch

    def begin(self):
        length, width = self.rot.shape
        heads, blocks = width // 3 // HEAD_DIM, length // PIECE
        rot, out, cosine, sine, gk, gv = self.rot, self.out, self.cosine, self.sine, self.gk, self.gv
        inv_root = 1.0 / math.sqrt(HEAD_DIM)

        @pl.loop(0, blocks)
        def _(i):
            rows = pl.ds(pl.multiple_of(i * PIECE, PIECE), PIECE)
            self.go[rows, :] = dot_t(self.ga[rows, :], self.w_out[...]).astype(bf16)

        @pl.loop(0, heads)
        def _(h):
            at = lambda part: pl.ds(pl.multiple_of((part * heads + h) * HEAD_DIM, HEAD_DIM), HEAD_DIM)
            gk[...] = jnp.zeros_like(gk)
            gv[...] = jnp.zeros_like(gv)
            for i in range(blocks):
                keys = (i + 1) * PIECE
                own = pl.ds(i * PIECE, PIECE)
                q, g = rot[own, at(0)], self.go[own, at(0)]
                sg, visible = squash(q, rot[0:keys, at(1)], self.piece[own, :], keys, length)
                p = masked(sg, visible, keys).astype(bf16)
                gs = masked(dot_t(g, rot[0:keys, at(2)]) * sg * (1.0 - sg), visible, keys).astype(bf16)
                gq = dot(gs, rot[0:keys, at(1)]) * inv_root
                out[own, at(0)] = rotate(gq, cosine[own, :], -sine[own, :]).astype(bf16)
                gk[0:keys, :] += t_dot(gs, q)
                gv[0:keys, :] += t_dot(p, g)

            @pl.loop(0, blocks)
            def _(i):
                rows = pl.ds(pl.multiple_of(i * PIECE, PIECE), PIECE)
                out[rows, at(1)] = rotate(gk[rows, :] * inv_root, cosine[rows, :], -sine[rows, :]).astype(bf16)
                out[rows, at(2)] = gv[rows, :].astype(bf16)

    def after_step(self, s):
        pass


class Forward:
    early = False

    def __init__(self, gathers, spreads, nz, z, blocks, ins, outs, scratch):
        (gather,) = gathers
        self.gather, self.spreads, self.nz, self.z, self.blocks = gather, spreads, nz, z, blocks
        self.cot, self.w_down = ins[:2]
        self.hid, self.ggu = outs
        self.ghid = scratch[0]
        if spreads:
            self.w, self.sem = scratch[1:]
        else:
            self.w = ins[2:]
        self.rows = 2 * gather.x.shape[0]
        self.tile = min(256, self.hid.shape[1])

    def load(self, i, k):
        q = self.blocks[k]
        return pltpu.make_async_copy(self.spreads[i].out.at[q], self.w.at[i, q], self.sem.at[i, k])

    def each_tile(self, put):
        @pl.loop(0, self.hid.shape[1] // self.tile)
        def _(t):
            put(pl.multiple_of(t * self.tile, self.tile))

    def begin(self):
        if self.spreads:
            for i in (0, 1):
                for k in (0, 1, 2):
                    self.load(i, k).start()

        @pl.loop(0, self.nz)
        def _(b):
            rows = pl.ds(pl.multiple_of(b * self.rows, self.rows), self.rows)

            def put(first):
                cols = pl.ds(first, self.tile)
                self.ghid[rows, cols] = dot_t(self.cot[rows, :], self.w_down[cols, :])

            self.each_tile(put)

    def weights(self):
        if self.spreads:
            for i in (0, 1):
                self.spreads[i].arrive()
                self.load(i, 3).start()
            for i in (0, 1):
                for k in range(4):
                    self.load(i, k).wait()

    def chip(self, d):
        width = self.hid.shape[1]
        rows = pl.ds(pl.multiple_of(d * self.rows, self.rows), self.rows)

        def put(first):
            cols = pl.ds(first, self.tile)
            x = self.gather.out[pl.ds(2 * d, 2)].reshape(self.rows, -1)
            if self.spreads:
                gate, up = [dot(x, self.w[i, :, :, :, cols].reshape(x.shape[1], self.tile)) for i in (0, 1)]
            else:
                gate, up = [dot(x, w[:, cols]) for w in self.w]
            ghid = self.ghid[rows, cols]
            s = 1.0 / (1.0 + jnp.exp(-gate))
            silu = gate * s
            self.hid[rows, cols] = (silu * up).astype(bf16)
            self.ggu[rows, cols] = (ghid * up * s * (1.0 + gate * (1.0 - s))).astype(bf16)
            self.ggu[rows, pl.ds(width + first, self.tile)] = (ghid * silu).astype(bf16)

        self.each_tile(put)

    def away(self, s):
        self.gather.arrive(s)

        @pl.when(self.z >= s)
        def _():
            self.chip(self.z - s)

        if s > 0:
            @pl.when(self.z + s < self.nz)
            def _():
                self.chip(self.z + s)

    def after_step(self, s):
        last = max(1, self.nz - 2)
        if s == last:
            self.weights()
            for k in range(last):
                self.away(k)
        if s == self.nz - 1:
            for k in range(last, self.nz):
                self.away(k)


class Later:
    early = False

    def __init__(self, gathers, spreads, nz, z, blocks, ins, outs, scratch):
        (self.x, self.w), (self.out,) = ins, outs
        self.steps, self.tile = nz - 1, min(512, self.out.shape[1])

    def begin(self):
        pass

    def after_step(self, s):
        tiles = self.out.shape[1] // self.tile

        @pl.loop(tiles * (s - 1) // self.steps, tiles * s // self.steps)
        def _(t):
            cols = pl.ds(pl.multiple_of(t * self.tile, self.tile), self.tile)
            self.out[:, cols] = t_dot(self.x[...], self.w[:, cols]).astype(bf16)


def line_comm(cid, name, us, ag=(), rs=(), a2a=(), spread=(), sums=(), chain=(), chain_at=None, work=None, owners=False, parts=2):
    n = lax.axis_size("inner")
    nz = n // 2
    chain_at = nz - 2 if chain_at is None else chain_at
    dma = pltpu.SemaphoreType.DMA
    hbm = pl.BlockSpec(memory_space=pl.ANY)
    vmem = pl.BlockSpec(memory_space=pltpu.VMEM)
    products = [tuple(t[2:] + (t[0] is None,) for t in p) if isinstance(p, list) else () for p in rs]
    rs_out = [
        (p[0][0].shape[0] // n if p[0][0] is not None else work[2][0][0] // n, p[0][1].shape[0 if p[0][2] else 1]) if isinstance(p, list) else (p.shape[0] // n, p.shape[1])
        for p in rs
    ]
    rs_in = []
    for p, shape in zip(rs, rs_out):
        rs_in += [a for t in p for a in t[:2] if a is not None] if isinstance(p, list) else [p.reshape((n,) + shape)]
    sum_shapes = [(p[0].shape[1] // 4, p[2]) if isinstance(p, tuple) else (p.shape[0] // 4, p.shape[1]) for p in sums]
    sum_kinds = [(3 if p[1] is None else 2) if isinstance(p, tuple) else 1 for p in sums]
    sums = [p[:2] if isinstance(p, tuple) else (p.reshape((4,) + shape),) for p, shape in zip(sums, sum_shapes)]
    work_in, work_out, work_scratch = work[1:] if work else ((), (), [])
    inputs, in_specs, out_shape, out_specs, scratch = [], [], [], [], []

    def give(arrays, space):
        inputs.extend(arrays)
        in_specs.extend([space] * len(arrays))

    def get(shape, dtype, space):
        out_shape.append(jax.ShapeDtypeStruct(shape, dtype))
        out_specs.append(space)

    near = vmem if work else hbm
    give(ag, hbm)
    give(rs_in, vmem)
    give([w for t in a2a for w in t[0]], hbm)
    aliases = {len(inputs) + i: len(ag) + len(rs) + len(a2a) + i for i, (_, ph) in enumerate(spread) if 1 not in ph}
    give([b for b, _ in spread], hbm)
    give([x for p in sums for x in p if x is not None], vmem)
    give(work_in, vmem)
    for x in ag:
        get((n,) + x.shape, x.dtype, near)
        scratch += [dma, dma((nz, parts)), dma((nz + 1, parts)), dma((nz, parts)), dma((nz + 1, parts))]
        scratch += [dma((2, nz, parts)), dma((2, nz, parts))]
    for shape, flips in zip(rs_out, products):
        get(shape, f32, vmem)
        scratch += [pltpu.VMEM((n,) + shape, bf16)] if flips else []
        scratch += [pltpu.VMEM((nz,) + shape, bf16)] * 3 + [dma((nz, parts))] * 6
    for t in a2a:
        get(t[1], t[0][0].dtype, hbm)
        scratch += [dma((t[4],)), dma((n, t[4])), dma((n, t[4]))]
    for b, phases in spread:
        get(b.shape if 1 not in phases else (4,) + b.shape, b.dtype, hbm)
        scratch += [pltpu.VMEM(b.shape, b.dtype)] if 1 in phases else []
        scratch += [dma((2,)), dma((2,)), dma((2,)), dma((2,)), dma((2,))]
    for p, shape in zip(sums, sum_shapes):
        get(shape, bf16, vmem)
        half = (shape[0] // 2, shape[1])
        scratch += [pltpu.VMEM((4,) + shape, bf16)] if len(p) > 1 else []
        scratch += [pltpu.VMEM((2, 2) + half, bf16), pltpu.VMEM((2,) + half, bf16)]
        scratch += [dma((2, 2)), dma((2, 2)), dma((2,)), dma((2,))]
    for i in chain:
        get((4,) + a2a[i][1], a2a[i][0][0].dtype, hbm)
        scratch += [pltpu.VMEM(a2a[i][1], a2a[i][0][0].dtype), dma((2,)), dma((2,)), dma((2,)), dma((2,)), dma((2,))]
    for shape in work_out:
        get(shape, bf16, vmem)
    scratch += work_scratch
    outs = pl.pallas_call(
        functools.partial(
            line_body,
            n,
            len(ag),
            products,
            [(len(t[0]),) + t[2:6] for t in a2a],
            [ph for _, ph in spread],
            sum_kinds,
            chain,
            chain_at,
            (work[0], len(work_in), len(work_out), len(work_scratch)) if work else None,
            owners,
            parts,
        ),
        out_shape=out_shape,
        in_specs=in_specs,
        out_specs=out_specs,
        input_output_aliases=aliases,
        scratch_shapes=scratch,
        compiler_params=pltpu.CompilerParams(
            collective_id=cid, has_side_effects=True, vmem_limit_bytes=62 * 2**20
        ),
        cost_estimate=pl.CostEstimate(flops=us * 1150000000, bytes_accessed=us * 3600000, transcendentals=0),
        name=name,
    )(*inputs)
    return [o.reshape((-1,) + o.shape[2:]) if i < len(ag) else o for i, o in enumerate(outs)]


def rotate(flat, cosine, sine):
    return flat * cosine + pltpu.roll(flat, HEAD_DIM // 2, 1) * sine


def squash(q, k, piece, keys, length):
    scale = -math.log2(math.e) / math.sqrt(HEAD_DIM)
    sg = 1.0 / (1.0 + jnp.exp2(dot_t(q, k) * scale + math.log2(length)))
    row = lax.broadcasted_iota(jnp.int32, (PIECE, PIECE), 0)
    col = lax.broadcasted_iota(jnp.int32, (PIECE, PIECE), 1)
    return sg, (col <= row) | (piece >= 0)


def masked(value, visible, keys):
    last = jnp.where(visible, value[:, keys - PIECE :], 0.0)
    return last if keys == PIECE else jnp.concatenate([value[:, : keys - PIECE], last], axis=1)


def attn_body(heads, length, lin, cosine, sine, piece, out, rot):
    h, b = pl.program_id(0), pl.program_id(1)
    at = lambda part: pl.ds(pl.multiple_of((part * heads + h) * HEAD_DIM, HEAD_DIM), HEAD_DIM)
    blocks = length // PIECE

    @pl.when(b == 0)
    def _():
        @pl.loop(0, blocks)
        def _(i):
            rows = pl.ds(pl.multiple_of(i * PIECE, PIECE), PIECE)
            for part in (0, 1):
                rot[rows, at(part)] = rotate(lin[rows, at(part)], cosine[rows, :], sine[rows, :]).astype(bf16)
            rot[rows, at(2)] = lin[rows, at(2)].astype(bf16)

    for i in range(blocks):
        @pl.when(b == i)
        def _():
            keys = (i + 1) * PIECE
            own = pl.ds(i * PIECE, PIECE)
            sg, visible = squash(rot[own, at(0)], rot[0:keys, at(1)], piece[...], keys, length)
            out[...] = dot(masked(sg, visible, keys).astype(bf16), rot[0:keys, at(2)]).astype(bf16)


def attention(lin, cosine, sine, piece):
    length, width = lin.shape
    heads = width // 3 // HEAD_DIM
    whole = lambda x: pl.BlockSpec(x.shape, lambda h, b: (0, 0))
    return pl.pallas_call(
        functools.partial(attn_body, heads, length),
        grid=(heads, length // PIECE),
        out_shape=[
            jax.ShapeDtypeStruct((length, width // 3), bf16),
            jax.ShapeDtypeStruct((length, width), bf16),
        ],
        in_specs=[whole(lin), whole(cosine), whole(sine), pl.BlockSpec((PIECE, 1), lambda h, b: (b, 0))],
        out_specs=[
            pl.BlockSpec((PIECE, HEAD_DIM), lambda h, b: (b, h)),
            pl.BlockSpec((length, width), lambda h, b: (0, 0)),
        ],
        compiler_params=pltpu.CompilerParams(vmem_limit_bytes=48 * 2**20),
        cost_estimate=pl.CostEstimate(
            flops=4 * heads * length * length * HEAD_DIM // 2, bytes_accessed=8 * length * width, transcendentals=heads * length * length
        ),
        name="attention",
    )(lin, cosine, sine, piece)


def columns_out(w):
    n, nr = lax.axis_size("inner"), lax.axis_size("replica")
    part = w.shape[0] // nr
    cols = w.shape[1] // n

    def source(refs, other, m):
        rows = pl.ds(pl.multiple_of(lax.axis_index("replica") * part, part), part)
        return refs[0].at[rows, pl.ds(pl.multiple_of(other * cols, cols), cols)]

    return ((w,), (n, part, cols), source, lambda ref, other, m: ref.at[other], 1, False)


def to_all(block):
    n = lax.axis_size("inner")
    return ((block,), (n,) + block.shape, lambda refs, other, m: refs[0], lambda ref, other, m: ref.at[other], 1, False)


def rows_back(share, first, count, late=False):
    n, part, _ = share.shape
    cols = first[1]

    def source(refs, other, m):
        return refs[0].at[other, :, pl.ds((first[0] + m) * cols, cols)]

    def target(ref, other, m):
        return ref.at[pl.ds(m * part, part), pl.ds(pl.multiple_of(other * cols, cols), cols)]

    return ((share,), (count * part, n * cols), source, target, count, late)


def sum_blocks(g):
    n = lax.axis_size("inner")
    cols = g.shape[1]
    return ((g,), (n,) + (g.shape[0] // n, cols), lambda refs, other, m: refs[0].at[pl.ds(pl.multiple_of(other * 16, 16), 16)], lambda ref, other, m: ref.at[other], 1, False)


def shares_first(x):
    n, nr = lax.axis_size("inner"), lax.axis_size("replica")
    part = x.shape[1] // n // nr
    return x.reshape(x.shape[0], n, nr, part).transpose(0, 2, 1, 3).reshape(x.shape)


def owners_first(x):
    n, nr = lax.axis_size("inner"), lax.axis_size("replica")
    part = x.shape[1] // n // nr
    return x.reshape(x.shape[0], nr, n, part).transpose(0, 2, 1, 3).reshape(x.shape)


def sum_share(product):
    return lax.psum_scatter(product.astype(bf16), "replica", scatter_dimension=0, tiled=True)


def join(block):
    return lax.all_gather(block, "replica", axis=0, tiled=False)


def flat(w):
    return w.reshape(-1, w.shape[-1])


def local(
    tokens,
    w_query,
    w_key,
    w_value,
    w_out,
    w_gate,
    w_up,
    w_down,
    gain_attn,
    gain_ffn,
    pieces,
    positions,
    cotangent,
):
    n = lax.axis_size("inner")
    nr = lax.axis_size("replica")
    square = nr == 4
    own, width = tokens.shape
    length = own * n
    rows = gain_attn.shape[0]
    after = lax.optimization_barrier

    marks = jnp.zeros((8, own), jnp.int32).at[0].set(pieces).at[1].set(positions)
    gains = jnp.zeros((8, rows), f32).at[0].set(gain_attn.astype(f32)).at[1].set(gain_ffn.astype(f32))
    q_share, k_share, v_share, marks, gains = line_comm(
        0,
        "load_attn", 25,
        a2a=[columns_out(w_query), columns_out(w_key), columns_out(w_value), to_all(marks), to_all(gains)],
    )
    qkv_share = jnp.concatenate([q_share, k_share, v_share], axis=2)
    loads = [columns_out(w_gate), columns_out(w_up)]
    if square:
        x, g_share, u_share, w_qkv = line_comm(
            1, "load_ffn", 80, ag=[shares_first(tokens)], a2a=loads, spread=[(qkv_share, (1, 2))]
        )
    else:
        w_qkv = join(qkv_share)
        x, g_share, u_share = line_comm(1, "load_ffn", 80, ag=[shares_first(tokens)], a2a=loads)
    w_qkv = flat(w_qkv)
    cot, x = after((cotangent, x))
    cot = lax.all_gather(cot, "inner", axis=0, tiled=True)
    pieces, positions = marks[:, 0].reshape(length, 1), marks[:, 1].reshape(length)
    attn_gain, ffn_gain = gains[:, 0].reshape(1, -1), gains[:, 1].reshape(1, -1)

    x = x.astype(f32)
    cosine, sine = rope_tables(positions)
    u1 = x * rms_scale(x)
    n1 = (u1 * shares_first(attn_gain)).astype(bf16)
    o, rot = attention(dot(n1, w_qkv), cosine, sine, pieces)
    if square:
        a, w_g, w_u = line_comm(2, "attn_out", 50, rs=[[(o, w_out, False, 0)]], spread=[(g_share, (1,)), (u_share, (1,))])
    else:
        w_g, w_u = join(g_share), join(u_share)
        (a,) = line_comm(2, "attn_out", 50, rs=[[(o, w_out, False, 0)]])
    mid = tokens.astype(f32) + a
    r2 = rms_scale(mid)
    u2 = mid * r2
    n2 = shares_first((u2 * ffn_gain).astype(bf16))
    ffn = w_down.shape[0]
    results = [(length, ffn), (length, 2 * ffn)]
    held = [pltpu.VMEM((length, ffn), f32)]
    if square:
        held += [pltpu.VMEM((2,) + w_g.shape, bf16), pltpu.SemaphoreType.DMA((2, 4))]
        n2, w_g, w_u, hid, ggu = line_comm(
            3,
            "ffn_forward",
            60,
            ag=[n2],
            spread=[(w_g, (2,)), (w_u, (2,))],
            work=(Forward, [cot, w_down], results, held),
        )
        w_g, w_u = flat(w_g), flat(w_u)
    else:
        w_g, w_u = flat(w_g), flat(w_u)
        n2, hid, ggu = line_comm(3, "ffn_forward", 60, ag=[n2], work=(Forward, [cot, w_down, w_g, w_u], results, held))

    gu = t_dot(n2, ggu).astype(bf16)
    gu, ggu = after((gu, ggu))
    gu_share = sum_share(gu)
    tidy = square and width // n // nr == 64
    gn2, g_down = line_comm(4, "scatter_gn2", 44, owners=tidy, work=(Later, [hid, cot], [w_down.shape], []), rs=[[(ggu, w_g, True, 0), (ggu, w_u, True, w_g.shape[1])]])
    gn2 = gn2 if tidy else owners_first(gn2)
    gu2 = gn2 * ffn_gain
    ffn_gain_part = jnp.sum(gn2 * u2, axis=0)
    gmid = cotangent.astype(f32) + r2 * (gu2 - u2 * jnp.mean(gu2 * u2, axis=1, keepdims=True))
    (ga,) = line_comm(5, "gather_ga", 40, ag=[gmid.astype(bf16)])
    ga, gu_share, g_down = after((ga, gu_share, g_down))
    grad_down = lax.psum(g_down, "replica")

    cols = w_gate.shape[1] // n
    heads_width = rot.shape[1] // 3
    gu_share = gu_share.reshape(n, -1, 2 * cols)
    own_x = tokens.astype(f32)
    r1 = rms_scale(own_x)
    u1 = own_x * r1

    def gain_parts(gn1):
        both = jnp.stack([jnp.sum(gn1 * u1, axis=0).reshape(n, rows), ffn_gain_part.reshape(n, rows)], axis=1)
        return sum_blocks(jnp.pad(both, ((0, 0), (0, 14), (0, 0))).reshape(n * 16, rows))

    held = [pltpu.VMEM((length, heads_width), bf16)] + [pltpu.VMEM((length, HEAD_DIM), f32)] * 2
    work = (Backward, [ga, w_out, rot, cosine, sine, pieces], [rot.shape], held)
    gn1_part = [(None, w_qkv, True, 0)]
    if square:
        gn1, gate_rows, up_rows, out_share, qkv_share, grad_gate, _ = line_comm(
            6,
            "scatter_gn1",
            1,
            owners=tidy,
            rs=[gn1_part],
            a2a=[rows_back(gu_share, (0, cols), 1), rows_back(gu_share, (1, cols), 1, False)],
            sums=[(o, ga, width), (n1, None, rot.shape[1])],
            chain=(0,),
            chain_at=0,
            work=work,
        )
        gn1 = gn1 if tidy else owners_first(gn1)
        qkv_back = rows_back(qkv_share.reshape(n, -1, 3 * heads_width), (0, heads_width), 3)
        up_rows, grad_down = after((up_rows, grad_down))
        mlp, _, _, grad_up, grad_out, grad_qkv, gains = line_comm(
            7,
            "rows_attn",
            70,
            rs=[[(hid, w_down, False, 0)]],
            a2a=[qkv_back, gain_parts(gn1)],
            spread=[(up_rows, (1, 2)), (out_share, (1, 2))],
            chain=(0, 1),
            chain_at=0,
        )
        gains = jnp.sum(gains, axis=(0, 1))
    else:
        gu_back = rows_back(gu_share, (0, cols), 2)
        gn1, gu_rows, gqkv = line_comm(6, "scatter_gn1", 80, rs=[gn1_part], a2a=[gu_back], work=work)
        gn1 = owners_first(gn1)
        g_qkv = sum_share(t_dot(n1, gqkv))
        qkv_back = rows_back(g_qkv.reshape(n, -1, 3 * heads_width), (0, heads_width), 3)
        mlp, qkv_rows, gains = line_comm(
            7, "rows_attn", 75, rs=[[(hid, w_down, False, 0)]], a2a=[qkv_back, gain_parts(gn1)]
        )
        gains = lax.psum(jnp.sum(gains, axis=0), "replica")
        grad_gu = join(gu_rows).reshape(nr, 2, -1, n * cols)
        grad_gate, grad_up, grad_out, grad_qkv = grad_gu[:, 0], grad_gu[:, 1], join(sum_share(t_dot(o, ga))), join(qkv_rows)
    output = (mid + mlp).astype(bf16)
    grad_qkv = grad_qkv.reshape(nr, 3, -1, width).astype(f32)

    gu1 = gn1 * attn_gain
    grad_tokens = gmid + r1 * (gu1 - u1 * jnp.mean(gu1 * u1, axis=1, keepdims=True))
    return (
        output,
        grad_tokens,
        grad_qkv[:, 0].reshape(w_query.shape),
        grad_qkv[:, 1].reshape(w_key.shape),
        grad_qkv[:, 2].reshape(w_value.shape),
        grad_out.reshape(w_out.shape).astype(f32),
        grad_gate.reshape(w_gate.shape).astype(f32),
        grad_up.reshape(w_up.shape).astype(f32),
        grad_down.reshape(w_down.shape).astype(f32),
        gains[0],
        gains[1],
    )


def solution(mesh):
    tok = P(("replica", "inner"), None)
    row = P("inner", None)
    vec = P("inner")
    mark = P(("replica", "inner"))
    return jax.shard_map(
        local,
        mesh=mesh,
        in_specs=(tok, row, row, row, row, row, row, row, vec, vec, mark, mark, tok),
        out_specs=(tok, tok, row, row, row, row, row, row, row, vec, vec),
        check_vma=False,
    )
```

```python
import functools
import math

import jax
import jax.numpy as jnp
from jax import lax
from jax.experimental import pallas as pl
from jax.experimental.pallas import tpu as pltpu
from jax.sharding import PartitionSpec as P

HEAD_DIM = 128
PIECE = 256
epsilon = 1e-06
rope_base = 10000.0
dims_rows = (((1,), (1,)), ((), ()))
dims_cols = (((0,), (0,)), ((), ()))
f32 = jnp.float32
bf16 = jnp.bfloat16


def dot(a, b):
    return jnp.dot(a, b, preferred_element_type=f32)


def dot_t(a, b):
    return lax.dot_general(a, b, dims_rows, preferred_element_type=f32)


def t_dot(a, b):
    return lax.dot_general(a, b, dims_cols, preferred_element_type=f32)


def rope_tables(positions):
    half_dim = HEAD_DIM // 2
    frequency = rope_base ** (-jnp.arange(half_dim, dtype=f32) * 2.0 / HEAD_DIM)
    angle = positions.astype(f32)[:, None] * frequency[None, :]
    cosine, sine = jnp.cos(angle), jnp.sin(angle)
    return jnp.concatenate([cosine, cosine], axis=1), jnp.concatenate([-sine, sine], axis=1)


def rms_scale(values):
    return lax.rsqrt(jnp.mean(values * values, axis=1, keepdims=True) + epsilon)


def rcopy(src, dst, ssem, rsem, to, axis="inner"):
    return pltpu.make_async_remote_copy(
        src_ref=src,
        dst_ref=dst,
        send_sem=ssem,
        recv_sem=rsem,
        device_id={axis: to},
        device_id_type=pl.DeviceIdType.MESH,
    )


def signal(sem, to, axis="inner"):
    pl.semaphore_signal(sem, inc=1, device_id={axis: to}, device_id_type=pl.DeviceIdType.MESH)


def line_body(n, n_ag, products, a2a_blocks, spreads, sum_kinds, chain, chain_at, work, owners, parts, *refs):
    refs = list(refs)
    nz = n // 2
    n_a2a = len(a2a_blocks)
    take = lambda count: [refs.pop(0) for _ in range(count)]
    n_sp, n_rs, n_sum = len(spreads), len(products), len(sum_kinds)
    ag_in, rs_in, a2a_in = take(n_ag), [take(sum(2 - made for _, _, made in t) or 1) for t in products], [take(t[0]) for t in a2a_blocks]
    sp_in, sum_in = take(n_sp), [take(2 if k == 2 else 1) for k in sum_kinds]
    work_in = take(work[1]) if work else []
    ag_out, rs_out, a2a_out, sp_out, sum_out = take(n_ag), take(n_rs), take(n_a2a), take(n_sp), take(n_sum)
    chain_out = take(len(chain))
    work_out = take(work[2]) if work else []
    ag_sem = [take(7) for _ in range(n_ag)]
    rs_scr = [take(10 if t else 9) for t in products]
    a2a_sem = [take(3) for _ in range(n_a2a)]
    sp_sem = [take(5 + (1 in ph)) for ph in spreads]
    sum_scr = [take(6 if k == 1 else 7) for k in sum_kinds]
    chain_sem = [take(6) for _ in chain]
    work_scr = take(work[3]) if work else []
    me = lax.axis_index("inner")
    z, c = me // 2, lax.rem(me, 2)
    sib = me + 1 - 2 * c
    r = lax.axis_index("replica")
    across_x, across_y = r + 1 - 2 * lax.rem(r, 2), r + 2 - 4 * (r // 2)
    barrier = pltpu.get_barrier_semaphore()
    more = 0
    if n_sp + n_sum + len(chain):
        signal(barrier, across_x, "replica")
        signal(barrier, across_y, "replica")
        more = 2
    if n_a2a:
        for k in range(1, n):
            signal(barrier, lax.rem(me + k, n))
        pl.semaphore_wait(barrier, n - 1 + more)
    else:
        signal(barrier, sib)

        @pl.when(z + 1 < nz)
        def _():
            signal(barrier, me + 2)

        @pl.when(z > 0)
        def _():
            signal(barrier, me - 2)

        pl.semaphore_wait(barrier, 1 + more + (z + nz - 1) // nz + (2 * nz - 2 - z) // nz)

    def rows_of(ref, j):
        count = ref.shape[0] // parts
        return pl.ds(pl.multiple_of(j * count, count), count)

    class Gather:
        def __init__(self, x, out, sems):
            self.x, self.out, self.here = x, out, set()
            self.own_sem, self.rs, self.rr, self.ls, self.lr, self.ss, self.sr = sems

        def own(self):
            return pltpu.make_async_copy(self.x, self.out.at[me], self.own_sem)

        def piece(self, block, s, j):
            rows = rows_of(self.x, j)
            return self.x.at[rows] if s == 0 else self.out.at[block, rows]

        def right(self, s, j):
            b = me - 2 * s
            dst = self.out.at[b, rows_of(self.x, j)]
            return rcopy(self.piece(b, s, j), dst, self.rs.at[s, j], self.rr.at[s + 1, j], me + 2)

        def left(self, s, j):
            b = me + 2 * s
            dst = self.out.at[b, rows_of(self.x, j)]
            return rcopy(self.piece(b, s, j), dst, self.ls.at[s, j], self.lr.at[s + 1, j], me - 2)

        def side(self, s, k, j):
            b = me - 2 * s if k == 0 else me + 2 * s
            dst = self.out.at[b, rows_of(self.x, j)]
            return rcopy(self.piece(b, s, j), dst, self.ss.at[k, s, j], self.sr.at[k, s, j], sib)

        def from_left(self, s, j):
            dst = self.out.at[me - 2 * s, rows_of(self.x, j)]
            return rcopy(dst, dst, self.rs.at[s, j], self.rr.at[s, j], me - 2)

        def from_right(self, s, j):
            dst = self.out.at[me + 2 * s, rows_of(self.x, j)]
            return rcopy(dst, dst, self.ls.at[s, j], self.lr.at[s, j], me + 2)

        def from_side(self, s, k, j):
            b = sib - 2 * s if k == 0 else sib + 2 * s
            dst = self.out.at[b, rows_of(self.x, j)]
            return rcopy(dst, dst, self.ss.at[k, s, j], self.sr.at[k, s, j], sib)

        def begin(self):
            @pl.loop(0, parts)
            def _(j):
                @pl.when(z + 1 < nz)
                def _():
                    self.right(0, j).start()

                @pl.when(z > 0)
                def _():
                    self.left(0, j).start()

            self.own().start()

            @pl.loop(0, parts)
            def _(j):
                self.side(0, 0, j).start()

        def step(self, s, j):
            @pl.when(z >= s)
            def _():
                self.from_left(s, j).wait_recv()

                @pl.when(z + 1 < nz)
                def _():
                    self.right(s, j).start()

                self.side(s, 0, j).start()

            @pl.when(z + s < nz)
            def _():
                self.from_right(s, j).wait_recv()

                @pl.when(z > 0)
                def _():
                    self.left(s, j).start()

                self.side(s, 1, j).start()

        def arrive(self, s):
            self.here.add(s)
            if s == 0:
                self.own().wait()

            @pl.loop(0, parts)
            def _(j):
                @pl.when(z >= s)
                def _():
                    self.from_side(s, 0, j).wait_recv()

                if s > 0:
                    @pl.when(z + s < nz)
                    def _():
                        self.from_side(s, 1, j).wait_recv()

        def end(self):
            for s in range(nz):
                if s not in self.here:
                    self.arrive(s)

                @pl.loop(0, parts)
                def _(j):
                    @pl.when(z >= s)
                    def _():
                        @pl.when(z + 1 < nz)
                        def _():
                            self.right(s, j).wait_send()

                        self.side(s, 0, j).wait_send()

                    @pl.when(z + s < nz)
                    def _():
                        @pl.when(z > 0)
                        def _():
                            self.left(s, j).wait_send()

                        if s > 0:
                            self.side(s, 1, j).wait_send()

    class Scatter:
        def __init__(self, operands, flips, out, scratch):
            self.pairs, self.out = [(x, w) + t[:2] for x, w, t in zip(operands[::2], operands[1::2], flips)], out
            self.p, *scratch = scratch if flips else operands + scratch
            self.sib_buf, self.l_buf, self.r_buf, self.ss, self.sr, self.rs, self.rr, self.ls, self.lr = scratch
            self.count = out.shape[0] // parts

        def side(self, d, j):
            rows = rows_of(self.out, j)
            return rcopy(self.p.at[2 * d + 1 - c, rows], self.sib_buf.at[d, rows], self.ss.at[d, j], self.sr.at[d, j], sib)

        def right(self, d, j, to=2):
            rows = rows_of(self.out, j)
            return rcopy(self.l_buf.at[d, rows], self.l_buf.at[d, rows], self.rs.at[d, j], self.rr.at[d, j], me + to)

        def left(self, d, j, to=-2):
            rows = rows_of(self.out, j)
            return rcopy(self.r_buf.at[d, rows], self.r_buf.at[d, rows], self.ls.at[d, j], self.lr.at[d, j], me + to)

        def product(self, d):
            own, width = self.out.shape
            rows = pl.ds(d * 2 * own, 2 * own)
            tile = min(512, width)

            @pl.loop(0, width // tile)
            def _(t):
                cols = pl.ds(pl.multiple_of(t * tile, tile), tile)
                total = 0.0
                for x, w, flip, first in self.pairs:
                    x = x[rows, first : first + w.shape[1 if flip else 0]]
                    total += dot_t(x, w[cols, :]) if flip else dot(x, w[:, cols])
                total = total.astype(bf16)
                self.p[2 * d, :, cols] = total[:own]
                self.p[2 * d + 1, :, cols] = total[own:]

        def begin(self):
            for s in range(1 if self.pairs else nz // 2):
                self.offer(s)

        def offer(self, s):
            for d in (nz - 1 - s, s):
                if self.pairs:
                    self.product(d)

                @pl.loop(0, parts)
                def _(j):
                    self.side(d, j).start()

        def after_step(self, s):
            if self.pairs and s < nz // 2:
                self.offer(s)

        def pair(self, d, rows):
            return self.p[2 * d + c, rows, :].astype(f32) + self.sib_buf[d, rows, :].astype(f32)

        def step(self, s, j):
            tick = (s - 1) * parts + j
            k = tick - z

            @pl.when((k >= 0) & (k < (nz - 1 - z) * parts))
            def _():
                d, i = nz - 1 - k // parts, lax.rem(k, parts)
                rows = rows_of(self.out, i)
                self.side(d, i).wait_recv()

                @pl.when(z > 0)
                def _():
                    self.right(d, i, -2).wait_recv()
                    self.l_buf[d, rows, :] = (self.pair(d, rows) + self.l_buf[d, rows, :].astype(f32)).astype(bf16)

                @pl.when(z == 0)
                def _():
                    self.l_buf[d, rows, :] = self.pair(d, rows).astype(bf16)

                self.right(d, i).start()

            m = tick - (nz - 1 - z)

            @pl.when((m >= 0) & (m < z * parts))
            def _():
                d, i = m // parts, lax.rem(m, parts)
                rows = rows_of(self.out, i)
                self.side(d, i).wait_recv()

                @pl.when(z + 1 < nz)
                def _():
                    self.left(d, i, 2).wait_recv()
                    self.r_buf[d, rows, :] = (self.pair(d, rows) + self.r_buf[d, rows, :].astype(f32)).astype(bf16)

                @pl.when(z + 1 == nz)
                def _():
                    self.r_buf[d, rows, :] = self.pair(d, rows).astype(bf16)

                self.left(d, i).start()

        def owners_first(self, rows):
            tiles = [self.out[rows, k * 128 : (k + 1) * 128] for k in range(self.out.shape[1] // 128)]
            low = lax.broadcasted_iota(jnp.int32, tiles[0].shape, 1) < 64
            for k in range(len(tiles)):
                i = k // 2
                first = 2 * (k % 2) * n + i
                a, b = tiles[first // 2], tiles[(first + n) // 2]
                new = jnp.where(low, pltpu.roll(a, 64, 1), b) if i % 2 else jnp.where(low, a, pltpu.roll(b, 64, 1))
                self.out[rows, k * 128 : (k + 1) * 128] = new

        def end(self):
            @pl.loop(0, parts)
            def _(j):
                rows = rows_of(self.out, j)
                self.side(z, j).wait_recv()
                self.out[rows, :] = self.pair(z, rows)

                @pl.when(z > 0)
                def _():
                    self.right(z, j, -2).wait_recv()
                    self.out[rows, :] = self.out[rows, :] + self.l_buf[z, rows, :].astype(f32)

                @pl.when(z + 1 < nz)
                def _():
                    self.left(z, j, 2).wait_recv()
                    self.out[rows, :] = self.out[rows, :] + self.r_buf[z, rows, :].astype(f32)

                if owners:
                    self.owners_first(rows)

            for d in range(nz):
                @pl.loop(0, parts)
                def _(j):
                    self.side(d, j).wait_send()

                    @pl.when(d > z)
                    def _():
                        self.right(d, j).wait_send()

                    @pl.when(d < z)
                    def _():
                        self.left(d, j).wait_send()

    class Exchange:
        def __init__(self, src, dst, sems, blocks):
            self.src, self.dst = src, dst
            self.own_sem, self.sent, self.recv = sems
            _, self.src_of, self.dst_of, self.count, self.late = blocks
            self.arrived = False

        def to(self, k, m):
            other = lax.rem(me + k, n)
            return rcopy(
                self.src_of(self.src, other, m), self.dst_of(self.dst, me, m), self.sent.at[k, m], self.recv.at[k, m], other
            )

        def came(self, k, m):
            other = lax.rem(me - k + n, n)
            return rcopy(
                self.src_of(self.src, other, m), self.dst_of(self.dst, other, m), self.sent.at[k, m], self.recv.at[k, m], other
            )

        def own(self, m):
            return pltpu.make_async_copy(
                self.src_of(self.src, me, m), self.dst_of(self.dst, me, m), self.own_sem.at[m]
            )

        def send(self, first, last):
            for k in range(first, last):
                for m in range(self.count):
                    self.to(k, m).start()

        def begin(self):
            if not self.late:
                self.send(1, n)
            for m in range(self.count):
                self.own(m).start()

        def step(self, s, j):
            pass

        def after_step(self, s):
            if self.late:
                self.send(1 + (n - 1) * (s - 1) // (nz - 1), 1 + (n - 1) * s // (nz - 1))

        def arrive(self):
            if not self.arrived:
                self.arrived = True
                for m in range(self.count):
                    self.own(m).wait()
                for k in range(1, n):
                    for m in range(self.count):
                        self.came(k, m).wait_recv()

        def end(self):
            self.arrive()
            for k in range(1, n):
                for m in range(self.count):
                    self.to(k, m).wait_send()

    class Spread:
        factors = None

        def __init__(self, src, out, sems, phases):
            self.src, self.out, self.phases = src, out, phases
            if 1 in phases:
                self.held, *sems = sems
            self.own_sem, self.send, self.recv, self.send_half, self.recv_half = sems
            self.half, self.here = out.shape[1] // 2, False

        def own(self, leg):
            if leg == 0:
                return pltpu.make_async_copy(self.src, self.held, self.own_sem.at[0])
            return pltpu.make_async_copy(self.held, self.out.at[r], self.own_sem.at[1])

        def first(self, axis):
            to = across_y if axis else across_x
            return rcopy(self.src, self.out.at[r], self.send.at[axis], self.recv.at[axis], to, "replica")

        def first_came(self, axis):
            who = across_y if axis else across_x
            return rcopy(self.out.at[who], self.out.at[who], self.send.at[axis], self.recv.at[axis], who, "replica")

        def half_of(self, block, axis):
            return self.out.at[block, pl.ds(axis * self.half, self.half)]

        def second(self, axis):
            block, to = (across_x, across_y) if axis else (across_y, across_x)
            piece = self.half_of(block, axis)
            return rcopy(piece, piece, self.send_half.at[axis], self.recv_half.at[axis], to, "replica")

        def second_came(self, axis):
            piece = self.half_of(3 - r, axis)
            who = across_y if axis else across_x
            return rcopy(piece, piece, self.send_half.at[axis], self.recv_half.at[axis], who, "replica")

        def begin(self):
            if 1 in self.phases:
                self.first(0).start()
                self.first(1).start()
                self.own(0).start()
            else:
                self.second(0).start()
                self.second(1).start()

        def step(self, s, j):
            pass

        def mid(self):
            if self.phases == (1, 2):
                self.first_came(0).wait_recv()
                self.second(1).start()
                self.first_came(1).wait_recv()
                self.second(0).start()

        def end(self):
            if 1 in self.phases:
                self.own(0).wait()
                self.own(1).start()
                self.own(1).wait()
                for axis in (0, 1):
                    self.first(axis).wait_send()
                    if 2 not in self.phases:
                        self.first_came(axis).wait_recv()
            if 2 in self.phases:
                for axis in (0, 1):
                    self.second(axis).wait_send()
                if not self.here:
                    self.arrive()

        def arrive(self):
            self.here = True
            for axis in (0, 1):
                self.second_came(axis).wait_recv()

    class Sum:
        def __init__(self, operands, out, scratch):
            self.factors, self.out = operands if len(operands) > 1 else None, out
            self.p, *scratch = scratch if self.factors else operands + scratch
            self.a, self.b, self.send_a, self.recv_a, self.send_b, self.recv_b = scratch
            self.half = out.shape[0] // 2
            self.bits = (lax.rem(r, 2), r // 2)

        def rows(self, h):
            return pl.ds(h * self.half, self.half)

        def who(self, h):
            return across_y if h else across_x

        def first(self, h, k):
            other = 1 - self.bits[h]
            q = 2 * other + k if h else other + 2 * k
            return rcopy(
                self.p.at[q, self.rows(h)], self.a.at[h, k], self.send_a.at[h, k], self.recv_a.at[h, k], self.who(h), "replica"
            )

        def second(self, h):
            piece = self.a.at[h, 1 - self.bits[1 - h]]
            return rcopy(piece, self.b.at[h], self.send_b.at[h], self.recv_b.at[h], self.who(1 - h), "replica")

        def each(self, h, put):
            step = 16

            @pl.loop(0, self.half // step)
            def _(i):
                put(pl.multiple_of(i * step, step), step)

        def mine(self, h, k, at, step):
            q = 2 * self.bits[1] + k if h else self.bits[0] + 2 * k
            rows = pl.ds(h * self.half + at, step)
            return self.p[q, rows, :].astype(f32) + self.a[h, k, pl.ds(at, step), :].astype(f32)

        def product(self):
            x, w = self.factors
            rows, width = self.out.shape
            tile = min(512, width)
            while width % tile:
                tile -= 128

            @pl.loop(0, width // tile)
            def _(t):
                cols = pl.ds(pl.multiple_of(t * tile, tile), tile)
                if rows % 128:
                    self.p[:, :, cols] = t_dot(x[...], w[:, cols]).astype(bf16).reshape(4, rows, tile)
                else:
                    for q in range(4):
                        self.p[q, :, cols] = t_dot(x[:, q * rows : (q + 1) * rows], w[:, cols]).astype(bf16)

        def begin(self):
            if self.factors:
                self.product()
            for h in (0, 1):
                self.first(h, 1 - self.bits[1 - h]).start()
            for h in (0, 1):
                self.first(h, self.bits[1 - h]).start()

        def step(self, s, j):
            pass

        def mid(self):
            for h in (0, 1):
                k = 1 - self.bits[1 - h]
                self.first(h, k).wait_recv()

                def put(at, step):
                    self.a[h, k, pl.ds(at, step), :] = self.mine(h, k, at, step).astype(bf16)

                self.each(h, put)
                self.second(h).start()

        def end(self):
            for h in (0, 1):
                k = self.bits[1 - h]
                self.first(h, k).wait_recv()
                self.second(h).wait_recv()

                def put(at, step):
                    total = self.mine(h, k, at, step) + self.b[h, pl.ds(at, step), :].astype(f32)
                    self.out[pl.ds(h * self.half + at, step), :] = total.astype(bf16)

                self.each(h, put)
            for h in (0, 1):
                for k in (0, 1):
                    self.first(h, k).wait_send()
                self.second(h).wait_send()

    gathers = [Gather(*t) for t in zip(ag_in, ag_out, ag_sem)]

    def operands(given, flips):
        for i, (_, _, made) in enumerate(flips):
            if made:
                given.insert(2 * i, work_out[0])
        return given

    rs_in = [operands(*t) for t in zip(rs_in, products)]
    sum_in = [given + work_out[:1] if k == 3 else given for given, k in zip(sum_in, sum_kinds)]
    scatters = [Scatter(*t) for t in zip(rs_in, products, rs_out, rs_scr)]
    exchanges = [Exchange(*t) for t in zip(a2a_in, a2a_out, a2a_sem, a2a_blocks)]
    square_parts = [Spread(*t) for t in zip(sp_in, sp_out, sp_sem, spreads)]
    square_parts += [Sum(*t) for t in zip(sum_in, sum_out, sum_scr)]
    chained = [Spread(a2a_out[i], out, sems, (1, 2)) for i, out, sems in zip(chain, chain_out, chain_sem)]
    worker = work[0](gathers, square_parts, nz, z, (r, across_x, across_y, 3 - r), work_in, work_out, work_scr) if work else None

    def begin_chain():
        for i, part in zip(chain, chained):
            exchanges[i].arrive()
            part.begin()

    line_parts = gathers + scatters
    for part in gathers + exchanges:
        part.begin()
    early = []
    if worker and worker.early:
        early = [part for part in square_parts if not part.factors]
        for part in early:
            part.begin()
        worker.begin()
    late = [part for part in square_parts if part not in early]
    for part in late:
        part.begin()
    for part in early:
        part.mid()
    if chain and worker:
        begin_chain()
    for part in scatters:
        part.begin()
    if worker and not worker.early:
        worker.begin()
    if line_parts:
        if chain_at == 0 and not worker:
            begin_chain()
        for s in range(1, nz):
            @pl.loop(0, parts)
            def _(j):
                for part in line_parts:
                    part.step(s, j)

            for part in exchanges + scatters:
                part.after_step(s)
            if s == chain_at:
                begin_chain()
            if s == max(1, chain_at):
                for part in late:
                    part.mid()
            if worker:
                worker.after_step(s)
    else:
        begin_chain()
        for part in late:
            part.mid()
    for part in line_parts:
        part.end()
    for part in chained:
        part.mid()
    for part in exchanges + square_parts + chained:
        part.end()


class Backward:
    early = True

    def __init__(self, gathers, spreads, nz, z, blocks, ins, outs, scratch):
        self.ga, self.w_out, self.rot, self.cosine, self.sine, self.piece = ins
        (self.out,) = outs
        self.go, self.gk, self.gv = scratch

    def begin(self):
        length, width = self.rot.shape
        heads, blocks = width // 3 // HEAD_DIM, length // PIECE
        rot, out, cosine, sine, gk, gv = self.rot, self.out, self.cosine, self.sine, self.gk, self.gv
        inv_root = 1.0 / math.sqrt(HEAD_DIM)

        @pl.loop(0, blocks)
        def _(i):
            rows = pl.ds(pl.multiple_of(i * PIECE, PIECE), PIECE)
            self.go[rows, :] = dot_t(self.ga[rows, :], self.w_out[...]).astype(bf16)

        @pl.loop(0, heads)
        def _(h):
            at = lambda part: pl.ds(pl.multiple_of((part * heads + h) * HEAD_DIM, HEAD_DIM), HEAD_DIM)
            gk[...] = jnp.zeros_like(gk)
            gv[...] = jnp.zeros_like(gv)
            for i in range(blocks):
                keys = (i + 1) * PIECE
                own = pl.ds(i * PIECE, PIECE)
                q, g = rot[own, at(0)], self.go[own, at(0)]
                sg, visible = squash(q, rot[0:keys, at(1)], self.piece[own, :], keys, length)
                p = masked(sg, visible, keys).astype(bf16)
                gs = masked(dot_t(g, rot[0:keys, at(2)]) * sg * (1.0 - sg), visible, keys).astype(bf16)
                gq = dot(gs, rot[0:keys, at(1)]) * inv_root
                out[own, at(0)] = rotate(gq, cosine[own, :], -sine[own, :]).astype(bf16)
                gk[0:keys, :] += t_dot(gs, q)
                gv[0:keys, :] += t_dot(p, g)

            @pl.loop(0, blocks)
            def _(i):
                rows = pl.ds(pl.multiple_of(i * PIECE, PIECE), PIECE)
                out[rows, at(1)] = rotate(gk[rows, :] * inv_root, cosine[rows, :], -sine[rows, :]).astype(bf16)
                out[rows, at(2)] = gv[rows, :].astype(bf16)

    def after_step(self, s):
        pass


class Forward:
    early = False

    def __init__(self, gathers, spreads, nz, z, blocks, ins, outs, scratch):
        (gather,) = gathers
        self.gather, self.spreads, self.nz, self.z, self.blocks = gather, spreads, nz, z, blocks
        self.cot, self.w_down = ins[:2]
        self.hid, self.ggu = outs
        self.ghid = scratch[0]
        if spreads:
            self.w, self.sem = scratch[1:]
        else:
            self.w = ins[2:]
        self.rows = 2 * gather.x.shape[0]
        self.tile = min(512, self.hid.shape[1])

    def load(self, i, k):
        q = self.blocks[k]
        return pltpu.make_async_copy(self.spreads[i].out.at[q], self.w.at[i, q], self.sem.at[i, k])

    def each_tile(self, put):
        @pl.loop(0, self.hid.shape[1] // self.tile)
        def _(t):
            put(pl.multiple_of(t * self.tile, self.tile))

    def begin(self):
        if self.spreads:
            for i in (0, 1):
                for k in (0, 1, 2):
                    self.load(i, k).start()

        @pl.loop(0, self.nz)
        def _(b):
            rows = pl.ds(pl.multiple_of(b * self.rows, self.rows), self.rows)

            def put(first):
                cols = pl.ds(first, self.tile)
                self.ghid[rows, cols] = dot_t(self.cot[rows, :], self.w_down[cols, :])

            self.each_tile(put)

    def weights(self):
        if self.spreads:
            for i in (0, 1):
                self.spreads[i].arrive()
                self.load(i, 3).start()
            for i in (0, 1):
                for k in range(4):
                    self.load(i, k).wait()

    def chip(self, d):
        width = self.hid.shape[1]
        rows = pl.ds(pl.multiple_of(d * self.rows, self.rows), self.rows)

        def put(first):
            cols = pl.ds(first, self.tile)
            x = self.gather.out[pl.ds(2 * d, 2)].reshape(self.rows, -1)
            if self.spreads:
                gate, up = [dot(x, self.w[i, :, :, :, cols].reshape(x.shape[1], self.tile)) for i in (0, 1)]
            else:
                gate, up = [dot(x, w[:, cols]) for w in self.w]
            ghid = self.ghid[rows, cols]
            s = 1.0 / (1.0 + jnp.exp(-gate))
            silu = gate * s
            self.hid[rows, cols] = (silu * up).astype(bf16)
            self.ggu[rows, cols] = (ghid * up * s * (1.0 + gate * (1.0 - s))).astype(bf16)
            self.ggu[rows, pl.ds(width + first, self.tile)] = (ghid * silu).astype(bf16)

        self.each_tile(put)

    def away(self, s):
        self.gather.arrive(s)

        @pl.when(self.z >= s)
        def _():
            self.chip(self.z - s)

        if s > 0:
            @pl.when(self.z + s < self.nz)
            def _():
                self.chip(self.z + s)

    def after_step(self, s):
        last = max(1, self.nz - 2)
        if s == last:
            self.weights()
            for k in range(last):
                self.away(k)
        if s == self.nz - 1:
            for k in range(last, self.nz):
                self.away(k)


class Later:
    early = False

    def __init__(self, gathers, spreads, nz, z, blocks, ins, outs, scratch):
        (self.x, self.w), (self.out,) = ins, outs
        self.steps, self.tile = nz - 1, min(512, self.out.shape[1])

    def begin(self):
        pass

    def after_step(self, s):
        tiles = self.out.shape[1] // self.tile

        @pl.loop(tiles * (s - 1) // self.steps, tiles * s // self.steps)
        def _(t):
            cols = pl.ds(pl.multiple_of(t * self.tile, self.tile), self.tile)
            self.out[:, cols] = t_dot(self.x[...], self.w[:, cols]).astype(bf16)


def line_comm(cid, name, us, ag=(), rs=(), a2a=(), spread=(), sums=(), chain=(), chain_at=None, work=None, owners=False, parts=2):
    n = lax.axis_size("inner")
    nz = n // 2
    chain_at = nz - 2 if chain_at is None else chain_at
    dma = pltpu.SemaphoreType.DMA
    hbm = pl.BlockSpec(memory_space=pl.ANY)
    vmem = pl.BlockSpec(memory_space=pltpu.VMEM)
    products = [tuple(t[2:] + (t[0] is None,) for t in p) if isinstance(p, list) else () for p in rs]
    rs_out = [
        (p[0][0].shape[0] // n if p[0][0] is not None else work[2][0][0] // n, p[0][1].shape[0 if p[0][2] else 1]) if isinstance(p, list) else (p.shape[0] // n, p.shape[1])
        for p in rs
    ]
    rs_in = []
    for p, shape in zip(rs, rs_out):
        rs_in += [a for t in p for a in t[:2] if a is not None] if isinstance(p, list) else [p.reshape((n,) + shape)]
    sum_shapes = [(p[0].shape[1] // 4, p[2]) if isinstance(p, tuple) else (p.shape[0] // 4, p.shape[1]) for p in sums]
    sum_kinds = [(3 if p[1] is None else 2) if isinstance(p, tuple) else 1 for p in sums]
    sums = [p[:2] if isinstance(p, tuple) else (p.reshape((4,) + shape),) for p, shape in zip(sums, sum_shapes)]
    work_in, work_out, work_scratch = work[1:] if work else ((), (), [])
    inputs, in_specs, out_shape, out_specs, scratch = [], [], [], [], []

    def give(arrays, space):
        inputs.extend(arrays)
        in_specs.extend([space] * len(arrays))

    def get(shape, dtype, space):
        out_shape.append(jax.ShapeDtypeStruct(shape, dtype))
        out_specs.append(space)

    near = vmem if work else hbm
    give(ag, hbm)
    give(rs_in, vmem)
    give([w for t in a2a for w in t[0]], hbm)
    aliases = {len(inputs) + i: len(ag) + len(rs) + len(a2a) + i for i, (_, ph) in enumerate(spread) if 1 not in ph}
    give([b for b, _ in spread], hbm)
    give([x for p in sums for x in p if x is not None], vmem)
    give(work_in, vmem)
    for x in ag:
        get((n,) + x.shape, x.dtype, near)
        scratch += [dma, dma((nz, parts)), dma((nz + 1, parts)), dma((nz, parts)), dma((nz + 1, parts))]
        scratch += [dma((2, nz, parts)), dma((2, nz, parts))]
    for shape, flips in zip(rs_out, products):
        get(shape, f32, vmem)
        scratch += [pltpu.VMEM((n,) + shape, bf16)] if flips else []
        scratch += [pltpu.VMEM((nz,) + shape, bf16)] * 3 + [dma((nz, parts))] * 6
    for t in a2a:
        get(t[1], t[0][0].dtype, hbm)
        scratch += [dma((t[4],)), dma((n, t[4])), dma((n, t[4]))]
    for b, phases in spread:
        get(b.shape if 1 not in phases else (4,) + b.shape, b.dtype, hbm)
        scratch += [pltpu.VMEM(b.shape, b.dtype)] if 1 in phases else []
        scratch += [dma((2,)), dma((2,)), dma((2,)), dma((2,)), dma((2,))]
    for p, shape in zip(sums, sum_shapes):
        get(shape, bf16, vmem)
        half = (shape[0] // 2, shape[1])
        scratch += [pltpu.VMEM((4,) + shape, bf16)] if len(p) > 1 else []
        scratch += [pltpu.VMEM((2, 2) + half, bf16), pltpu.VMEM((2,) + half, bf16)]
        scratch += [dma((2, 2)), dma((2, 2)), dma((2,)), dma((2,))]
    for i in chain:
        get((4,) + a2a[i][1], a2a[i][0][0].dtype, hbm)
        scratch += [pltpu.VMEM(a2a[i][1], a2a[i][0][0].dtype), dma((2,)), dma((2,)), dma((2,)), dma((2,)), dma((2,))]
    for shape in work_out:
        get(shape, bf16, vmem)
    scratch += work_scratch
    outs = pl.pallas_call(
        functools.partial(
            line_body,
            n,
            len(ag),
            products,
            [(len(t[0]),) + t[2:6] for t in a2a],
            [ph for _, ph in spread],
            sum_kinds,
            chain,
            chain_at,
            (work[0], len(work_in), len(work_out), len(work_scratch)) if work else None,
            owners,
            parts,
        ),
        out_shape=out_shape,
        in_specs=in_specs,
        out_specs=out_specs,
        input_output_aliases=aliases,
        scratch_shapes=scratch,
        compiler_params=pltpu.CompilerParams(
            collective_id=cid, has_side_effects=True, vmem_limit_bytes=62 * 2**20
        ),
        cost_estimate=pl.CostEstimate(flops=us * 1150000000, bytes_accessed=us * 3600000, transcendentals=0),
        name=name,
    )(*inputs)
    return [o.reshape((-1,) + o.shape[2:]) if i < len(ag) else o for i, o in enumerate(outs)]


def rotate(flat, cosine, sine):
    return flat * cosine + pltpu.roll(flat, HEAD_DIM // 2, 1) * sine


def squash(q, k, piece, keys, length):
    scale = -math.log2(math.e) / math.sqrt(HEAD_DIM)
    sg = 1.0 / (1.0 + jnp.exp2(dot_t(q, k) * scale + math.log2(length)))
    row = lax.broadcasted_iota(jnp.int32, (PIECE, PIECE), 0)
    col = lax.broadcasted_iota(jnp.int32, (PIECE, PIECE), 1)
    return sg, (col <= row) | (piece >= 0)


def masked(value, visible, keys):
    last = jnp.where(visible, value[:, keys - PIECE :], 0.0)
    return last if keys == PIECE else jnp.concatenate([value[:, : keys - PIECE], last], axis=1)


def attn_body(heads, length, lin, cosine, sine, piece, out, rot):
    h, b = pl.program_id(0), pl.program_id(1)
    at = lambda part: pl.ds(pl.multiple_of((part * heads + h) * HEAD_DIM, HEAD_DIM), HEAD_DIM)
    blocks = length // PIECE

    @pl.when(b == 0)
    def _():
        @pl.loop(0, blocks)
        def _(i):
            rows = pl.ds(pl.multiple_of(i * PIECE, PIECE), PIECE)
            for part in (0, 1):
                rot[rows, at(part)] = rotate(lin[rows, at(part)], cosine[rows, :], sine[rows, :]).astype(bf16)
            rot[rows, at(2)] = lin[rows, at(2)].astype(bf16)

    for i in range(blocks):
        @pl.when(b == i)
        def _():
            keys = (i + 1) * PIECE
            own = pl.ds(i * PIECE, PIECE)
            sg, visible = squash(rot[own, at(0)], rot[0:keys, at(1)], piece[...], keys, length)
            out[...] = dot(masked(sg, visible, keys).astype(bf16), rot[0:keys, at(2)]).astype(bf16)


def attention(lin, cosine, sine, piece):
    length, width = lin.shape
    heads = width // 3 // HEAD_DIM
    whole = lambda x: pl.BlockSpec(x.shape, lambda h, b: (0, 0))
    return pl.pallas_call(
        functools.partial(attn_body, heads, length),
        grid=(heads, length // PIECE),
        out_shape=[
            jax.ShapeDtypeStruct((length, width // 3), bf16),
            jax.ShapeDtypeStruct((length, width), bf16),
        ],
        in_specs=[whole(lin), whole(cosine), whole(sine), pl.BlockSpec((PIECE, 1), lambda h, b: (b, 0))],
        out_specs=[
            pl.BlockSpec((PIECE, HEAD_DIM), lambda h, b: (b, h)),
            pl.BlockSpec((length, width), lambda h, b: (0, 0)),
        ],
        compiler_params=pltpu.CompilerParams(vmem_limit_bytes=48 * 2**20),
        cost_estimate=pl.CostEstimate(
            flops=4 * heads * length * length * HEAD_DIM // 2, bytes_accessed=8 * length * width, transcendentals=heads * length * length
        ),
        name="attention",
    )(lin, cosine, sine, piece)


def columns_out(w):
    n, nr = lax.axis_size("inner"), lax.axis_size("replica")
    part = w.shape[0] // nr
    cols = w.shape[1] // n

    def source(refs, other, m):
        rows = pl.ds(pl.multiple_of(lax.axis_index("replica") * part, part), part)
        return refs[0].at[rows, pl.ds(pl.multiple_of(other * cols, cols), cols)]

    return ((w,), (n, part, cols), source, lambda ref, other, m: ref.at[other], 1, False)


def to_all(block):
    n = lax.axis_size("inner")
    return ((block,), (n,) + block.shape, lambda refs, other, m: refs[0], lambda ref, other, m: ref.at[other], 1, False)


def rows_back(share, first, count, late=False):
    n, part, _ = share.shape
    cols = first[1]

    def source(refs, other, m):
        return refs[0].at[other, :, pl.ds((first[0] + m) * cols, cols)]

    def target(ref, other, m):
        return ref.at[pl.ds(m * part, part), pl.ds(pl.multiple_of(other * cols, cols), cols)]

    return ((share,), (count * part, n * cols), source, target, count, late)


def sum_blocks(g):
    n = lax.axis_size("inner")
    cols = g.shape[1]
    return ((g,), (n,) + (g.shape[0] // n, cols), lambda refs, other, m: refs[0].at[pl.ds(pl.multiple_of(other * 16, 16), 16)], lambda ref, other, m: ref.at[other], 1, False)


def shares_first(x):
    n, nr = lax.axis_size("inner"), lax.axis_size("replica")
    part = x.shape[1] // n // nr
    return x.reshape(x.shape[0], n, nr, part).transpose(0, 2, 1, 3).reshape(x.shape)


def owners_first(x):
    n, nr = lax.axis_size("inner"), lax.axis_size("replica")
    part = x.shape[1] // n // nr
    return x.reshape(x.shape[0], nr, n, part).transpose(0, 2, 1, 3).reshape(x.shape)


def sum_share(product):
    return lax.psum_scatter(product.astype(bf16), "replica", scatter_dimension=0, tiled=True)


def join(block):
    return lax.all_gather(block, "replica", axis=0, tiled=False)


def flat(w):
    return w.reshape(-1, w.shape[-1])


def local(
    tokens,
    w_query,
    w_key,
    w_value,
    w_out,
    w_gate,
    w_up,
    w_down,
    gain_attn,
    gain_ffn,
    pieces,
    positions,
    cotangent,
):
    n = lax.axis_size("inner")
    nr = lax.axis_size("replica")
    square = nr == 4
    own, width = tokens.shape
    length = own * n
    rows = gain_attn.shape[0]
    after = lax.optimization_barrier

    marks = jnp.zeros((8, own), jnp.int32).at[0].set(pieces).at[1].set(positions)
    gains = jnp.zeros((8, rows), f32).at[0].set(gain_attn.astype(f32)).at[1].set(gain_ffn.astype(f32))
    q_share, k_share, v_share, marks, gains = line_comm(
        0,
        "load_attn", 25,
        a2a=[columns_out(w_query), columns_out(w_key), columns_out(w_value), to_all(marks), to_all(gains)],
    )
    qkv_share = jnp.concatenate([q_share, k_share, v_share], axis=2)
    loads = [columns_out(w_gate), columns_out(w_up)]
    if square:
        x, g_share, u_share, w_qkv = line_comm(
            1, "load_ffn", 80, ag=[shares_first(tokens)], a2a=loads, spread=[(qkv_share, (1, 2))]
        )
    else:
        w_qkv = join(qkv_share)
        x, g_share, u_share = line_comm(1, "load_ffn", 80, ag=[shares_first(tokens)], a2a=loads)
    w_qkv = flat(w_qkv)
    cot, x = after((cotangent, x))
    cot = lax.all_gather(cot, "inner", axis=0, tiled=True)
    pieces, positions = marks[:, 0].reshape(length, 1), marks[:, 1].reshape(length)
    attn_gain, ffn_gain = gains[:, 0].reshape(1, -1), gains[:, 1].reshape(1, -1)

    x = x.astype(f32)
    cosine, sine = rope_tables(positions)
    u1 = x * rms_scale(x)
    n1 = (u1 * shares_first(attn_gain)).astype(bf16)
    o, rot = attention(dot(n1, w_qkv), cosine, sine, pieces)
    if square:
        a, w_g, w_u = line_comm(2, "attn_out", 50, rs=[[(o, w_out, False, 0)]], spread=[(g_share, (1,)), (u_share, (1,))])
    else:
        w_g, w_u = join(g_share), join(u_share)
        (a,) = line_comm(2, "attn_out", 50, rs=[[(o, w_out, False, 0)]])
    mid = tokens.astype(f32) + a
    r2 = rms_scale(mid)
    u2 = mid * r2
    n2 = shares_first((u2 * ffn_gain).astype(bf16))
    ffn = w_down.shape[0]
    results = [(length, ffn), (length, 2 * ffn)]
    held = [pltpu.VMEM((length, ffn), f32)]
    if square:
        held += [pltpu.VMEM((2,) + w_g.shape, bf16), pltpu.SemaphoreType.DMA((2, 4))]
        n2, w_g, w_u, hid, ggu = line_comm(
            3,
            "ffn_forward",
            60,
            ag=[n2],
            spread=[(w_g, (2,)), (w_u, (2,))],
            work=(Forward, [cot, w_down], results, held),
        )
        w_g, w_u = flat(w_g), flat(w_u)
    else:
        w_g, w_u = flat(w_g), flat(w_u)
        n2, hid, ggu = line_comm(3, "ffn_forward", 60, ag=[n2], work=(Forward, [cot, w_down, w_g, w_u], results, held))

    gu = t_dot(n2, ggu).astype(bf16)
    gu, ggu = after((gu, ggu))
    gu_share = sum_share(gu)
    tidy = square and width // n // nr == 64
    gn2, g_down = line_comm(4, "scatter_gn2", 44, owners=tidy, work=(Later, [hid, cot], [w_down.shape], []), rs=[[(ggu, w_g, True, 0), (ggu, w_u, True, w_g.shape[1])]])
    gn2 = gn2 if tidy else owners_first(gn2)
    gu2 = gn2 * ffn_gain
    ffn_gain_part = jnp.sum(gn2 * u2, axis=0)
    gmid = cotangent.astype(f32) + r2 * (gu2 - u2 * jnp.mean(gu2 * u2, axis=1, keepdims=True))
    (ga,) = line_comm(5, "gather_ga", 40, ag=[gmid.astype(bf16)])
    ga, gu_share, g_down = after((ga, gu_share, g_down))
    grad_down = lax.psum(g_down, "replica")

    cols = w_gate.shape[1] // n
    heads_width = rot.shape[1] // 3
    gu_share = gu_share.reshape(n, -1, 2 * cols)
    own_x = tokens.astype(f32)
    r1 = rms_scale(own_x)
    u1 = own_x * r1

    def gain_parts(gn1):
        both = jnp.stack([jnp.sum(gn1 * u1, axis=0).reshape(n, rows), ffn_gain_part.reshape(n, rows)], axis=1)
        return sum_blocks(jnp.pad(both, ((0, 0), (0, 14), (0, 0))).reshape(n * 16, rows))

    held = [pltpu.VMEM((length, heads_width), bf16)] + [pltpu.VMEM((length, HEAD_DIM), f32)] * 2
    work = (Backward, [ga, w_out, rot, cosine, sine, pieces], [rot.shape], held)
    gn1_part = [(None, w_qkv, True, 0)]
    if square:
        gn1, gate_rows, up_rows, out_share, qkv_share, grad_gate, _ = line_comm(
            6,
            "scatter_gn1",
            1,
            owners=tidy,
            rs=[gn1_part],
            a2a=[rows_back(gu_share, (0, cols), 1), rows_back(gu_share, (1, cols), 1, False)],
            sums=[(o, ga, width), (n1, None, rot.shape[1])],
            chain=(0,),
            chain_at=0,
            work=work,
        )
        gn1 = gn1 if tidy else owners_first(gn1)
        qkv_back = rows_back(qkv_share.reshape(n, -1, 3 * heads_width), (0, heads_width), 3)
        mlp, _, _, grad_up, grad_out, grad_qkv, gains = line_comm(
            7,
            "rows_attn",
            1,
            rs=[[(hid, w_down, False, 0)]],
            a2a=[qkv_back, gain_parts(gn1)],
            spread=[(up_rows, (1, 2)), (out_share, (1, 2))],
            chain=(0, 1),
            chain_at=0,
        )
        gains = jnp.sum(gains, axis=(0, 1))
    else:
        gu_back = rows_back(gu_share, (0, cols), 2)
        gn1, gu_rows, gqkv = line_comm(6, "scatter_gn1", 80, rs=[gn1_part], a2a=[gu_back], work=work)
        gn1 = owners_first(gn1)
        g_qkv = sum_share(t_dot(n1, gqkv))
        qkv_back = rows_back(g_qkv.reshape(n, -1, 3 * heads_width), (0, heads_width), 3)
        mlp, qkv_rows, gains = line_comm(
            7, "rows_attn", 75, rs=[[(hid, w_down, False, 0)]], a2a=[qkv_back, gain_parts(gn1)]
        )
        gains = lax.psum(jnp.sum(gains, axis=0), "replica")
        grad_gu = join(gu_rows).reshape(nr, 2, -1, n * cols)
        grad_gate, grad_up, grad_out, grad_qkv = grad_gu[:, 0], grad_gu[:, 1], join(sum_share(t_dot(o, ga))), join(qkv_rows)
    output = (mid + mlp).astype(bf16)
    grad_qkv = grad_qkv.reshape(nr, 3, -1, width).astype(f32)

    gu1 = gn1 * attn_gain
    grad_tokens = gmid + r1 * (gu1 - u1 * jnp.mean(gu1 * u1, axis=1, keepdims=True))
    return (
        output,
        grad_tokens,
        grad_qkv[:, 0].reshape(w_query.shape),
        grad_qkv[:, 1].reshape(w_key.shape),
        grad_qkv[:, 2].reshape(w_value.shape),
        grad_out.reshape(w_out.shape).astype(f32),
        grad_gate.reshape(w_gate.shape).astype(f32),
        grad_up.reshape(w_up.shape).astype(f32),
        grad_down.reshape(w_down.shape).astype(f32),
        gains[0],
        gains[1],
    )


def solution(mesh):
    tok = P(("replica", "inner"), None)
    row = P("inner", None)
    vec = P("inner")
    mark = P(("replica", "inner"))
    return jax.shard_map(
        local,
        mesh=mesh,
        in_specs=(tok, row, row, row, row, row, row, row, vec, vec, mark, mark, tok),
        out_specs=(tok, tok, row, row, row, row, row, row, row, vec, vec),
        check_vma=False,
    )
```

```python
import functools
import math

import jax
import jax.numpy as jnp
from jax import lax
from jax.experimental import pallas as pl
from jax.experimental.pallas import tpu as pltpu
from jax.sharding import PartitionSpec as P

HEAD_DIM = 128
PIECE = 256
epsilon = 1e-06
rope_base = 10000.0
dims_rows = (((1,), (1,)), ((), ()))
dims_cols = (((0,), (0,)), ((), ()))
f32 = jnp.float32
bf16 = jnp.bfloat16


def dot(a, b):
    return jnp.dot(a, b, preferred_element_type=f32)


def dot_t(a, b):
    return lax.dot_general(a, b, dims_rows, preferred_element_type=f32)


def t_dot(a, b):
    return lax.dot_general(a, b, dims_cols, preferred_element_type=f32)


def rope_tables(positions):
    half_dim = HEAD_DIM // 2
    frequency = rope_base ** (-jnp.arange(half_dim, dtype=f32) * 2.0 / HEAD_DIM)
    angle = positions.astype(f32)[:, None] * frequency[None, :]
    cosine, sine = jnp.cos(angle), jnp.sin(angle)
    return jnp.concatenate([cosine, cosine], axis=1), jnp.concatenate([-sine, sine], axis=1)


def rms_scale(values):
    return lax.rsqrt(jnp.mean(values * values, axis=1, keepdims=True) + epsilon)


def rcopy(src, dst, ssem, rsem, to, axis="inner"):
    return pltpu.make_async_remote_copy(
        src_ref=src,
        dst_ref=dst,
        send_sem=ssem,
        recv_sem=rsem,
        device_id={axis: to},
        device_id_type=pl.DeviceIdType.MESH,
    )


def signal(sem, to, axis="inner"):
    pl.semaphore_signal(sem, inc=1, device_id={axis: to}, device_id_type=pl.DeviceIdType.MESH)


def line_body(n, n_ag, products, a2a_blocks, spreads, sum_kinds, chain, chain_at, work, owners, parts, *refs):
    refs = list(refs)
    nz = n // 2
    n_a2a = len(a2a_blocks)
    take = lambda count: [refs.pop(0) for _ in range(count)]
    n_sp, n_rs, n_sum = len(spreads), len(products), len(sum_kinds)
    ag_in, rs_in, a2a_in = take(n_ag), [take(sum(2 - made for _, _, made in t) or 1) for t in products], [take(t[0]) for t in a2a_blocks]
    sp_in, sum_in = take(n_sp), [take(2 if k == 2 else 1) for k in sum_kinds]
    work_in = take(work[1]) if work else []
    ag_out, rs_out, a2a_out, sp_out, sum_out = take(n_ag), take(n_rs), take(n_a2a), take(n_sp), take(n_sum)
    chain_out = take(len(chain))
    work_out = take(work[2]) if work else []
    ag_sem = [take(7) for _ in range(n_ag)]
    rs_scr = [take(10 if t else 9) for t in products]
    a2a_sem = [take(3) for _ in range(n_a2a)]
    sp_sem = [take(5 + (1 in ph)) for ph in spreads]
    sum_scr = [take(6 if k == 1 else 7) for k in sum_kinds]
    chain_sem = [take(6) for _ in chain]
    work_scr = take(work[3]) if work else []
    me = lax.axis_index("inner")
    z, c = me // 2, lax.rem(me, 2)
    sib = me + 1 - 2 * c
    r = lax.axis_index("replica")
    across_x, across_y = r + 1 - 2 * lax.rem(r, 2), r + 2 - 4 * (r // 2)
    barrier = pltpu.get_barrier_semaphore()
    more = 0
    if n_sp + n_sum + len(chain):
        signal(barrier, across_x, "replica")
        signal(barrier, across_y, "replica")
        more = 2
    if n_a2a:
        for k in range(1, n):
            signal(barrier, lax.rem(me + k, n))
        pl.semaphore_wait(barrier, n - 1 + more)
    else:
        signal(barrier, sib)

        @pl.when(z + 1 < nz)
        def _():
            signal(barrier, me + 2)

        @pl.when(z > 0)
        def _():
            signal(barrier, me - 2)

        pl.semaphore_wait(barrier, 1 + more + (z + nz - 1) // nz + (2 * nz - 2 - z) // nz)

    def rows_of(ref, j):
        count = ref.shape[0] // parts
        return pl.ds(pl.multiple_of(j * count, count), count)

    class Gather:
        def __init__(self, x, out, sems):
            self.x, self.out, self.here = x, out, set()
            self.own_sem, self.rs, self.rr, self.ls, self.lr, self.ss, self.sr = sems

        def own(self):
            return pltpu.make_async_copy(self.x, self.out.at[me], self.own_sem)

        def piece(self, block, s, j):
            rows = rows_of(self.x, j)
            return self.x.at[rows] if s == 0 else self.out.at[block, rows]

        def right(self, s, j):
            b = me - 2 * s
            dst = self.out.at[b, rows_of(self.x, j)]
            return rcopy(self.piece(b, s, j), dst, self.rs.at[s, j], self.rr.at[s + 1, j], me + 2)

        def left(self, s, j):
            b = me + 2 * s
            dst = self.out.at[b, rows_of(self.x, j)]
            return rcopy(self.piece(b, s, j), dst, self.ls.at[s, j], self.lr.at[s + 1, j], me - 2)

        def side(self, s, k, j):
            b = me - 2 * s if k == 0 else me + 2 * s
            dst = self.out.at[b, rows_of(self.x, j)]
            return rcopy(self.piece(b, s, j), dst, self.ss.at[k, s, j], self.sr.at[k, s, j], sib)

        def from_left(self, s, j):
            dst = self.out.at[me - 2 * s, rows_of(self.x, j)]
            return rcopy(dst, dst, self.rs.at[s, j], self.rr.at[s, j], me - 2)

        def from_right(self, s, j):
            dst = self.out.at[me + 2 * s, rows_of(self.x, j)]
            return rcopy(dst, dst, self.ls.at[s, j], self.lr.at[s, j], me + 2)

        def from_side(self, s, k, j):
            b = sib - 2 * s if k == 0 else sib + 2 * s
            dst = self.out.at[b, rows_of(self.x, j)]
            return rcopy(dst, dst, self.ss.at[k, s, j], self.sr.at[k, s, j], sib)

        def begin(self):
            @pl.loop(0, parts)
            def _(j):
                @pl.when(z + 1 < nz)
                def _():
                    self.right(0, j).start()

                @pl.when(z > 0)
                def _():
                    self.left(0, j).start()

            self.own().start()

            @pl.loop(0, parts)
            def _(j):
                self.side(0, 0, j).start()

        def step(self, s, j):
            @pl.when(z >= s)
            def _():
                self.from_left(s, j).wait_recv()

                @pl.when(z + 1 < nz)
                def _():
                    self.right(s, j).start()

                self.side(s, 0, j).start()

            @pl.when(z + s < nz)
            def _():
                self.from_right(s, j).wait_recv()

                @pl.when(z > 0)
                def _():
                    self.left(s, j).start()

                self.side(s, 1, j).start()

        def arrive(self, s):
            self.here.add(s)
            if s == 0:
                self.own().wait()

            @pl.loop(0, parts)
            def _(j):
                @pl.when(z >= s)
                def _():
                    self.from_side(s, 0, j).wait_recv()

                if s > 0:
                    @pl.when(z + s < nz)
                    def _():
                        self.from_side(s, 1, j).wait_recv()

        def end(self):
            for s in range(nz):
                if s not in self.here:
                    self.arrive(s)

                @pl.loop(0, parts)
                def _(j):
                    @pl.when(z >= s)
                    def _():
                        @pl.when(z + 1 < nz)
                        def _():
                            self.right(s, j).wait_send()

                        self.side(s, 0, j).wait_send()

                    @pl.when(z + s < nz)
                    def _():
                        @pl.when(z > 0)
                        def _():
                            self.left(s, j).wait_send()

                        if s > 0:
                            self.side(s, 1, j).wait_send()

    class Scatter:
        def __init__(self, operands, flips, out, scratch):
            self.pairs, self.out = [(x, w) + t[:2] for x, w, t in zip(operands[::2], operands[1::2], flips)], out
            self.p, *scratch = scratch if flips else operands + scratch
            self.sib_buf, self.l_buf, self.r_buf, self.ss, self.sr, self.rs, self.rr, self.ls, self.lr = scratch
            self.count = out.shape[0] // parts

        def side(self, d, j):
            rows = rows_of(self.out, j)
            return rcopy(self.p.at[2 * d + 1 - c, rows], self.sib_buf.at[d, rows], self.ss.at[d, j], self.sr.at[d, j], sib)

        def right(self, d, j, to=2):
            rows = rows_of(self.out, j)
            return rcopy(self.l_buf.at[d, rows], self.l_buf.at[d, rows], self.rs.at[d, j], self.rr.at[d, j], me + to)

        def left(self, d, j, to=-2):
            rows = rows_of(self.out, j)
            return rcopy(self.r_buf.at[d, rows], self.r_buf.at[d, rows], self.ls.at[d, j], self.lr.at[d, j], me + to)

        def product(self, d):
            own, width = self.out.shape
            rows = pl.ds(d * 2 * own, 2 * own)
            tile = min(512, width)

            @pl.loop(0, width // tile)
            def _(t):
                cols = pl.ds(pl.multiple_of(t * tile, tile), tile)
                total = 0.0
                for x, w, flip, first in self.pairs:
                    x = x[rows, first : first + w.shape[1 if flip else 0]]
                    total += dot_t(x, w[cols, :]) if flip else dot(x, w[:, cols])
                total = total.astype(bf16)
                self.p[2 * d, :, cols] = total[:own]
                self.p[2 * d + 1, :, cols] = total[own:]

        def begin(self):
            for s in range(1 if self.pairs else nz // 2):
                self.offer(s)

        def offer(self, s):
            for d in (nz - 1 - s, s):
                if self.pairs:
                    self.product(d)

                @pl.loop(0, parts)
                def _(j):
                    self.side(d, j).start()

        def after_step(self, s):
            if self.pairs and s < nz // 2:
                self.offer(s)

        def pair(self, d, rows):
            return self.p[2 * d + c, rows, :].astype(f32) + self.sib_buf[d, rows, :].astype(f32)

        def step(self, s, j):
            tick = (s - 1) * parts + j
            k = tick - z

            @pl.when((k >= 0) & (k < (nz - 1 - z) * parts))
            def _():
                d, i = nz - 1 - k // parts, lax.rem(k, parts)
                rows = rows_of(self.out, i)
                self.side(d, i).wait_recv()

                @pl.when(z > 0)
                def _():
                    self.right(d, i, -2).wait_recv()
                    self.l_buf[d, rows, :] = (self.pair(d, rows) + self.l_buf[d, rows, :].astype(f32)).astype(bf16)

                @pl.when(z == 0)
                def _():
                    self.l_buf[d, rows, :] = self.pair(d, rows).astype(bf16)

                self.right(d, i).start()

            m = tick - (nz - 1 - z)

            @pl.when((m >= 0) & (m < z * parts))
            def _():
                d, i = m // parts, lax.rem(m, parts)
                rows = rows_of(self.out, i)
                self.side(d, i).wait_recv()

                @pl.when(z + 1 < nz)
                def _():
                    self.left(d, i, 2).wait_recv()
                    self.r_buf[d, rows, :] = (self.pair(d, rows) + self.r_buf[d, rows, :].astype(f32)).astype(bf16)

                @pl.when(z + 1 == nz)
                def _():
                    self.r_buf[d, rows, :] = self.pair(d, rows).astype(bf16)

                self.left(d, i).start()

        def owners_first(self, rows):
            tiles = [self.out[rows, k * 128 : (k + 1) * 128] for k in range(self.out.shape[1] // 128)]
            low = lax.broadcasted_iota(jnp.int32, tiles[0].shape, 1) < 64
            for k in range(len(tiles)):
                i = k // 2
                first = 2 * (k % 2) * n + i
                a, b = tiles[first // 2], tiles[(first + n) // 2]
                new = jnp.where(low, pltpu.roll(a, 64, 1), b) if i % 2 else jnp.where(low, a, pltpu.roll(b, 64, 1))
                self.out[rows, k * 128 : (k + 1) * 128] = new

        def end(self):
            @pl.loop(0, parts)
            def _(j):
                rows = rows_of(self.out, j)
                self.side(z, j).wait_recv()
                self.out[rows, :] = self.pair(z, rows)

                @pl.when(z > 0)
                def _():
                    self.right(z, j, -2).wait_recv()
                    self.out[rows, :] = self.out[rows, :] + self.l_buf[z, rows, :].astype(f32)

                @pl.when(z + 1 < nz)
                def _():
                    self.left(z, j, 2).wait_recv()
                    self.out[rows, :] = self.out[rows, :] + self.r_buf[z, rows, :].astype(f32)

                if owners:
                    self.owners_first(rows)

            for d in range(nz):
                @pl.loop(0, parts)
                def _(j):
                    self.side(d, j).wait_send()

                    @pl.when(d > z)
                    def _():
                        self.right(d, j).wait_send()

                    @pl.when(d < z)
                    def _():
                        self.left(d, j).wait_send()

    class Exchange:
        def __init__(self, src, dst, sems, blocks):
            self.src, self.dst = src, dst
            self.own_sem, self.sent, self.recv = sems
            _, self.src_of, self.dst_of, self.count, self.late = blocks
            self.arrived = False

        def to(self, k, m):
            other = lax.rem(me + k, n)
            return rcopy(
                self.src_of(self.src, other, m), self.dst_of(self.dst, me, m), self.sent.at[k, m], self.recv.at[k, m], other
            )

        def came(self, k, m):
            other = lax.rem(me - k + n, n)
            return rcopy(
                self.src_of(self.src, other, m), self.dst_of(self.dst, other, m), self.sent.at[k, m], self.recv.at[k, m], other
            )

        def own(self, m):
            return pltpu.make_async_copy(
                self.src_of(self.src, me, m), self.dst_of(self.dst, me, m), self.own_sem.at[m]
            )

        def send(self, first, last):
            for k in range(first, last):
                for m in range(self.count):
                    self.to(k, m).start()

        def begin(self):
            if not self.late:
                self.send(1, n)
            for m in range(self.count):
                self.own(m).start()

        def step(self, s, j):
            pass

        def after_step(self, s):
            if self.late:
                self.send(1 + (n - 1) * (s - 1) // (nz - 1), 1 + (n - 1) * s // (nz - 1))

        def arrive(self):
            if not self.arrived:
                self.arrived = True
                for m in range(self.count):
                    self.own(m).wait()
                for k in range(1, n):
                    for m in range(self.count):
                        self.came(k, m).wait_recv()

        def end(self):
            self.arrive()
            for k in range(1, n):
                for m in range(self.count):
                    self.to(k, m).wait_send()

    class Spread:
        factors = None

        def __init__(self, src, out, sems, phases):
            self.src, self.out, self.phases = src, out, phases
            if 1 in phases:
                self.held, *sems = sems
            self.own_sem, self.send, self.recv, self.send_half, self.recv_half = sems
            self.half, self.here = out.shape[1] // 2, False

        def own(self, leg):
            if leg == 0:
                return pltpu.make_async_copy(self.src, self.held, self.own_sem.at[0])
            return pltpu.make_async_copy(self.held, self.out.at[r], self.own_sem.at[1])

        def first(self, axis):
            to = across_y if axis else across_x
            return rcopy(self.src, self.out.at[r], self.send.at[axis], self.recv.at[axis], to, "replica")

        def first_came(self, axis):
            who = across_y if axis else across_x
            return rcopy(self.out.at[who], self.out.at[who], self.send.at[axis], self.recv.at[axis], who, "replica")

        def half_of(self, block, axis):
            return self.out.at[block, pl.ds(axis * self.half, self.half)]

        def second(self, axis):
            block, to = (across_x, across_y) if axis else (across_y, across_x)
            piece = self.half_of(block, axis)
            return rcopy(piece, piece, self.send_half.at[axis], self.recv_half.at[axis], to, "replica")

        def second_came(self, axis):
            piece = self.half_of(3 - r, axis)
            who = across_y if axis else across_x
            return rcopy(piece, piece, self.send_half.at[axis], self.recv_half.at[axis], who, "replica")

        def begin(self):
            if 1 in self.phases:
                self.first(0).start()
                self.first(1).start()
                self.own(0).start()
            else:
                self.second(0).start()
                self.second(1).start()

        def step(self, s, j):
            pass

        def mid(self):
            if self.phases == (1, 2):
                self.first_came(0).wait_recv()
                self.second(1).start()
                self.first_came(1).wait_recv()
                self.second(0).start()

        def end(self):
            if 1 in self.phases:
                self.own(0).wait()
                self.own(1).start()
                self.own(1).wait()
                for axis in (0, 1):
                    self.first(axis).wait_send()
                    if 2 not in self.phases:
                        self.first_came(axis).wait_recv()
            if 2 in self.phases:
                for axis in (0, 1):
                    self.second(axis).wait_send()
                if not self.here:
                    self.arrive()

        def arrive(self):
            self.here = True
            for axis in (0, 1):
                self.second_came(axis).wait_recv()

    class Sum:
        def __init__(self, operands, out, scratch):
            self.factors, self.out = operands if len(operands) > 1 else None, out
            self.p, *scratch = scratch if self.factors else operands + scratch
            self.a, self.b, self.send_a, self.recv_a, self.send_b, self.recv_b = scratch
            self.half = out.shape[0] // 2
            self.bits = (lax.rem(r, 2), r // 2)

        def rows(self, h):
            return pl.ds(h * self.half, self.half)

        def who(self, h):
            return across_y if h else across_x

        def first(self, h, k):
            other = 1 - self.bits[h]
            q = 2 * other + k if h else other + 2 * k
            return rcopy(
                self.p.at[q, self.rows(h)], self.a.at[h, k], self.send_a.at[h, k], self.recv_a.at[h, k], self.who(h), "replica"
            )

        def second(self, h):
            piece = self.a.at[h, 1 - self.bits[1 - h]]
            return rcopy(piece, self.b.at[h], self.send_b.at[h], self.recv_b.at[h], self.who(1 - h), "replica")

        def each(self, h, put):
            step = 16

            @pl.loop(0, self.half // step)
            def _(i):
                put(pl.multiple_of(i * step, step), step)

        def mine(self, h, k, at, step):
            q = 2 * self.bits[1] + k if h else self.bits[0] + 2 * k
            rows = pl.ds(h * self.half + at, step)
            return self.p[q, rows, :].astype(f32) + self.a[h, k, pl.ds(at, step), :].astype(f32)

        def product(self):
            x, w = self.factors
            rows, width = self.out.shape
            tile = min(512, width)
            while width % tile:
                tile -= 128

            @pl.loop(0, width // tile)
            def _(t):
                cols = pl.ds(pl.multiple_of(t * tile, tile), tile)
                if rows % 128:
                    self.p[:, :, cols] = t_dot(x[...], w[:, cols]).astype(bf16).reshape(4, rows, tile)
                else:
                    for q in range(4):
                        self.p[q, :, cols] = t_dot(x[:, q * rows : (q + 1) * rows], w[:, cols]).astype(bf16)

        def begin(self):
            if self.factors:
                self.product()
            for h in (0, 1):
                self.first(h, 1 - self.bits[1 - h]).start()
            for h in (0, 1):
                self.first(h, self.bits[1 - h]).start()

        def step(self, s, j):
            pass

        def mid(self):
            for h in (0, 1):
                k = 1 - self.bits[1 - h]
                self.first(h, k).wait_recv()

                def put(at, step):
                    self.a[h, k, pl.ds(at, step), :] = self.mine(h, k, at, step).astype(bf16)

                self.each(h, put)
                self.second(h).start()

        def end(self):
            for h in (0, 1):
                k = self.bits[1 - h]
                self.first(h, k).wait_recv()
                self.second(h).wait_recv()

                def put(at, step):
                    total = self.mine(h, k, at, step) + self.b[h, pl.ds(at, step), :].astype(f32)
                    self.out[pl.ds(h * self.half + at, step), :] = total.astype(bf16)

                self.each(h, put)
            for h in (0, 1):
                for k in (0, 1):
                    self.first(h, k).wait_send()
                self.second(h).wait_send()

    gathers = [Gather(*t) for t in zip(ag_in, ag_out, ag_sem)]

    def operands(given, flips):
        for i, (_, _, made) in enumerate(flips):
            if made:
                given.insert(2 * i, work_out[0])
        return given

    rs_in = [operands(*t) for t in zip(rs_in, products)]
    sum_in = [given + work_out[:1] if k == 3 else given for given, k in zip(sum_in, sum_kinds)]
    scatters = [Scatter(*t) for t in zip(rs_in, products, rs_out, rs_scr)]
    exchanges = [Exchange(*t) for t in zip(a2a_in, a2a_out, a2a_sem, a2a_blocks)]
    square_parts = [Spread(*t) for t in zip(sp_in, sp_out, sp_sem, spreads)]
    square_parts += [Sum(*t) for t in zip(sum_in, sum_out, sum_scr)]
    chained = [Spread(a2a_out[i], out, sems, (1, 2)) for i, out, sems in zip(chain, chain_out, chain_sem)]
    worker = work[0](gathers, square_parts, nz, z, (r, across_x, across_y, 3 - r), work_in, work_out, work_scr) if work else None

    def begin_chain():
        for i, part in zip(chain, chained):
            exchanges[i].arrive()
            part.begin()

    line_parts = gathers + scatters
    for part in gathers + exchanges:
        part.begin()
    early = []
    if worker and worker.early:
        early = [part for part in square_parts if not part.factors]
        for part in early:
            part.begin()
        worker.begin()
    late = [part for part in square_parts if part not in early]
    for part in late:
        part.begin()
    for part in early:
        part.mid()
    if chain and worker:
        begin_chain()
    for part in scatters:
        part.begin()
    if worker and not worker.early:
        worker.begin()
    if line_parts:
        if chain_at == 0 and not worker:
            begin_chain()
        for s in range(1, nz):
            @pl.loop(0, parts)
            def _(j):
                for part in line_parts:
                    part.step(s, j)

            for part in exchanges + scatters:
                part.after_step(s)
            if s == chain_at:
                begin_chain()
            if s == max(1, chain_at):
                for part in late:
                    part.mid()
            if worker:
                worker.after_step(s)
    else:
        begin_chain()
        for part in late:
            part.mid()
    for part in line_parts:
        part.end()
    for part in chained:
        part.mid()
    for part in exchanges + square_parts + chained:
        part.end()


class Backward:
    early = True

    def __init__(self, gathers, spreads, nz, z, blocks, ins, outs, scratch):
        self.ga, self.w_out, self.rot, self.cosine, self.sine, self.piece = ins
        (self.out,) = outs
        self.go, self.gk, self.gv = scratch

    def begin(self):
        length, width = self.rot.shape
        heads, blocks = width // 3 // HEAD_DIM, length // PIECE
        rot, out, cosine, sine, gk, gv = self.rot, self.out, self.cosine, self.sine, self.gk, self.gv
        inv_root = 1.0 / math.sqrt(HEAD_DIM)

        @pl.loop(0, blocks)
        def _(i):
            rows = pl.ds(pl.multiple_of(i * PIECE, PIECE), PIECE)
            self.go[rows, :] = dot_t(self.ga[rows, :], self.w_out[...]).astype(bf16)

        @pl.loop(0, heads)
        def _(h):
            at = lambda part: pl.ds(pl.multiple_of((part * heads + h) * HEAD_DIM, HEAD_DIM), HEAD_DIM)
            gk[...] = jnp.zeros_like(gk)
            gv[...] = jnp.zeros_like(gv)
            for i in range(blocks):
                keys = (i + 1) * PIECE
                own = pl.ds(i * PIECE, PIECE)
                q, g = rot[own, at(0)], self.go[own, at(0)]
                sg, visible = squash(q, rot[0:keys, at(1)], self.piece[own, :], keys, length)
                p = masked(sg, visible, keys).astype(bf16)
                gs = masked(dot_t(g, rot[0:keys, at(2)]) * sg * (1.0 - sg), visible, keys).astype(bf16)
                gq = dot(gs, rot[0:keys, at(1)]) * inv_root
                out[own, at(0)] = rotate(gq, cosine[own, :], -sine[own, :]).astype(bf16)
                gk[0:keys, :] += t_dot(gs, q)
                gv[0:keys, :] += t_dot(p, g)

            @pl.loop(0, blocks)
            def _(i):
                rows = pl.ds(pl.multiple_of(i * PIECE, PIECE), PIECE)
                out[rows, at(1)] = rotate(gk[rows, :] * inv_root, cosine[rows, :], -sine[rows, :]).astype(bf16)
                out[rows, at(2)] = gv[rows, :].astype(bf16)

    def after_step(self, s):
        pass


class Forward:
    early = False

    def __init__(self, gathers, spreads, nz, z, blocks, ins, outs, scratch):
        (gather,) = gathers
        self.gather, self.spreads, self.nz, self.z, self.blocks = gather, spreads, nz, z, blocks
        self.cot, self.w_down = ins[:2]
        self.hid, self.ggu = outs
        self.ghid = scratch[0]
        if spreads:
            self.w, self.sem = scratch[1:]
        else:
            self.w = ins[2:]
        self.rows = 2 * gather.x.shape[0]
        self.tile = min(512, self.hid.shape[1])

    def load(self, i, k):
        q = self.blocks[k]
        return pltpu.make_async_copy(self.spreads[i].out.at[q], self.w.at[i, q], self.sem.at[i, k])

    def each_tile(self, put):
        @pl.loop(0, self.hid.shape[1] // self.tile)
        def _(t):
            put(pl.multiple_of(t * self.tile, self.tile))

    def begin(self):
        if self.spreads:
            for i in (0, 1):
                for k in (0, 1, 2):
                    self.load(i, k).start()

        @pl.loop(0, self.nz)
        def _(b):
            rows = pl.ds(pl.multiple_of(b * self.rows, self.rows), self.rows)

            def put(first):
                cols = pl.ds(first, self.tile)
                self.ghid[rows, cols] = dot_t(self.cot[rows, :], self.w_down[cols, :])

            self.each_tile(put)

    def weights(self):
        if self.spreads:
            for i in (0, 1):
                self.spreads[i].arrive()
                self.load(i, 3).start()
            for i in (0, 1):
                for k in range(4):
                    self.load(i, k).wait()

    def chip(self, d):
        width = self.hid.shape[1]
        rows = pl.ds(pl.multiple_of(d * self.rows, self.rows), self.rows)

        def put(first):
            cols = pl.ds(first, self.tile)
            x = self.gather.out[pl.ds(2 * d, 2)].reshape(self.rows, -1)
            if self.spreads:
                gate, up = [dot(x, self.w[i, :, :, :, cols].reshape(x.shape[1], self.tile)) for i in (0, 1)]
            else:
                gate, up = [dot(x, w[:, cols]) for w in self.w]
            ghid = self.ghid[rows, cols]
            s = 1.0 / (1.0 + jnp.exp(-gate))
            silu = gate * s
            self.hid[rows, cols] = (silu * up).astype(bf16)
            self.ggu[rows, cols] = (ghid * up * s * (1.0 + gate * (1.0 - s))).astype(bf16)
            self.ggu[rows, pl.ds(width + first, self.tile)] = (ghid * silu).astype(bf16)

        self.each_tile(put)

    def away(self, s):
        self.gather.arrive(s)

        @pl.when(self.z >= s)
        def _():
            self.chip(self.z - s)

        if s > 0:
            @pl.when(self.z + s < self.nz)
            def _():
                self.chip(self.z + s)

    def after_step(self, s):
        last = max(1, self.nz - 2)
        if s == last:
            self.weights()
            for k in range(last):
                self.away(k)
        if s == self.nz - 1:
            for k in range(last, self.nz):
                self.away(k)


class Later:
    early = False

    def __init__(self, gathers, spreads, nz, z, blocks, ins, outs, scratch):
        (self.x, self.w), (self.out,) = ins, outs
        self.steps, self.tile = nz - 1, min(512, self.out.shape[1])

    def begin(self):
        pass

    def after_step(self, s):
        tiles = self.out.shape[1] // self.tile

        @pl.loop(tiles * (s - 1) // self.steps, tiles * s // self.steps)
        def _(t):
            cols = pl.ds(pl.multiple_of(t * self.tile, self.tile), self.tile)
            self.out[:, cols] = t_dot(self.x[...], self.w[:, cols]).astype(bf16)


def line_comm(cid, name, us, ag=(), rs=(), a2a=(), spread=(), sums=(), chain=(), chain_at=None, work=None, owners=False, parts=2):
    n = lax.axis_size("inner")
    nz = n // 2
    chain_at = nz - 2 if chain_at is None else chain_at
    dma = pltpu.SemaphoreType.DMA
    hbm = pl.BlockSpec(memory_space=pl.ANY)
    vmem = pl.BlockSpec(memory_space=pltpu.VMEM)
    products = [tuple(t[2:] + (t[0] is None,) for t in p) if isinstance(p, list) else () for p in rs]
    rs_out = [
        (p[0][0].shape[0] // n if p[0][0] is not None else work[2][0][0] // n, p[0][1].shape[0 if p[0][2] else 1]) if isinstance(p, list) else (p.shape[0] // n, p.shape[1])
        for p in rs
    ]
    rs_in = []
    for p, shape in zip(rs, rs_out):
        rs_in += [a for t in p for a in t[:2] if a is not None] if isinstance(p, list) else [p.reshape((n,) + shape)]
    sum_shapes = [(p[0].shape[1] // 4, p[2]) if isinstance(p, tuple) else (p.shape[0] // 4, p.shape[1]) for p in sums]
    sum_kinds = [(3 if p[1] is None else 2) if isinstance(p, tuple) else 1 for p in sums]
    sums = [p[:2] if isinstance(p, tuple) else (p.reshape((4,) + shape),) for p, shape in zip(sums, sum_shapes)]
    work_in, work_out, work_scratch = work[1:] if work else ((), (), [])
    inputs, in_specs, out_shape, out_specs, scratch = [], [], [], [], []

    def give(arrays, space):
        inputs.extend(arrays)
        in_specs.extend([space] * len(arrays))

    def get(shape, dtype, space):
        out_shape.append(jax.ShapeDtypeStruct(shape, dtype))
        out_specs.append(space)

    near = vmem if work else hbm
    give(ag, hbm)
    give(rs_in, vmem)
    give([w for t in a2a for w in t[0]], hbm)
    aliases = {len(inputs) + i: len(ag) + len(rs) + len(a2a) + i for i, (_, ph) in enumerate(spread) if 1 not in ph}
    give([b for b, _ in spread], hbm)
    give([x for p in sums for x in p if x is not None], vmem)
    give(work_in, vmem)
    for x in ag:
        get((n,) + x.shape, x.dtype, near)
        scratch += [dma, dma((nz, parts)), dma((nz + 1, parts)), dma((nz, parts)), dma((nz + 1, parts))]
        scratch += [dma((2, nz, parts)), dma((2, nz, parts))]
    for shape, flips in zip(rs_out, products):
        get(shape, f32, vmem)
        scratch += [pltpu.VMEM((n,) + shape, bf16)] if flips else []
        scratch += [pltpu.VMEM((nz,) + shape, bf16)] * 3 + [dma((nz, parts))] * 6
    for t in a2a:
        get(t[1], t[0][0].dtype, hbm)
        scratch += [dma((t[4],)), dma((n, t[4])), dma((n, t[4]))]
    for b, phases in spread:
        get(b.shape if 1 not in phases else (4,) + b.shape, b.dtype, hbm)
        scratch += [pltpu.VMEM(b.shape, b.dtype)] if 1 in phases else []
        scratch += [dma((2,)), dma((2,)), dma((2,)), dma((2,)), dma((2,))]
    for p, shape in zip(sums, sum_shapes):
        get(shape, bf16, vmem)
        half = (shape[0] // 2, shape[1])
        scratch += [pltpu.VMEM((4,) + shape, bf16)] if len(p) > 1 else []
        scratch += [pltpu.VMEM((2, 2) + half, bf16), pltpu.VMEM((2,) + half, bf16)]
        scratch += [dma((2, 2)), dma((2, 2)), dma((2,)), dma((2,))]
    for i in chain:
        get((4,) + a2a[i][1], a2a[i][0][0].dtype, hbm)
        scratch += [pltpu.VMEM(a2a[i][1], a2a[i][0][0].dtype), dma((2,)), dma((2,)), dma((2,)), dma((2,)), dma((2,))]
    for shape in work_out:
        get(shape, bf16, vmem)
    scratch += work_scratch
    outs = pl.pallas_call(
        functools.partial(
            line_body,
            n,
            len(ag),
            products,
            [(len(t[0]),) + t[2:6] for t in a2a],
            [ph for _, ph in spread],
            sum_kinds,
            chain,
            chain_at,
            (work[0], len(work_in), len(work_out), len(work_scratch)) if work else None,
            owners,
            parts,
        ),
        out_shape=out_shape,
        in_specs=in_specs,
        out_specs=out_specs,
        input_output_aliases=aliases,
        scratch_shapes=scratch,
        compiler_params=pltpu.CompilerParams(
            collective_id=cid, has_side_effects=True, vmem_limit_bytes=62 * 2**20
        ),
        cost_estimate=pl.CostEstimate(flops=us * 1150000000, bytes_accessed=us * 3600000, transcendentals=0),
        name=name,
    )(*inputs)
    return [o.reshape((-1,) + o.shape[2:]) if i < len(ag) else o for i, o in enumerate(outs)]


def rotate(flat, cosine, sine):
    return flat * cosine + pltpu.roll(flat, HEAD_DIM // 2, 1) * sine


def squash(q, k, piece, keys, length):
    scale = -math.log2(math.e) / math.sqrt(HEAD_DIM)
    sg = 1.0 / (1.0 + jnp.exp2(dot_t(q, k) * scale + math.log2(length)))
    row = lax.broadcasted_iota(jnp.int32, (PIECE, PIECE), 0)
    col = lax.broadcasted_iota(jnp.int32, (PIECE, PIECE), 1)
    return sg, (col <= row) | (piece >= 0)


def masked(value, visible, keys):
    last = jnp.where(visible, value[:, keys - PIECE :], 0.0)
    return last if keys == PIECE else jnp.concatenate([value[:, : keys - PIECE], last], axis=1)


def attn_body(heads, length, lin, cosine, sine, piece, out, rot):
    h, b = pl.program_id(0), pl.program_id(1)
    at = lambda part: pl.ds(pl.multiple_of((part * heads + h) * HEAD_DIM, HEAD_DIM), HEAD_DIM)
    blocks = length // PIECE

    @pl.when(b == 0)
    def _():
        @pl.loop(0, blocks)
        def _(i):
            rows = pl.ds(pl.multiple_of(i * PIECE, PIECE), PIECE)
            for part in (0, 1):
                rot[rows, at(part)] = rotate(lin[rows, at(part)], cosine[rows, :], sine[rows, :]).astype(bf16)
            rot[rows, at(2)] = lin[rows, at(2)].astype(bf16)

    for i in range(blocks):
        @pl.when(b == i)
        def _():
            keys = (i + 1) * PIECE
            own = pl.ds(i * PIECE, PIECE)
            sg, visible = squash(rot[own, at(0)], rot[0:keys, at(1)], piece[...], keys, length)
            out[...] = dot(masked(sg, visible, keys).astype(bf16), rot[0:keys, at(2)]).astype(bf16)


def attention(lin, cosine, sine, piece):
    length, width = lin.shape
    heads = width // 3 // HEAD_DIM
    whole = lambda x: pl.BlockSpec(x.shape, lambda h, b: (0, 0))
    return pl.pallas_call(
        functools.partial(attn_body, heads, length),
        grid=(heads, length // PIECE),
        out_shape=[
            jax.ShapeDtypeStruct((length, width // 3), bf16),
            jax.ShapeDtypeStruct((length, width), bf16),
        ],
        in_specs=[whole(lin), whole(cosine), whole(sine), pl.BlockSpec((PIECE, 1), lambda h, b: (b, 0))],
        out_specs=[
            pl.BlockSpec((PIECE, HEAD_DIM), lambda h, b: (b, h)),
            pl.BlockSpec((length, width), lambda h, b: (0, 0)),
        ],
        compiler_params=pltpu.CompilerParams(vmem_limit_bytes=48 * 2**20),
        cost_estimate=pl.CostEstimate(
            flops=4 * heads * length * length * HEAD_DIM // 2, bytes_accessed=8 * length * width, transcendentals=heads * length * length
        ),
        name="attention",
    )(lin, cosine, sine, piece)


def columns_out(w):
    n, nr = lax.axis_size("inner"), lax.axis_size("replica")
    part = w.shape[0] // nr
    cols = w.shape[1] // n

    def source(refs, other, m):
        rows = pl.ds(pl.multiple_of(lax.axis_index("replica") * part, part), part)
        return refs[0].at[rows, pl.ds(pl.multiple_of(other * cols, cols), cols)]

    return ((w,), (n, part, cols), source, lambda ref, other, m: ref.at[other], 1, False)


def to_all(block):
    n = lax.axis_size("inner")
    return ((block,), (n,) + block.shape, lambda refs, other, m: refs[0], lambda ref, other, m: ref.at[other], 1, False)


def rows_back(share, first, count, late=False):
    n, part, _ = share.shape
    cols = first[1]

    def source(refs, other, m):
        return refs[0].at[other, :, pl.ds((first[0] + m) * cols, cols)]

    def target(ref, other, m):
        return ref.at[pl.ds(m * part, part), pl.ds(pl.multiple_of(other * cols, cols), cols)]

    return ((share,), (count * part, n * cols), source, target, count, late)


def sum_blocks(g):
    n = lax.axis_size("inner")
    cols = g.shape[1]
    return ((g,), (n,) + (g.shape[0] // n, cols), lambda refs, other, m: refs[0].at[pl.ds(pl.multiple_of(other * 8, 8), 8)], lambda ref, other, m: ref.at[other], 1, False)


def shares_first(x):
    n, nr = lax.axis_size("inner"), lax.axis_size("replica")
    part = x.shape[1] // n // nr
    return x.reshape(x.shape[0], n, nr, part).transpose(0, 2, 1, 3).reshape(x.shape)


def owners_first(x):
    n, nr = lax.axis_size("inner"), lax.axis_size("replica")
    part = x.shape[1] // n // nr
    return x.reshape(x.shape[0], nr, n, part).transpose(0, 2, 1, 3).reshape(x.shape)


def sum_share(product):
    return lax.psum_scatter(product.astype(bf16), "replica", scatter_dimension=0, tiled=True)


def join(block):
    return lax.all_gather(block, "replica", axis=0, tiled=False)


def flat(w):
    return w.reshape(-1, w.shape[-1])


def local(
    tokens,
    w_query,
    w_key,
    w_value,
    w_out,
    w_gate,
    w_up,
    w_down,
    gain_attn,
    gain_ffn,
    pieces,
    positions,
    cotangent,
):
    n = lax.axis_size("inner")
    nr = lax.axis_size("replica")
    square = nr == 4
    own, width = tokens.shape
    length = own * n
    rows = gain_attn.shape[0]
    after = lax.optimization_barrier

    marks = jnp.zeros((8, own), jnp.int32).at[0].set(pieces).at[1].set(positions)
    gains = jnp.zeros((8, rows), f32).at[0].set(gain_attn.astype(f32)).at[1].set(gain_ffn.astype(f32))
    q_share, k_share, v_share, marks, gains = line_comm(
        0,
        "load_attn", 25,
        a2a=[columns_out(w_query), columns_out(w_key), columns_out(w_value), to_all(marks), to_all(gains)],
    )
    qkv_share = jnp.concatenate([q_share, k_share, v_share], axis=2)
    loads = [columns_out(w_gate), columns_out(w_up)]
    if square:
        x, g_share, u_share, w_qkv = line_comm(
            1, "load_ffn", 80, ag=[shares_first(tokens)], a2a=loads, spread=[(qkv_share, (1, 2))]
        )
    else:
        w_qkv = join(qkv_share)
        x, g_share, u_share = line_comm(1, "load_ffn", 80, ag=[shares_first(tokens)], a2a=loads)
    w_qkv = flat(w_qkv)
    cot, x = after((cotangent, x))
    cot = lax.all_gather(cot, "inner", axis=0, tiled=True)
    pieces, positions = marks[:, 0].reshape(length, 1), marks[:, 1].reshape(length)
    attn_gain, ffn_gain = gains[:, 0].reshape(1, -1), gains[:, 1].reshape(1, -1)

    x = x.astype(f32)
    cosine, sine = rope_tables(positions)
    u1 = x * rms_scale(x)
    n1 = (u1 * shares_first(attn_gain)).astype(bf16)
    o, rot = attention(dot(n1, w_qkv), cosine, sine, pieces)
    if square:
        a, w_g, w_u = line_comm(2, "attn_out", 50, rs=[[(o, w_out, False, 0)]], spread=[(g_share, (1,)), (u_share, (1,))])
    else:
        w_g, w_u = join(g_share), join(u_share)
        (a,) = line_comm(2, "attn_out", 50, rs=[[(o, w_out, False, 0)]])
    mid = tokens.astype(f32) + a
    r2 = rms_scale(mid)
    u2 = mid * r2
    n2 = shares_first((u2 * ffn_gain).astype(bf16))
    ffn = w_down.shape[0]
    results = [(length, ffn), (length, 2 * ffn)]
    held = [pltpu.VMEM((length, ffn), f32)]
    if square:
        held += [pltpu.VMEM((2,) + w_g.shape, bf16), pltpu.SemaphoreType.DMA((2, 4))]
        n2, w_g, w_u, hid, ggu = line_comm(
            3,
            "ffn_forward",
            60,
            ag=[n2],
            spread=[(w_g, (2,)), (w_u, (2,))],
            work=(Forward, [cot, w_down], results, held),
        )
        w_g, w_u = flat(w_g), flat(w_u)
    else:
        w_g, w_u = flat(w_g), flat(w_u)
        n2, hid, ggu = line_comm(3, "ffn_forward", 60, ag=[n2], work=(Forward, [cot, w_down, w_g, w_u], results, held))

    gu = t_dot(n2, ggu).astype(bf16)
    gu, ggu = after((gu, ggu))
    gu_share = sum_share(gu)
    tidy = square and width // n // nr == 64
    gn2, g_down = line_comm(4, "scatter_gn2", 44, owners=tidy, work=(Later, [hid, cot], [w_down.shape], []), rs=[[(ggu, w_g, True, 0), (ggu, w_u, True, w_g.shape[1])]])
    gn2 = gn2 if tidy else owners_first(gn2)
    gu2 = gn2 * ffn_gain
    ffn_gain_part = jnp.sum(gn2 * u2, axis=0)
    gmid = cotangent.astype(f32) + r2 * (gu2 - u2 * jnp.mean(gu2 * u2, axis=1, keepdims=True))
    (ga,) = line_comm(5, "gather_ga", 40, ag=[gmid.astype(bf16)])
    ga, gu_share, g_down = after((ga, gu_share, g_down))
    grad_down = lax.psum(g_down, "replica")

    cols = w_gate.shape[1] // n
    heads_width = rot.shape[1] // 3
    gu_share = gu_share.reshape(n, -1, 2 * cols)
    own_x = tokens.astype(f32)
    r1 = rms_scale(own_x)
    u1 = own_x * r1

    def gain_parts(gn1):
        both = jnp.stack([jnp.sum(gn1 * u1, axis=0).reshape(n, rows), ffn_gain_part.reshape(n, rows)], axis=1)
        return sum_blocks(jnp.pad(both, ((0, 0), (0, 6), (0, 0))).reshape(n * 8, rows))

    held = [pltpu.VMEM((length, heads_width), bf16)] + [pltpu.VMEM((length, HEAD_DIM), f32)] * 2
    work = (Backward, [ga, w_out, rot, cosine, sine, pieces], [rot.shape], held)
    gn1_part = [(None, w_qkv, True, 0)]
    if square:
        gn1, gate_rows, up_rows, out_share, qkv_share, grad_gate, _ = line_comm(
            6,
            "scatter_gn1",
            1,
            owners=tidy,
            rs=[gn1_part],
            a2a=[rows_back(gu_share, (0, cols), 1), rows_back(gu_share, (1, cols), 1, False)],
            sums=[(o, ga, width), (n1, None, rot.shape[1])],
            chain=(0,),
            chain_at=0,
            work=work,
        )
        gn1 = gn1 if tidy else owners_first(gn1)
        qkv_back = rows_back(qkv_share.reshape(n, -1, 3 * heads_width), (0, heads_width), 3)
        mlp, _, _, grad_up, grad_out, grad_qkv, gains = line_comm(
            7,
            "rows_attn",
            1,
            rs=[[(hid, w_down, False, 0)]],
            a2a=[qkv_back, gain_parts(gn1)],
            spread=[(up_rows, (1, 2)), (out_share, (1, 2))],
            chain=(0, 1),
            chain_at=0,
        )
        gains = jnp.sum(gains, axis=(0, 1))
    else:
        gu_back = rows_back(gu_share, (0, cols), 2)
        gn1, gu_rows, gqkv = line_comm(6, "scatter_gn1", 80, rs=[gn1_part], a2a=[gu_back], work=work)
        gn1 = owners_first(gn1)
        g_qkv = sum_share(t_dot(n1, gqkv))
        qkv_back = rows_back(g_qkv.reshape(n, -1, 3 * heads_width), (0, heads_width), 3)
        mlp, qkv_rows, gains = line_comm(
            7, "rows_attn", 75, rs=[[(hid, w_down, False, 0)]], a2a=[qkv_back, gain_parts(gn1)]
        )
        gains = lax.psum(jnp.sum(gains, axis=0), "replica")
        grad_gu = join(gu_rows).reshape(nr, 2, -1, n * cols)
        grad_gate, grad_up, grad_out, grad_qkv = grad_gu[:, 0], grad_gu[:, 1], join(sum_share(t_dot(o, ga))), join(qkv_rows)
    output = (mid + mlp).astype(bf16)
    grad_qkv = grad_qkv.reshape(nr, 3, -1, width).astype(f32)

    gu1 = gn1 * attn_gain
    grad_tokens = gmid + r1 * (gu1 - u1 * jnp.mean(gu1 * u1, axis=1, keepdims=True))
    return (
        output,
        grad_tokens,
        grad_qkv[:, 0].reshape(w_query.shape),
        grad_qkv[:, 1].reshape(w_key.shape),
        grad_qkv[:, 2].reshape(w_value.shape),
        grad_out.reshape(w_out.shape).astype(f32),
        grad_gate.reshape(w_gate.shape).astype(f32),
        grad_up.reshape(w_up.shape).astype(f32),
        grad_down.reshape(w_down.shape).astype(f32),
        gains[0],
        gains[1],
    )


def solution(mesh):
    tok = P(("replica", "inner"), None)
    row = P("inner", None)
    vec = P("inner")
    mark = P(("replica", "inner"))
    return jax.shard_map(
        local,
        mesh=mesh,
        in_specs=(tok, row, row, row, row, row, row, row, vec, vec, mark, mark, tok),
        out_specs=(tok, tok, row, row, row, row, row, row, row, vec, vec),
        check_vma=False,
    )
```
